256 devices in a mesh: dp: 16 (over y, z_hi), node: 16 (over z_lo, x, core).
Axes of the slice: x: 4, y: 4, z: 8 (z_hi: 4, z_lo: 2; z = z_hi * 2 + z_lo), core: 2. Of those that a mesh axis runs over, the one named last changes fastest.
Arguments:
- tokens: bfloat16 [81920, 8192], P(('dp', 'node')), may hold values from -60 to 60
- norm_gain: float32 [8192], replicated, may hold values from 0.1 to 1.9
- weight_values: bfloat16 [8192, 512], P('node'), may hold values from -127 to 127, as said below
- weight_scale: bfloat16 [8192, 4], P('node'), may hold values from 4.9829483e-05 to 0.00049972534
- key_cotangent: bfloat16 [81920, 512], P(('dp', 'node')), may hold values from -8 to 8
Outputs:
- projected: bfloat16 [81920, 512], P(('dp', 'node'))
- token_grads: bfloat16 [81920, 8192], P(('dp', 'node'))
- weight_grads: float32 [8192, 512], P('node')
- gain_grads: float32 [8192], replicated
The draws below stay inside these ranges and needn't reach their ends.
Inputs may be any that keep to these rules, and one draw needn't show every extreme that they name: `weight_values`: entries are whole numbers.
All inputs are finite; a program needn't handle non-finite values.
Results may differ from the reference program's by a relative error of at most 0.0057.
Values may be sent and summed in bfloat16 or wider, within the bound.
No kernel may reach another device: no remote copies, remote signals or barrier semaphores. Data moves between devices by JAX's collectives and lax.ppermute only.
A program may use at most 128 MiB of HBM per device.

```python
import math
import jax
import jax.numpy as jnp
from jax import lax

D = 8192
BLOCK = 128
TOK_DEV = 320
COLS = 512
TOKENS = 81920
N_DP = 16
N_NODE = 16


def draw_tokens(key, part):
    key = jax.random.fold_in(key, 11)
    return jnp.clip(jax.random.normal(key, (TOKENS, D), jnp.float32), -6.0, 6.0).astype(jnp.bfloat16)


def draw_weight_values(key, part):
    key = jax.random.fold_in(key, 23)
    return jax.random.randint(key, (D, COLS), -127, 128).astype(jnp.bfloat16)


def draw_key_cotangent(key, part):
    key = jax.random.fold_in(key, 37)
    return jnp.clip(jax.random.normal(key, (TOKENS, COLS), jnp.float32), -6.0, 6.0).astype(jnp.bfloat16)


def block_levels(stream_key, dims, pieces, least, top_value):
    gain, own = 1.0, jax.random.fold_in(stream_key, 6)
    for dim, blocks in pieces:
        steps = jnp.exp(jax.random.uniform(jax.random.fold_in(own, dim), (blocks,), jnp.float32, least / len(pieces), top_value / len(pieces)))
        gain = gain * jnp.repeat(steps, dims[dim] // blocks).reshape([-1 if axis == dim else 1 for axis in range(len(dims))])
    return gain


def setup_inputs(seed: int = 0) -> dict:
    seeds = jax.random.split(jax.random.key(seed), 6)
    return {
        "tokens": draw_tokens(jax.random.fold_in(seeds[5], 71), 0),
        "norm_gain": jnp.clip(1.0 + 0.18 * jax.random.normal(seeds[1], (D,), jnp.float32), 0.1, 1.9),
        "weight_values": draw_weight_values(jax.random.fold_in(seeds[5], 71), 0),
        "weight_scale": jnp.clip(jnp.exp(math.log(0.00049972534) - 2.3054518 * jax.random.uniform(seeds[3], (D, COLS // BLOCK), jnp.float32) ** block_levels(seeds[3], (D, COLS // BLOCK), ((0, 16),), -0.2, 0.2)), 4.982948303222656e-05, 0.00049972534).astype(jnp.bfloat16),
        "key_cotangent": draw_key_cotangent(jax.random.fold_in(seeds[5], 71), 0),
    }


def reference(tokens, norm_gain, weight_values, weight_scale, key_cotangent):
    blocks_per_row = COLS // BLOCK
    weight = (weight_values.astype(jnp.float32).reshape(D, blocks_per_row, BLOCK) * weight_scale.astype(jnp.float32)[:, :, None]).reshape(D, COLS).astype(jnp.bfloat16)
    gain_wide = norm_gain.astype(jnp.float32)
    devices = N_DP * N_NODE
    token_blocks = tokens.reshape(devices, TOK_DEV, D)
    cotangent_blocks = key_cotangent.reshape(devices, TOK_DEV, COLS)

    def one_device(carry, blocks):
        block_tokens, block_cotangent = blocks
        wide = block_tokens.astype(jnp.float32)
        inverse = lax.rsqrt(lax.optimization_barrier(jnp.mean(wide * wide, axis=1, keepdims=True)) + 1e-05)
        scaled = wide * inverse
        normed = (scaled * gain_wide).astype(jnp.bfloat16)
        projected = jnp.dot(normed, weight, preferred_element_type=jnp.float32).astype(jnp.bfloat16)
        normed_grads = lax.dot_general(block_cotangent, weight, (((1,), (1,)), ((), ())), preferred_element_type=jnp.float32)
        gained = normed_grads * gain_wide
        moment = lax.optimization_barrier(jnp.mean(wide * gained, axis=1, keepdims=True))
        token_grads = (inverse * gained - wide * inverse ** 3 * moment).astype(jnp.bfloat16)
        gain_terms = lax.optimization_barrier(jnp.sum(normed_grads * scaled, axis=0))
        local_grads = lax.dot_general(normed, block_cotangent, (((0,), (0,)), ((), ())), preferred_element_type=jnp.float32)
        blocked = local_grads.reshape(D, blocks_per_row, BLOCK)
        peaks = (lax.optimization_barrier(jnp.max(jnp.abs(blocked), axis=2)) + 1e-06).astype(jnp.bfloat16)
        peak_wide = lax.optimization_barrier(peaks).astype(jnp.float32)
        levels = (blocked / peak_wide[:, :, None]).astype(jnp.bfloat16)
        restored = lax.optimization_barrier(levels).astype(jnp.float32) * peak_wide[:, :, None]
        weight_total, gain_total = carry
        return ((weight_total + restored.reshape(D, COLS), gain_total + gain_terms), (projected, token_grads))
    start = (jnp.zeros((D, COLS), jnp.float32), jnp.zeros((D,), jnp.float32))
    (weight_total, gain_total), (projected, token_grads) = lax.scan(one_device, start, (token_blocks, cotangent_blocks))
    return (projected.reshape(TOKENS, COLS), token_grads.reshape(TOKENS, D), weight_total / devices, gain_total / devices)
```

```python
import functools

import jax
import jax.numpy as jnp
from jax import lax
from jax.experimental import pallas as pl
from jax.experimental.pallas import tpu as pltpu
from jax.sharding import Mesh, PartitionSpec as P

NODE = ("zl", "x", "c")
EVERY = ("y", "zh", "zl", "x", "c")
TILE = 128
GROUPS = 4
Y_MASKS = ((1, 3), (3, 1), (1, 3), (3, 1))
LIMIT = 48 * 2**20


def widen_weight(values, scales):
    rows, blocks = scales.shape
    block = values.shape[1] // blocks
    shaped = values.astype(jnp.float32).reshape(rows, blocks, block)
    return (
        (shaped * scales.astype(jnp.float32)[:, :, None])
        .reshape(rows, blocks * block)
        .astype(jnp.bfloat16)
    )


def norm_kernel(tab_ref, tok_ref, gain_ref, own_ref, oth_ref, inv_ref):
    rows, width = tok_ref.shape
    total = jnp.zeros((rows, TILE), jnp.float32)
    for t in range(width // TILE):
        wide = tok_ref[:, t * TILE : (t + 1) * TILE].astype(jnp.float32)
        total = total + wide * wide
    mean = jnp.sum(total, axis=1, keepdims=True) / width
    inverse = lax.rsqrt(mean + 1e-05)
    inv_ref[...] = inverse
    for side, out_ref in enumerate((own_ref, oth_ref)):
        for r in range(width // TILE // 2):
            at = pl.multiple_of(tab_ref[side, r] * TILE, TILE)
            wide = tok_ref[:, pl.ds(at, TILE)].astype(jnp.float32)
            scaled = wide * inverse * gain_ref[:, pl.ds(at, TILE)]
            out_ref[:, r * TILE : (r + 1) * TILE] = scaled.astype(jnp.bfloat16)


def norm_tiles(tokens, gain, table):
    rows, width = tokens.shape
    step = 64 if rows % 64 == 0 else rows
    half = pl.BlockSpec((step, width // 2), lambda i, tab: (i, 0))
    return pl.pallas_call(
        norm_kernel,
        grid_spec=pltpu.PrefetchScalarGridSpec(
            num_scalar_prefetch=1,
            grid=(rows // step,),
            in_specs=[
                pl.BlockSpec((step, width), lambda i, tab: (i, 0)),
                pl.BlockSpec((1, width), lambda i, tab: (0, 0)),
            ],
            out_specs=[half, half, pl.BlockSpec((step, 1), lambda i, tab: (i, 0))],
        ),
        out_shape=[
            jax.ShapeDtypeStruct((rows, width // 2), jnp.bfloat16),
            jax.ShapeDtypeStruct((rows, width // 2), jnp.bfloat16),
            jax.ShapeDtypeStruct((rows, 1), jnp.float32),
        ],
        compiler_params=pltpu.CompilerParams(vmem_limit_bytes=LIMIT),
        cost_estimate=pl.CostEstimate(
            flops=6 * rows * width, bytes_accessed=4 * rows * width, transcendentals=rows
        ),
    )(table, tokens, gain)


def place(group, rz, ry, rx):
    first, second = Y_MASKS[group]
    y1, y2 = next(
        (a, b) for a in (0, 1) for b in (0, 1) if (a * first) ^ (b * second) == ry
    )
    if group < 2:
        return y1, (rz * 2 + y2) * 4 + rx
    return rz, (y1 * 2 + y2) * 4 + rx


def grad_kernel(own_ref, got_ref, cot_own_ref, cot_got_ref, *out_refs):
    span = 2 * TILE
    cot_own = cot_own_ref[...]
    cot_got = cot_got_ref[...]
    for pair in range(own_ref.shape[1] // span):
        part = slice(pair * span, (pair + 1) * span)
        grads = jnp.dot(cot_own, own_ref[:, part], preferred_element_type=jnp.float32)
        grads += jnp.dot(cot_got, got_ref[:, part], preferred_element_type=jnp.float32)
        for which in range(2):
            tile = pair * 2 + which
            for group in range(GROUPS):
                piece = grads[
                    group * TILE : (group + 1) * TILE, which * TILE : (which + 1) * TILE
                ]
                sent, at = place(group, tile // 16, tile // 4 % 4, tile % 4)
                if sent:
                    out_refs[group][at] = piece.astype(jnp.bfloat16)
                else:
                    out_refs[GROUPS + group][at] = piece


def grad_tiles(own, got, cot_own, cot_got):
    rows, width = own.shape
    tiles = width // TILE // 2
    shape = (tiles, TILE, TILE)
    outs = pl.pallas_call(
        grad_kernel,
        out_shape=[jax.ShapeDtypeStruct(shape, jnp.bfloat16)] * GROUPS
        + [jax.ShapeDtypeStruct(shape, jnp.float32)] * GROUPS,
        compiler_params=pltpu.CompilerParams(vmem_limit_bytes=LIMIT),
        cost_estimate=pl.CostEstimate(
            flops=4 * rows * width * GROUPS * TILE,
            bytes_accessed=4 * rows * width + 6 * GROUPS * tiles * TILE * TILE,
            transcendentals=0,
        ),
    )(own, got, cot_own, cot_got)
    return outs[:GROUPS], outs[GROUPS:]


def project_kernel(tok_ref, inv_ref, gain_ref, w_ref, cot_ref, proj_ref, grads_ref, acc, moment, *, width):
    phase, step = pl.program_id(0), pl.program_id(1)
    last = pl.num_programs(1) - 1
    inverse = inv_ref[...]

    @pl.when(phase == 0)
    def _():
        wide = tok_ref[...].astype(jnp.float32)
        normed = (wide * inverse * gain_ref[...]).astype(jnp.bfloat16)
        sums = jnp.dot(normed, w_ref[...], preferred_element_type=jnp.float32)

        @pl.when(step == 0)
        def _():
            acc[...] = sums

        @pl.when(step > 0)
        def _():
            acc[...] += sums

        @pl.when(step == last)
        def _():
            keys = acc[...]
            proj_ref[...] = keys.astype(jnp.bfloat16)
            inner = jnp.sum(cot_ref[...].astype(jnp.float32) * keys, axis=1, keepdims=True)
            moment[...] = inverse * inverse * inner / width

    @pl.when(phase == 1)
    def _():
        partial = lax.dot_general(
            cot_ref[...], w_ref[...], (((1,), (1,)), ((), ())), preferred_element_type=jnp.float32
        )
        wide = tok_ref[...].astype(jnp.float32)
        grads = inverse * gain_ref[...] * partial - wide * moment[...]
        grads_ref[...] = grads.astype(jnp.bfloat16)


def project(tokens, inverse, gain, weight, cotangent):
    rows, width = tokens.shape
    columns = cotangent.shape[1]
    span = 1024
    return pl.pallas_call(
        functools.partial(project_kernel, width=width),
        grid=(2, width // span),
        in_specs=[
            pl.BlockSpec((rows, span), lambda p, i: (0, i)),
            pl.BlockSpec((rows, 1), lambda p, i: (0, 0)),
            pl.BlockSpec((1, span), lambda p, i: (0, i)),
            pl.BlockSpec((span, columns), lambda p, i: (i, 0)),
            pl.BlockSpec((rows, columns), lambda p, i: (0, 0)),
        ],
        out_specs=[
            pl.BlockSpec((rows, columns), lambda p, i: (0, 0)),
            pl.BlockSpec((rows, span), lambda p, i: (0, i * p)),
        ],
        out_shape=[
            jax.ShapeDtypeStruct((rows, columns), jnp.bfloat16),
            jax.ShapeDtypeStruct((rows, width), jnp.bfloat16),
        ],
        scratch_shapes=[
            pltpu.VMEM((rows, columns), jnp.float32),
            pltpu.VMEM((rows, 1), jnp.float32),
        ],
        compiler_params=pltpu.CompilerParams(vmem_limit_bytes=LIMIT),
        cost_estimate=pl.CostEstimate(
            flops=4 * rows * width * columns,
            bytes_accessed=6 * rows * width + 4 * width * columns,
            transcendentals=0,
        ),
    )(tokens, inverse, gain, weight, cotangent)


def swap(array, axis, mask):
    size = lax.axis_size(axis)
    return lax.ppermute(array, axis, [(i, i ^ mask) for i in range(size)])


def swap_z(array, odd):
    size = lax.axis_size("zh") * lax.axis_size("zl")
    if odd:
        pairs = [(i, (i + 1 if i % 2 else i - 1) % size) for i in range(size)]
    else:
        pairs = [(i, i ^ 1) for i in range(size)]
    return lax.ppermute(array, ("zh", "zl"), pairs)


def halve(total):
    half = total.shape[0] // 2
    return total[half:].astype(jnp.bfloat16), total[:half]


def reduce_grads(sent, kept):
    moves = (
        lambda a: swap(a, "y", 1),
        lambda a: swap(a, "y", 3),
        lambda a: swap_z(a, False),
        lambda a: swap_z(a, True),
    )
    for order in ((0, 1, 2, 3), (2, 3, 0, 1)):
        got = [moves[m](s) for m, s in zip(order, sent)]
        totals = [k + g.astype(jnp.float32) for k, g in zip(kept, got)]
        sent, kept = zip(*[halve(t) for t in totals])
    got_even = swap(jnp.stack([sent[0], sent[2]]), "y", 3)
    got_odd = swap(jnp.stack([sent[1], sent[3]]), "y", 1)
    got = (got_even[0], got_odd[0], got_even[1], got_odd[1])
    total = jnp.stack([k + g.astype(jnp.float32) for k, g in zip(kept, got)], axis=1)
    out = total[0]
    for mask in (1, 3, 2):
        out = out + swap(total[mask].astype(jnp.bfloat16), "x", mask).astype(jnp.float32)
    send = out.astype(jnp.bfloat16)
    for mask in (1, 3, 2):
        out = out + swap(send, "zh", mask).astype(jnp.float32)
    return out


def shards(tokens, norm_gain, weight_values, weight_scale, key_cotangent):
    y, zl, x, c = (lax.axis_index(a) for a in ("y", "zl", "x", "c"))
    width = tokens.shape[1]
    columns = weight_values.shape[1]
    gain = norm_gain.reshape(1, width)
    own_weight = widen_weight(weight_values, weight_scale)
    weight = lax.all_gather(own_weight, NODE, axis=0, tiled=True)

    label = jnp.arange(32, dtype=jnp.int32)
    chip = (zl ^ (label // 16)) * 4 + (x ^ (label % 4))
    quarter = y ^ (label // 4 % 4)
    table = jnp.stack([(chip * 2 + side) * 4 + quarter for side in (c, 1 - c)])
    own, other, inverse = norm_tiles(tokens, gain, table)

    cot_own = key_cotangent.T
    cot_got = swap(cot_own, "c", 1)
    got = swap(other, "c", 1)
    sent, kept = grad_tiles(own, got, cot_own, cot_got)
    devices = 1
    for axis in EVERY:
        devices *= lax.axis_size(axis)
    mine = reduce_grads(sent, kept) / devices

    projected, token_grads = project(tokens, inverse, gain, weight, key_cotangent)

    mine = mine.reshape(columns, TILE)
    shard = columns
    node = (zl * 4 + x) * 2 + c
    my_weight = lax.dynamic_slice_in_dim(own_weight, y * TILE, TILE, 0).T.astype(jnp.float32)
    my_gain = lax.dynamic_slice_in_dim(norm_gain, node * shard + y * TILE, TILE, 0)
    gain_part = jnp.sum(my_weight * mine, axis=0, keepdims=True) / my_gain[None, :]
    high = gain_part.astype(jnp.bfloat16)
    low = (gain_part - high.astype(jnp.float32)).astype(jnp.bfloat16)
    packed = jnp.concatenate(
        [mine.astype(jnp.bfloat16), high, low, jnp.zeros((14, TILE), jnp.bfloat16)], axis=0
    )
    pieces = jnp.stack([packed] + [swap(packed, "y", mask) for mask in (1, 2, 3)])
    ordered = [lax.dynamic_index_in_dim(pieces, y ^ q, 0, keepdims=False) for q in range(4)]
    weight_grads = jnp.concatenate([p[:columns] for p in ordered], axis=1)
    weight_grads = weight_grads.astype(jnp.float32).T
    gains = jnp.concatenate(
        [p[columns].astype(jnp.float32) + p[columns + 1].astype(jnp.float32) for p in ordered]
    )
    pair = swap(gains, "c", 1)
    gains = jnp.where(c == 0, jnp.concatenate([gains, pair]), jnp.concatenate([pair, gains]))
    rows = jnp.stack([gains] + [swap(gains, "x", mask) for mask in (1, 2, 3)])
    gains = jnp.concatenate([lax.dynamic_index_in_dim(rows, x ^ q, 0, keepdims=False) for q in range(4)])
    pair = swap(gains, "zl", 1)
    gain_grads = jnp.where(zl == 0, jnp.concatenate([gains, pair]), jnp.concatenate([pair, gains]))
    return (projected, token_grads, weight_grads, gain_grads)


def solution(mesh):
    fine = Mesh(mesh.devices.reshape(4, 4, 2, 4, 2), EVERY)
    rows = P(EVERY, None)
    return jax.shard_map(
        shards,
        mesh=fine,
        in_specs=(rows, P(), P(NODE, None), P(NODE, None), rows),
        out_specs=(rows, rows, P(NODE, None), P()),
        check_vma=False,
    )
```

```python
import functools

import jax
import jax.numpy as jnp
from jax import lax
from jax.experimental import pallas as pl
from jax.experimental.pallas import tpu as pltpu
from jax.sharding import Mesh, PartitionSpec as P

NODE = ("zl", "x", "c")
EVERY = ("y", "zh", "zl", "x", "c")
TILE = 128
GROUPS = 4
Y_MASKS = ((1, 3), (3, 1), (1, 3), (3, 1))
LIMIT = 48 * 2**20


def widen_weight(values, scales):
    rows, blocks = scales.shape
    block = values.shape[1] // blocks
    shaped = values.astype(jnp.float32).reshape(rows, blocks, block)
    return (
        (shaped * scales.astype(jnp.float32)[:, :, None])
        .reshape(rows, blocks * block)
        .astype(jnp.bfloat16)
    )


def norm_kernel(tab_ref, tok_ref, gain_ref, out_ref, inv_ref):
    rows, width = tok_ref.shape
    total = jnp.zeros((rows, TILE), jnp.float32)
    for t in range(width // TILE):
        wide = tok_ref[:, t * TILE : (t + 1) * TILE].astype(jnp.float32)
        total = total + wide * wide
    mean = jnp.sum(total, axis=1, keepdims=True) / width
    inverse = lax.rsqrt(mean + 1e-05)
    inv_ref[...] = inverse
    for r in range(width // TILE // 2):
        at = pl.multiple_of(tab_ref[r] * TILE, TILE)
        wide = tok_ref[:, pl.ds(at, TILE)].astype(jnp.float32)
        scaled = wide * inverse * gain_ref[:, pl.ds(at, TILE)]
        out_ref[:, r * TILE : (r + 1) * TILE] = scaled.astype(jnp.bfloat16)


def norm_tiles(tokens, gain, table):
    rows, width = tokens.shape
    step = 64 if rows % 64 == 0 else rows
    return pl.pallas_call(
        norm_kernel,
        grid_spec=pltpu.PrefetchScalarGridSpec(
            num_scalar_prefetch=1,
            grid=(rows // step,),
            in_specs=[
                pl.BlockSpec((step, width), lambda i, tab: (i, 0)),
                pl.BlockSpec((1, width), lambda i, tab: (0, 0)),
            ],
            out_specs=[
                pl.BlockSpec((step, width // 2), lambda i, tab: (i, 0)),
                pl.BlockSpec((step, 1), lambda i, tab: (i, 0)),
            ],
        ),
        out_shape=[
            jax.ShapeDtypeStruct((rows, width // 2), jnp.bfloat16),
            jax.ShapeDtypeStruct((rows, 1), jnp.float32),
        ],
        compiler_params=pltpu.CompilerParams(vmem_limit_bytes=LIMIT),
        cost_estimate=pl.CostEstimate(
            flops=6 * rows * width, bytes_accessed=3 * rows * width, transcendentals=rows
        ),
    )(table, tokens, gain)


def split(group, ry):
    first, second = Y_MASKS[group]
    return next((a, b) for a in (0, 1) for b in (0, 1) if (a * first) ^ (b * second) == ry)


def grad_kernel(tab_ref, tok_ref, gain_ref, inv_ref, got_ref, cot_own_ref, cot_got_ref, *refs):
    sent_refs, kept_refs, normed = refs[:GROUPS], refs[GROUPS : 2 * GROUPS], refs[-1]
    y = tab_ref[8]
    rz = 1 - pl.program_id(0) // 4
    inverse = inv_ref[...]
    for ry in range(4):
        at = pl.multiple_of((y ^ ry) * TILE, TILE)
        wide = tok_ref[:, pl.ds(at, TILE)].astype(jnp.float32)
        scaled = wide * inverse * gain_ref[:, pl.ds(at, TILE)]
        normed[:, ry * TILE : (ry + 1) * TILE] = scaled.astype(jnp.bfloat16)
    span = 2 * TILE
    for pair in range(2):
        part = slice(pair * span, (pair + 1) * span)
        grads = jnp.dot(cot_own_ref[...], normed[:, part], preferred_element_type=jnp.float32)
        grads += jnp.dot(cot_got_ref[...], got_ref[:, part], preferred_element_type=jnp.float32)
        for which in range(2):
            ry = pair * 2 + which
            for group in range(GROUPS):
                piece = grads[
                    group * TILE : (group + 1) * TILE, which * TILE : (which + 1) * TILE
                ]
                y1, y2 = split(group, ry)
                if group < 2:
                    if y1:
                        sent_refs[group][0, y2, 0] = piece.astype(jnp.bfloat16)
                    else:
                        kept_refs[group][0, y2, 0] = piece
                else:

                    @pl.when(rz == 1)
                    def _(piece=piece, group=group, y1=y1, y2=y2):
                        sent_refs[group][y1, y2, 0] = piece.astype(jnp.bfloat16)

                    @pl.when(rz == 0)
                    def _(piece=piece, group=group, y1=y1, y2=y2):
                        kept_refs[group][y1, y2, 0] = piece


def grad_tiles(tokens, inverse, gain, got, cot_own, cot_got, table):
    rows = tokens.shape[0]
    columns = cot_own.shape[0]
    span = 4 * TILE
    shape = (2, 2, 4, TILE, TILE)
    y_block = (1, 2, 1, TILE, TILE)
    z_block = (2, 2, 1, TILE, TILE)

    def by_y(j, tab):
        return (1 - j // 4, 0, j % 4, 0, 0)

    def sent_z(j, tab):
        return (0, 0, jnp.minimum(j, 3), 0, 0)

    def kept_z(j, tab):
        return (0, 0, jnp.maximum(j - 4, 0), 0, 0)

    def whole(j, tab):
        return (0, 0)

    def rel(j, tab):
        return (0, (1 - j // 4) * 4 + j % 4)

    outs = pl.pallas_call(
        grad_kernel,
        grid_spec=pltpu.PrefetchScalarGridSpec(
            num_scalar_prefetch=1,
            grid=(8,),
            in_specs=[
                pl.BlockSpec((rows, span), lambda j, tab: (0, tab[j])),
                pl.BlockSpec((1, span), lambda j, tab: (0, tab[j])),
                pl.BlockSpec((rows, 1), whole),
                pl.BlockSpec((rows, span), rel),
                pl.BlockSpec((columns, rows), whole),
                pl.BlockSpec((columns, rows), whole),
            ],
            out_specs=[pl.BlockSpec(y_block, by_y)] * 2
            + [pl.BlockSpec(z_block, sent_z)] * 2
            + [pl.BlockSpec(y_block, by_y)] * 2
            + [pl.BlockSpec(z_block, kept_z)] * 2,
            scratch_shapes=[pltpu.VMEM((rows, span), jnp.bfloat16)],
        ),
        out_shape=[jax.ShapeDtypeStruct(shape, jnp.bfloat16)] * GROUPS
        + [jax.ShapeDtypeStruct(shape, jnp.float32)] * GROUPS,
        compiler_params=pltpu.CompilerParams(vmem_limit_bytes=LIMIT),
        cost_estimate=pl.CostEstimate(
            flops=4 * rows * 8 * span * columns,
            bytes_accessed=4 * rows * 8 * span + 6 * GROUPS * 16 * TILE * TILE,
            transcendentals=0,
        ),
    )(table, tokens, gain, inverse, got, cot_own, cot_got)
    return outs[:GROUPS], outs[GROUPS:]


def forward_kernel(tab_ref, tok_ref, inv_ref, gain_ref, cot_ref, *refs, width):
    w_refs, (proj_ref, moment_ref, acc) = refs[:4], refs[4:]
    step = pl.program_id(0)
    inverse = inv_ref[...]

    @pl.when(step == 0)
    def _():
        acc[...] = jnp.zeros_like(acc)

    wide = tok_ref[...].astype(jnp.float32)
    normed = (wide * inverse * gain_ref[...]).astype(jnp.bfloat16)
    for which in range(4):

        @pl.when(step // 4 == which)
        def _(which=which):
            acc[...] += jnp.dot(normed, w_refs[which][0], preferred_element_type=jnp.float32)

    @pl.when(step == pl.num_programs(0) - 1)
    def _():
        keys = acc[...]
        proj_ref[...] = keys.astype(jnp.bfloat16)
        inner = jnp.sum(cot_ref[...].astype(jnp.float32) * keys, axis=1, keepdims=True)
        moment_ref[...] = inverse * inverse * inner / width


def weight_specs(span, columns):
    return [
        pl.BlockSpec((1, span, columns), lambda j, tab, a=a: (jnp.clip(j - 4 * a, 0, 3), 0, 0))
        for a in range(4)
    ]


def forward(tokens, inverse, gain, cotangent, weights, table):
    rows, width = tokens.shape
    columns = cotangent.shape[1]
    span = weights[0].shape[1]

    def whole(j, tab):
        return (0, 0)

    def block(j, tab):
        return (0, tab[j])

    return pl.pallas_call(
        functools.partial(forward_kernel, width=width),
        grid_spec=pltpu.PrefetchScalarGridSpec(
            num_scalar_prefetch=1,
            grid=(width // span,),
            in_specs=[
                pl.BlockSpec((rows, span), block),
                pl.BlockSpec((rows, 1), whole),
                pl.BlockSpec((1, span), block),
                pl.BlockSpec((rows, columns), whole),
            ]
            + weight_specs(span, columns),
            out_specs=[pl.BlockSpec((rows, columns), whole), pl.BlockSpec((rows, 1), whole)],
            scratch_shapes=[pltpu.VMEM((rows, columns), jnp.float32)],
        ),
        out_shape=[
            jax.ShapeDtypeStruct((rows, columns), jnp.bfloat16),
            jax.ShapeDtypeStruct((rows, 1), jnp.float32),
        ],
        compiler_params=pltpu.CompilerParams(vmem_limit_bytes=LIMIT),
        cost_estimate=pl.CostEstimate(
            flops=2 * rows * width * columns,
            bytes_accessed=2 * rows * width + 2 * width * columns,
            transcendentals=0,
        ),
    )(table, tokens, inverse, gain, cotangent, *weights)


def backward_kernel(tab_ref, tok_ref, inv_ref, gain_ref, cot_ref, moment_ref, *refs):
    w_refs, grads_ref = refs[:4], refs[4]
    step = pl.program_id(0)
    for which in range(4):

        @pl.when(step // 4 == which)
        def _(which=which):
            partial = lax.dot_general(
                cot_ref[...],
                w_refs[which][0],
                (((1,), (1,)), ((), ())),
                preferred_element_type=jnp.float32,
            )
            wide = tok_ref[...].astype(jnp.float32)
            grads = inv_ref[...] * gain_ref[...] * partial - wide * moment_ref[...]
            grads_ref[...] = grads.astype(jnp.bfloat16)


def backward(tokens, inverse, gain, cotangent, moment, weights, table):
    rows, width = tokens.shape
    columns = cotangent.shape[1]
    span = weights[0].shape[1]

    def whole(j, tab):
        return (0, 0)

    def block(j, tab):
        return (0, tab[j])

    return pl.pallas_call(
        backward_kernel,
        grid_spec=pltpu.PrefetchScalarGridSpec(
            num_scalar_prefetch=1,
            grid=(width // span,),
            in_specs=[
                pl.BlockSpec((rows, span), block),
                pl.BlockSpec((rows, 1), whole),
                pl.BlockSpec((1, span), block),
                pl.BlockSpec((rows, columns), whole),
                pl.BlockSpec((rows, 1), whole),
            ]
            + weight_specs(span, columns),
            out_specs=pl.BlockSpec((rows, span), block),
        ),
        out_shape=jax.ShapeDtypeStruct((rows, width), jnp.bfloat16),
        compiler_params=pltpu.CompilerParams(vmem_limit_bytes=LIMIT),
        cost_estimate=pl.CostEstimate(
            flops=2 * rows * width * columns,
            bytes_accessed=4 * rows * width + 2 * width * columns,
            transcendentals=0,
        ),
    )(table, tokens, inverse, gain, cotangent, moment, *weights)


def swap(array, axis, mask):
    size = lax.axis_size(axis)
    return lax.ppermute(array, axis, [(i, i ^ mask) for i in range(size)])


def swap_z(array, odd):
    size = lax.axis_size("zh") * lax.axis_size("zl")
    if odd:
        pairs = [(i, (i + 1 if i % 2 else i - 1) % size) for i in range(size)]
    else:
        pairs = [(i, i ^ 1) for i in range(size)]
    return lax.ppermute(array, ("zh", "zl"), pairs)


def halve(total):
    return total[1].astype(jnp.bfloat16), total[0]


def reduce_grads(sent, kept):
    moves = (
        lambda a: swap(a, "y", 1),
        lambda a: swap(a, "y", 3),
        lambda a: swap_z(a, False),
        lambda a: swap_z(a, True),
    )
    for order in ((0, 1, 2, 3), (2, 3, 0, 1)):
        got = [moves[m](s) for m, s in zip(order, sent)]
        totals = [k + g.astype(jnp.float32) for k, g in zip(kept, got)]
        sent, kept = zip(*[halve(t) for t in totals])
    got_even = swap(jnp.stack([sent[0], sent[2]]), "y", 3)
    got_odd = swap(jnp.stack([sent[1], sent[3]]), "y", 1)
    got = (got_even[0], got_odd[0], got_even[1], got_odd[1])
    total = jnp.stack([k + g.astype(jnp.float32) for k, g in zip(kept, got)], axis=1)
    out = total[0]
    for mask in (1, 3, 2):
        out = out + swap(total[mask].astype(jnp.bfloat16), "x", mask).astype(jnp.float32)
    for mask in (1, 3):
        send = out.astype(jnp.bfloat16)
        out = send.astype(jnp.float32) + swap(send, "zh", mask).astype(jnp.float32)
    return out


def gather_weight(own):
    up = swap_z(own, False)
    near, far = swap(own, "x", 1), swap(own, "x", 3)
    up_near, up_far = swap(up, "x", 1), swap(up, "x", 3)
    half = own.shape[0] // 2
    top = swap(jnp.stack([far[:half], up_far[:half]]), "x", 1)
    low = swap(jnp.stack([near[half:], up_near[half:]]), "x", 3)
    first = jnp.stack([own, up, near, far])
    second = jnp.concatenate(
        [up_near[None], up_far[None], jnp.concatenate([top, low], axis=1)], axis=0
    )
    return (first, second, swap(first, "c", 1), swap(second, "c", 1))


ORDER = ((0, 0), (1, 0), (0, 1), (0, 3), (1, 1), (1, 3), (0, 2), (1, 2))


def order_kernel(tab_ref, in_ref, out_ref):
    nodes, quarters = in_ref.shape[:2]
    for node in range(nodes):
        for quarter in range(quarters):
            row = in_ref[tab_ref[node], pl.ds(tab_ref[nodes] ^ quarter, 1)]
            out_ref[node * quarters + quarter, :] = row[0]


def order_rows(rows, table):
    nodes, quarters, lanes = rows.shape
    return pl.pallas_call(
        order_kernel,
        grid_spec=pltpu.PrefetchScalarGridSpec(
            num_scalar_prefetch=1,
            grid=(1,),
            in_specs=[pl.BlockSpec(rows.shape, lambda i, tab: (0, 0, 0))],
            out_specs=pl.BlockSpec((nodes * quarters, lanes), lambda i, tab: (0, 0)),
        ),
        out_shape=jax.ShapeDtypeStruct((nodes * quarters, lanes), rows.dtype),
    )(table.astype(jnp.int32), rows)


def shards(tokens, norm_gain, weight_values, weight_scale, key_cotangent):
    y, zl, x, c = (lax.axis_index(a) for a in ("y", "zl", "x", "c"))
    width = tokens.shape[1]
    columns = weight_values.shape[1]
    gain = norm_gain.reshape(1, width)
    own_weight = widen_weight(weight_values, weight_scale)
    weights = gather_weight(own_weight)
    shards_at = jnp.stack(
        [((zl ^ rz) * 4 + (x ^ rx)) * 2 + (c ^ rc) for rc in (0, 1) for rz, rx in ORDER]
    ).astype(jnp.int32)

    label = jnp.arange(32, dtype=jnp.int32)
    chip = (zl ^ (label // 16)) * 4 + (x ^ (label // 4 % 4))
    other_at = (chip * 2 + 1 - c) * 4 + (y ^ (label % 4))
    own_at = jnp.stack(
        [((zl ^ rz) * 4 + (x ^ rx)) * 2 + c for rz in (1, 0) for rx in range(4)] + [y]
    ).astype(jnp.int32)
    cot_own = key_cotangent.T
    cot_got = swap(cot_own, "c", 1)
    other, inverse = norm_tiles(tokens, gain, other_at)
    got = swap(other, "c", 1)
    sent, kept = grad_tiles(tokens, inverse, gain, got, cot_own, cot_got, own_at)
    devices = 1
    for axis in EVERY:
        devices *= lax.axis_size(axis)
    mine = reduce_grads(sent, kept) / devices

    projected, moment = forward(tokens, inverse, gain, key_cotangent, weights, shards_at)
    token_grads = backward(tokens, inverse, gain, key_cotangent, moment, weights, shards_at)

    mine = mine.reshape(columns, TILE)
    node = (zl * 4 + x) * 2 + c
    my_weight = lax.dynamic_slice_in_dim(own_weight, y * TILE, TILE, 0).T.astype(jnp.float32)
    my_gain = lax.dynamic_slice_in_dim(gain, node * columns + y * TILE, TILE, 1)
    gain_part = jnp.sum(my_weight * mine, axis=0, keepdims=True) / my_gain
    high = gain_part.astype(jnp.bfloat16)
    low = (gain_part - high.astype(jnp.float32)).astype(jnp.bfloat16)
    packed = jnp.concatenate(
        [mine.astype(jnp.bfloat16), high, low, jnp.zeros((14, TILE), jnp.bfloat16)], axis=0
    )
    pieces = [packed] + [swap(packed, "y", mask) for mask in (1, 2, 3)]
    stacked = jnp.stack([p[:columns] for p in pieces])
    ordered = [lax.dynamic_index_in_dim(stacked, y ^ q, 0, keepdims=False) for q in range(4)]
    weight_grads = jnp.concatenate(ordered, axis=1).astype(jnp.float32).T
    tails = jnp.stack([p[columns : columns + 2].astype(jnp.float32) for p in pieces])
    gains = (tails[:, 0] + tails[:, 1])[None]
    gains = jnp.concatenate([gains, swap(gains, "c", 1)])
    gains = jnp.concatenate([gains] + [swap(gains, "x", mask) for mask in (1, 2, 3)])
    gains = jnp.concatenate([gains, swap(gains, "zl", 1)])
    node_at = jnp.arange(16, dtype=jnp.int32)
    table = (node_at // 8 ^ zl) * 8 + (node_at // 2 % 4 ^ x) * 2 + (node_at % 2 ^ c)
    gain_grads = order_rows(gains, jnp.append(table, y)).reshape(width)
    return (projected, token_grads, weight_grads, gain_grads)


def solution(mesh):
    fine = Mesh(mesh.devices.reshape(4, 4, 2, 4, 2), EVERY)
    rows = P(EVERY, None)
    return jax.shard_map(
        shards,
        mesh=fine,
        in_specs=(rows, P(), P(NODE, None), P(NODE, None), rows),
        out_specs=(rows, rows, P(NODE, None), P()),
        check_vma=False,
    )
```

```python
import functools

import jax
import jax.numpy as jnp
from jax import lax
from jax.experimental import pallas as pl
from jax.experimental.pallas import tpu as pltpu
from jax.sharding import Mesh, PartitionSpec as P

NODE = ("zl", "x", "c")
EVERY = ("y", "zh", "zl", "x", "c")
TILE = 128
GROUPS = 4
Y_MASKS = ((1, 3), (3, 1), (1, 3), (3, 1))
LIMIT = 48 * 2**20


def widen_kernel(values_ref, scales_ref, out_ref):
    blocks = scales_ref.shape[1]
    block = values_ref.shape[1] // blocks
    for k in range(blocks):
        part = slice(k * block, (k + 1) * block)
        wide = values_ref[:, part].astype(jnp.float32)
        scale = scales_ref[:, k : k + 1].astype(jnp.float32)
        out_ref[:, part] = (wide * scale).astype(jnp.bfloat16)


def widen_weight(values, scales):
    return pl.pallas_call(
        widen_kernel, out_shape=jax.ShapeDtypeStruct(values.shape, jnp.bfloat16)
    )(values, scales)


def norm_kernel(tab_ref, tok_ref, gain_ref, own_ref, oth_ref, inv_ref):
    rows, width = tok_ref.shape
    total = jnp.zeros((rows, TILE), jnp.float32)
    for t in range(width // TILE):
        wide = tok_ref[:, t * TILE : (t + 1) * TILE].astype(jnp.float32)
        total = total + wide * wide
    mean = jnp.sum(total, axis=1, keepdims=True) / width
    inverse = lax.rsqrt(mean + 1e-05)
    inv_ref[...] = inverse
    for side, out_ref in enumerate((own_ref, oth_ref)):
        for r in range(width // TILE // 2):
            at = pl.multiple_of(tab_ref[side, r] * TILE, TILE)
            wide = tok_ref[:, pl.ds(at, TILE)].astype(jnp.float32)
            scaled = wide * inverse * gain_ref[:, pl.ds(at, TILE)]
            out_ref[:, r * TILE : (r + 1) * TILE] = scaled.astype(jnp.bfloat16)


def norm_tiles(tokens, gain, table):
    rows, width = tokens.shape
    step = 64 if rows % 64 == 0 else rows
    half = pl.BlockSpec((step, width // 2), lambda i, tab: (i, 0))
    return pl.pallas_call(
        norm_kernel,
        grid_spec=pltpu.PrefetchScalarGridSpec(
            num_scalar_prefetch=1,
            grid=(rows // step,),
            in_specs=[
                pl.BlockSpec((step, width), lambda i, tab: (i, 0)),
                pl.BlockSpec((1, width), lambda i, tab: (0, 0)),
            ],
            out_specs=[half, half, pl.BlockSpec((step, 1), lambda i, tab: (i, 0))],
        ),
        out_shape=[
            jax.ShapeDtypeStruct((rows, width // 2), jnp.bfloat16),
            jax.ShapeDtypeStruct((rows, width // 2), jnp.bfloat16),
            jax.ShapeDtypeStruct((rows, 1), jnp.float32),
        ],
        compiler_params=pltpu.CompilerParams(vmem_limit_bytes=LIMIT),
        cost_estimate=pl.CostEstimate(
            flops=6 * rows * width, bytes_accessed=4 * rows * width, transcendentals=rows
        ),
    )(table, tokens, gain)


def place(group, rz, ry, rx):
    first, second = Y_MASKS[group]
    y1, y2 = next(
        (a, b) for a in (0, 1) for b in (0, 1) if (a * first) ^ (b * second) == ry
    )
    if group < 2:
        return y1, (rz * 2 + y2) * 4 + rx
    return rz, (y1 * 2 + y2) * 4 + rx


def grad_kernel(own_ref, got_ref, cot_own_ref, cot_got_ref, *out_refs):
    span = 2 * TILE
    cot_own = cot_own_ref[...]
    cot_got = cot_got_ref[...]
    for pair in range(own_ref.shape[1] // span):
        part = slice(pair * span, (pair + 1) * span)
        grads = jnp.dot(cot_own, own_ref[:, part], preferred_element_type=jnp.float32)
        grads += jnp.dot(cot_got, got_ref[:, part], preferred_element_type=jnp.float32)
        for which in range(2):
            tile = pair * 2 + which
            for group in range(GROUPS):
                piece = grads[
                    group * TILE : (group + 1) * TILE, which * TILE : (which + 1) * TILE
                ]
                sent, at = place(group, tile // 16, tile // 4 % 4, tile % 4)
                if sent:
                    out_refs[group][at] = piece.astype(jnp.bfloat16)
                else:
                    out_refs[GROUPS + group][at] = piece


def grad_tiles(own, got, cot_own, cot_got):
    rows, width = own.shape
    tiles = width // TILE // 2
    shape = (tiles, TILE, TILE)
    outs = pl.pallas_call(
        grad_kernel,
        out_shape=[jax.ShapeDtypeStruct(shape, jnp.bfloat16)] * GROUPS
        + [jax.ShapeDtypeStruct(shape, jnp.float32)] * GROUPS,
        compiler_params=pltpu.CompilerParams(vmem_limit_bytes=LIMIT),
        cost_estimate=pl.CostEstimate(
            flops=4 * rows * width * GROUPS * TILE,
            bytes_accessed=4 * rows * width + 6 * GROUPS * tiles * TILE * TILE,
            transcendentals=0,
        ),
    )(own, got, cot_own, cot_got)
    return outs[:GROUPS], outs[GROUPS:]


def forward_kernel(tab_ref, tok_ref, inv_ref, gain_ref, cot_ref, *refs):
    w_refs, (proj_ref, moment_ref, acc) = refs[:-3], refs[-3:]
    inverse = inv_ref[...]
    acc[...] = jnp.zeros_like(acc)
    for k, (slot, pieces) in enumerate(PIECES):
        span = tok_ref.shape[1] // len(PIECES)
        at = pl.multiple_of(tab_ref[k] * span, span)
        wide = tok_ref[:, pl.ds(at, span)].astype(jnp.float32)
        normed = (wide * inverse * gain_ref[:, pl.ds(at, span)]).astype(jnp.bfloat16)
        part = span // len(pieces)
        for h, which in enumerate(pieces):
            acc[...] += jnp.dot(
                normed[:, h * part : (h + 1) * part],
                w_refs[which][slot],
                preferred_element_type=jnp.float32,
            )
    keys = acc[...]
    proj_ref[...] = keys.astype(jnp.bfloat16)
    inner = jnp.sum(cot_ref[...].astype(jnp.float32) * keys, axis=1, keepdims=True)
    moment_ref[...] = inverse * inverse * inner / tok_ref.shape[1]


def backward_kernel(tab_ref, tok_ref, inv_ref, gain_ref, cot_ref, moment_ref, *refs):
    w_refs, grads_ref = refs[:-1], refs[-1]
    inverse, moment, cot = inv_ref[...], moment_ref[...], cot_ref[...]
    for k, (slot, pieces) in enumerate(PIECES):
        span = tok_ref.shape[1] // len(PIECES)
        part = span // len(pieces)
        for h, which in enumerate(pieces):
            at = pl.multiple_of(tab_ref[k] * span + h * part, part)
            partial = lax.dot_general(
                cot, w_refs[which][slot], (((1,), (1,)), ((), ())), preferred_element_type=jnp.float32
            )
            wide = tok_ref[:, pl.ds(at, part)].astype(jnp.float32)
            grads = inverse * gain_ref[:, pl.ds(at, part)] * partial - wide * moment
            grads_ref[:, pl.ds(at, part)] = grads.astype(jnp.bfloat16)


def forward(tokens, inverse, gain, cotangent, weights, table):
    rows, width = tokens.shape
    columns = cotangent.shape[1]
    count = len(weights)
    return pl.pallas_call(
        forward_kernel,
        in_specs=[pl.BlockSpec(memory_space=pltpu.SMEM)]
        + [pl.BlockSpec(memory_space=pltpu.VMEM)] * (4 + count),
        out_specs=[pl.BlockSpec(memory_space=pltpu.VMEM)] * 2,
        out_shape=[
            jax.ShapeDtypeStruct((rows, columns), jnp.bfloat16),
            jax.ShapeDtypeStruct((rows, 1), jnp.float32),
        ],
        scratch_shapes=[pltpu.VMEM((rows, columns), jnp.float32)],
        compiler_params=pltpu.CompilerParams(vmem_limit_bytes=LIMIT),
        cost_estimate=pl.CostEstimate(
            flops=2 * rows * width * columns,
            bytes_accessed=2 * rows * width + 2 * width * columns,
            transcendentals=0,
        ),
    )(table, tokens, inverse, gain, cotangent, *weights)


def backward(tokens, inverse, gain, cotangent, moment, weights, table):
    rows, width = tokens.shape
    columns = cotangent.shape[1]
    count = len(weights)
    return pl.pallas_call(
        backward_kernel,
        in_specs=[pl.BlockSpec(memory_space=pltpu.SMEM)]
        + [pl.BlockSpec(memory_space=pltpu.VMEM)] * (5 + count),
        out_specs=pl.BlockSpec(memory_space=pltpu.VMEM),
        out_shape=jax.ShapeDtypeStruct((rows, width), jnp.bfloat16),
        compiler_params=pltpu.CompilerParams(vmem_limit_bytes=LIMIT),
        cost_estimate=pl.CostEstimate(
            flops=2 * rows * width * columns,
            bytes_accessed=4 * rows * width + 2 * width * columns,
            transcendentals=0,
        ),
    )(table, tokens, inverse, gain, cotangent, moment, *weights)


def swap(array, axis, mask):
    size = lax.axis_size(axis)
    return lax.ppermute(array, axis, [(i, i ^ mask) for i in range(size)])


def swap_z(array, odd):
    size = lax.axis_size("zh") * lax.axis_size("zl")
    if odd:
        pairs = [(i, (i + 1 if i % 2 else i - 1) % size) for i in range(size)]
    else:
        pairs = [(i, i ^ 1) for i in range(size)]
    return lax.ppermute(array, ("zh", "zl"), pairs)


def halve(total):
    half = total.shape[0] // 2
    return total[half:].astype(jnp.bfloat16), total[:half]


def tie(first, *others):
    return lax.optimization_barrier((first, *others))[0]


def exchange(sent, order):
    moves = (
        lambda a: swap(a, "y", 1),
        lambda a: swap(a, "y", 3),
        lambda a: swap_z(a, False),
        lambda a: swap_z(a, True),
    )
    return [moves[m](s) for m, s in zip(order, sent)]


def add_halve(kept, got):
    return zip(*[halve(k + g.astype(jnp.float32)) for k, g in zip(kept, got)])


PIECES = tuple((k % 8, (k // 8,)) for k in range(16))


def pack_kernel(tab_ref, sent_ref, got_ref, weight_ref, gain_ref, out_ref, *, devices):
    columns = sent_ref.shape[0]
    mine = (sent_ref[...].astype(jnp.float32) + got_ref[...].astype(jnp.float32)) / devices
    out_ref[:columns, :] = mine.astype(jnp.bfloat16)
    rows = pl.ds(pl.multiple_of(tab_ref[0] * TILE, TILE), TILE)
    weight = weight_ref[rows, :].astype(jnp.float32).T
    gain = gain_ref[:, pl.ds(pl.multiple_of(tab_ref[1] * TILE, TILE), TILE)]
    part = jnp.sum(weight * mine, axis=0, keepdims=True) / gain
    high = part.astype(jnp.bfloat16).astype(jnp.float32)
    tail = out_ref.shape[0] - columns
    row = lax.broadcasted_iota(jnp.int32, (tail, TILE), 0)
    ends = jnp.where(row == 0, high, jnp.where(row == 1, part - high, 0.0))
    out_ref[columns:, :] = ends.astype(jnp.bfloat16)


def pack(sent, got, weight, gain, table, devices):
    vmem = pl.BlockSpec(memory_space=pltpu.VMEM)
    return pl.pallas_call(
        functools.partial(pack_kernel, devices=devices),
        in_specs=[pl.BlockSpec(memory_space=pltpu.SMEM)] + [vmem] * 4,
        out_specs=vmem,
        out_shape=jax.ShapeDtypeStruct((sent.shape[0] + 16, TILE), jnp.bfloat16),
    )(table, sent, got, weight, gain)


def finish_kernel(tab_ref, *refs):
    parts, (weight_ref, gain_ref) = refs[:4], refs[4:]
    columns = weight_ref.shape[1]
    for k, part in enumerate(parts):
        quarter = tab_ref[0] ^ k
        rows = pl.ds(pl.multiple_of(quarter * TILE, TILE), TILE)
        weight_ref[rows, :] = part[:columns, :].astype(jnp.float32).T
        ends = part[columns:, :].astype(jnp.float32)
        gain_ref[pl.ds(quarter, 1), :] = ends[0:1] + ends[1:2]


def finish(parts, table):
    vmem = pl.BlockSpec(memory_space=pltpu.VMEM)
    columns = parts[0].shape[0] - 16
    return pl.pallas_call(
        finish_kernel,
        in_specs=[pl.BlockSpec(memory_space=pltpu.SMEM)] + [vmem] * 4,
        out_specs=[vmem] * 2,
        out_shape=[
            jax.ShapeDtypeStruct((4 * TILE, columns), jnp.float32),
            jax.ShapeDtypeStruct((4, TILE), jnp.float32),
        ],
    )(table, *parts)


def order_kernel(tab_ref, in_ref, out_ref):
    for node in range(in_ref.shape[0]):
        out_ref[node] = in_ref[tab_ref[node]]


def order(rows, table):
    vmem = pl.BlockSpec(memory_space=pltpu.VMEM)
    return pl.pallas_call(
        order_kernel,
        in_specs=[pl.BlockSpec(memory_space=pltpu.SMEM), vmem],
        out_specs=vmem,
        out_shape=jax.ShapeDtypeStruct(rows.shape, rows.dtype),
    )(table, rows)


def shards(tokens, norm_gain, weight_values, weight_scale, key_cotangent):
    y, zl, x, c = (lax.axis_index(a) for a in ("y", "zl", "x", "c"))
    width = tokens.shape[1]
    columns = weight_values.shape[1]
    gain = norm_gain.reshape(1, width)
    devices = 1
    for axis in EVERY:
        devices *= lax.axis_size(axis)
    label = jnp.arange(32, dtype=jnp.int32)
    chip = (zl ^ (label // 16)) * 4 + (x ^ (label % 4))
    quarter = y ^ (label // 4 % 4)
    table = jnp.stack([(chip * 2 + side) * 4 + quarter for side in (c, 1 - c)])
    shards_at = jnp.arange(16, dtype=jnp.int32) ^ (zl * 8)

    own_weight = widen_weight(weight_values, weight_scale)
    up = swap_z(own_weight, False)
    weights = [lax.all_gather(part, ("x", "c"), axis=0) for part in (own_weight, up)]
    cot_own = key_cotangent.T
    cot_got = swap(cot_own, "c", 1)
    mine, other, inverse = norm_tiles(tie(tokens, own_weight, cot_own), gain, table)
    got = swap(other, "c", 1)
    sent, kept = grad_tiles(mine, got, cot_own, cot_got)

    moved = exchange(sent, (0, 1, 2, 3))
    sent, kept = add_halve(kept, moved)
    moved = exchange(sent, (2, 3, 0, 1))
    sent, kept = add_halve(kept, moved)
    even = swap(jnp.stack([sent[0], sent[2]]), "y", 3)
    odd = swap(jnp.stack([sent[1], sent[3]]), "y", 1)
    moved = (even[0], odd[0], even[1], odd[1])
    total = jnp.stack([k + m.astype(jnp.float32) for k, m in zip(kept, moved)], axis=1)
    out = total[0]
    for mask in (1, 3, 2):
        out = out + swap(total[mask].astype(jnp.bfloat16), "x", mask).astype(jnp.float32)
    send = out.astype(jnp.bfloat16)

    send, *weights = lax.optimization_barrier((send, *weights))
    arrived = swap(send, "zh", 1)
    projected, moment = forward(tokens, inverse, gain, key_cotangent, weights, shards_at)
    arrived, moment = lax.optimization_barrier((arrived, moment))
    send = (send.astype(jnp.float32) + arrived.astype(jnp.float32)).astype(jnp.bfloat16)
    arrived = swap(send, "zh", 3)

    node = (zl * 4 + x) * 2 + c
    at = jnp.stack([y, node * 4 + y]).astype(jnp.int32)
    packed = pack(
        send.reshape(columns, TILE), arrived.reshape(columns, TILE), own_weight, gain, at, devices
    )
    packed, moment = lax.optimization_barrier((packed, moment))
    pieces = [packed] + [swap(packed, "y", mask) for mask in (1, 2, 3)]
    token_grads = backward(tokens, inverse, gain, key_cotangent, moment, weights, shards_at)
    pieces[3] = tie(pieces[3], token_grads)
    weight_grads, gains = finish(pieces, at)
    gains = gains[None]
    gains = jnp.concatenate([gains, swap(gains, "c", 1)])
    gains = jnp.concatenate([gains] + [swap(gains, "x", mask) for mask in (1, 2, 3)])
    gains = jnp.concatenate([gains, swap(gains, "zl", 1)])
    nodes = jnp.arange(16, dtype=jnp.int32)
    relative = (nodes // 8 ^ zl) * 8 + (nodes // 2 % 4 ^ x) * 2 + (nodes % 2 ^ c)
    gain_grads = order(gains, relative.astype(jnp.int32)).reshape(width)
    return (projected, token_grads, weight_grads, gain_grads)


def solution(mesh):
    fine = Mesh(mesh.devices.reshape(4, 4, 2, 4, 2), EVERY)
    rows = P(EVERY, None)
    return jax.shard_map(
        shards,
        mesh=fine,
        in_specs=(rows, P(), P(NODE, None), P(NODE, None), rows),
        out_specs=(rows, rows, P(NODE, None), P()),
        check_vma=False,
    )
```

```python
import functools

import jax
import jax.numpy as jnp
from jax import lax
from jax.experimental import pallas as pl
from jax.experimental.pallas import tpu as pltpu
from jax.sharding import Mesh, PartitionSpec as P

NODE = ("zl", "x", "c")
EVERY = ("y", "zh", "zl", "x", "c")
TILE = 128
LIMIT = 48 * 2**20


def widen_kernel(values_ref, scales_ref, out_ref):
    blocks = scales_ref.shape[0]
    block = values_ref.shape[1] // blocks
    scales = scales_ref[...].astype(jnp.float32)
    scales = jnp.concatenate([scales] * (8 // blocks), axis=0).T
    for k in range(blocks):
        part = slice(k * block, (k + 1) * block)
        wide = values_ref[:, part].astype(jnp.float32)
        out_ref[:, part] = (wide * scales[:, k : k + 1]).astype(jnp.bfloat16)


def widen_weight(values, scales):
    return pl.pallas_call(
        widen_kernel, out_shape=jax.ShapeDtypeStruct(values.shape, jnp.bfloat16)
    )(values, scales.T)


def norm_kernel(tab_ref, tok_ref, gain_ref, own_ref, oth_ref, inv_ref):
    rows, width = tok_ref.shape
    total = jnp.zeros((rows, TILE), jnp.float32)
    for t in range(width // TILE):
        wide = tok_ref[:, t * TILE : (t + 1) * TILE].astype(jnp.float32)
        total = total + wide * wide
    mean = jnp.sum(total, axis=1, keepdims=True) / width
    inverse = lax.rsqrt(mean + 1e-05)
    inv_ref[...] = inverse
    for side, out_ref in enumerate((own_ref, oth_ref)):
        for r in range(width // TILE // 2):
            at = pl.multiple_of(tab_ref[side, r] * TILE, TILE)
            wide = tok_ref[:, pl.ds(at, TILE)].astype(jnp.float32)
            scaled = wide * inverse * gain_ref[:, pl.ds(at, TILE)]
            out_ref[:, r * TILE : (r + 1) * TILE] = scaled.astype(jnp.bfloat16)


def norm_tiles(tokens, gain, table):
    rows, width = tokens.shape
    step = 64 if rows % 64 == 0 else rows
    half = pl.BlockSpec((step, width // 2), lambda i, tab: (i, 0))
    return pl.pallas_call(
        norm_kernel,
        grid_spec=pltpu.PrefetchScalarGridSpec(
            num_scalar_prefetch=1,
            grid=(rows // step,),
            in_specs=[
                pl.BlockSpec((step, width), lambda i, tab: (i, 0)),
                pl.BlockSpec((1, width), lambda i, tab: (0, 0)),
            ],
            out_specs=[half, half, pl.BlockSpec((step, 1), lambda i, tab: (i, 0))],
        ),
        out_shape=[
            jax.ShapeDtypeStruct((rows, width // 2), jnp.bfloat16),
            jax.ShapeDtypeStruct((rows, width // 2), jnp.bfloat16),
            jax.ShapeDtypeStruct((rows, 1), jnp.float32),
        ],
        compiler_params=pltpu.CompilerParams(vmem_limit_bytes=LIMIT),
        cost_estimate=pl.CostEstimate(
            flops=6 * rows * width, bytes_accessed=4 * rows * width, transcendentals=rows
        ),
    )(table, tokens, gain)


def grad_kernel(own_ref, got_ref, cot_own_ref, cot_got_ref, *out_refs):
    span = 2 * TILE
    half = cot_own_ref.shape[0] // 2
    cot_own = cot_own_ref[...]
    cot_got = cot_got_ref[...]
    for pair in range(own_ref.shape[1] // span):
        part = slice(pair * span, (pair + 1) * span)
        grads = jnp.dot(cot_own, own_ref[:, part], preferred_element_type=jnp.float32)
        grads += jnp.dot(cot_got, got_ref[:, part], preferred_element_type=jnp.float32)
        for which in range(2):
            tile = pair * 2 + which
            z, y1, rest = tile // 16, tile // 8 % 2, tile % 8
            for side, (sent, at) in enumerate(((y1, z * 8 + rest), (z, y1 * 8 + rest))):
                piece = grads[side * half : (side + 1) * half, which * TILE : (which + 1) * TILE]
                if sent:
                    out_refs[side][at] = piece.astype(jnp.bfloat16)
                else:
                    out_refs[2 + side][at] = piece


def grad_tiles(own, got, cot_own, cot_got):
    rows, width = own.shape
    columns = cot_own.shape[0]
    tiles = width // TILE // 2
    shape = (tiles, columns // 2, TILE)
    outs = pl.pallas_call(
        grad_kernel,
        out_shape=[jax.ShapeDtypeStruct(shape, jnp.bfloat16)] * 2
        + [jax.ShapeDtypeStruct(shape, jnp.float32)] * 2,
        compiler_params=pltpu.CompilerParams(vmem_limit_bytes=LIMIT),
        cost_estimate=pl.CostEstimate(
            flops=4 * rows * width * columns,
            bytes_accessed=4 * rows * width + 6 * columns * tiles * TILE,
            transcendentals=0,
        ),
    )(own, got, cot_own, cot_got)
    return outs[:2], outs[2:]


def block_in(tab_ref, tok_ref, block, sem, k):
    span = block.shape[2]
    at = pl.multiple_of(tab_ref[k] * span, span)
    return pltpu.make_async_copy(tok_ref.at[:, pl.ds(at, span)], block.at[k], sem.at[k])


def forward_kernel(tab_ref, tok_ref, inv_ref, gain_ref, cot_ref, *refs):
    w_refs, (proj_ref, moment_ref, acc, block, sem) = refs[:-5], refs[-5:]
    count, _, span = block.shape
    for k in range(count):
        block_in(tab_ref, tok_ref, block, sem, k).start()
    inverse = inv_ref[...]
    acc[...] = jnp.zeros_like(acc)
    for k in range(count):
        block_in(tab_ref, tok_ref, block, sem, k).wait()
        at = pl.multiple_of(tab_ref[k] * span, span)
        wide = block[k].astype(jnp.float32)
        normed = (wide * inverse * gain_ref[:, pl.ds(at, span)]).astype(jnp.bfloat16)
        acc[...] += jnp.dot(normed, w_refs[k // 2][k % 2], preferred_element_type=jnp.float32)
    keys = acc[...]
    proj_ref[...] = keys.astype(jnp.bfloat16)
    inner = jnp.sum(cot_ref[...].astype(jnp.float32) * keys, axis=1, keepdims=True)
    moment_ref[...] = inverse * inverse * inner / (count * span)


def backward_kernel(tab_ref, tok_ref, inv_ref, gain_ref, cot_ref, moment_ref, *refs):
    w_refs, (grads_ref, block, out, sem, out_sem) = refs[:-5], refs[-5:]
    count, _, span = block.shape

    def block_out(k):
        at = pl.multiple_of(tab_ref[k] * span, span)
        return pltpu.make_async_copy(out.at[k], grads_ref.at[:, pl.ds(at, span)], out_sem.at[k])

    for k in range(count):
        block_in(tab_ref, tok_ref, block, sem, k).start()
    inverse, moment, cot = inv_ref[...], moment_ref[...], cot_ref[...]
    for k in range(count):
        partial = lax.dot_general(
            cot, w_refs[k // 2][k % 2], (((1,), (1,)), ((), ())), preferred_element_type=jnp.float32
        )
        block_in(tab_ref, tok_ref, block, sem, k).wait()
        at = pl.multiple_of(tab_ref[k] * span, span)
        wide = block[k].astype(jnp.float32)
        grads = inverse * gain_ref[:, pl.ds(at, span)] * partial - wide * moment
        out[k] = grads.astype(jnp.bfloat16)
        block_out(k).start()
    for k in range(count):
        block_out(k).wait()


def forward(tokens, inverse, gain, cotangent, weights, table):
    rows, width = tokens.shape
    columns = cotangent.shape[1]
    span = weights[0].shape[1]
    count = width // span
    vmem = pl.BlockSpec(memory_space=pltpu.VMEM)
    return pl.pallas_call(
        forward_kernel,
        in_specs=[pl.BlockSpec(memory_space=pltpu.SMEM), pl.BlockSpec(memory_space=pl.ANY)]
        + [vmem] * (3 + len(weights)),
        out_specs=[vmem] * 2,
        out_shape=[
            jax.ShapeDtypeStruct((rows, columns), jnp.bfloat16),
            jax.ShapeDtypeStruct((rows, 1), jnp.float32),
        ],
        scratch_shapes=[
            pltpu.VMEM((rows, columns), jnp.float32),
            pltpu.VMEM((count, rows, span), jnp.bfloat16),
            pltpu.SemaphoreType.DMA((count,)),
        ],
        compiler_params=pltpu.CompilerParams(vmem_limit_bytes=LIMIT),
        cost_estimate=pl.CostEstimate(
            flops=2 * rows * width * columns,
            bytes_accessed=2 * rows * width + 2 * width * columns,
            transcendentals=0,
        ),
    )(table, tokens, inverse, gain, cotangent, *weights)


def backward(tokens, inverse, gain, cotangent, moment, weights, table):
    rows, width = tokens.shape
    columns = cotangent.shape[1]
    span = weights[0].shape[1]
    count = width // span
    vmem = pl.BlockSpec(memory_space=pltpu.VMEM)
    return pl.pallas_call(
        backward_kernel,
        in_specs=[pl.BlockSpec(memory_space=pltpu.SMEM), pl.BlockSpec(memory_space=pl.ANY)]
        + [vmem] * (4 + len(weights)),
        out_specs=pl.BlockSpec(memory_space=pl.ANY),
        out_shape=jax.ShapeDtypeStruct((rows, width), jnp.bfloat16),
        scratch_shapes=[
            pltpu.VMEM((count, rows, span), jnp.bfloat16),
            pltpu.VMEM((count, rows, span), jnp.bfloat16),
            pltpu.SemaphoreType.DMA((count,)),
            pltpu.SemaphoreType.DMA((count,)),
        ],
        compiler_params=pltpu.CompilerParams(vmem_limit_bytes=LIMIT),
        cost_estimate=pl.CostEstimate(
            flops=2 * rows * width * columns,
            bytes_accessed=4 * rows * width + 2 * width * columns,
            transcendentals=0,
        ),
    )(table, tokens, inverse, gain, cotangent, moment, *weights)


def swap(array, axis):
    return lax.ppermute(array, axis, [(0, 1), (1, 0)])


def pair(array, axis, step):
    size = lax.axis_size(axis)
    masks = (1, 3) if step == 0 else (3, 1)
    moves = [(a * 2 + c, (a ^ masks[c]) * 2 + c) for a in range(size) for c in range(2)]
    return lax.ppermute(array, (axis, "c"), moves)


def pair_z(array):
    size = lax.axis_size("zh") * lax.axis_size("zl")
    moves = []
    for z in range(size):
        moves.append((z * 2, (z ^ 1) * 2))
        moves.append((z * 2 + 1, (z + (1 if z % 2 else -1)) % size * 2 + 1))
    return lax.ppermute(array, ("zh", "zl", "c"), moves)


def halve(total):
    half = total.shape[0] // 2
    return total[half:].astype(jnp.bfloat16), total[:half]


def add(kept, got):
    return kept + got.astype(jnp.float32)


def tie(first, *others):
    return lax.optimization_barrier((first, *others))[0]


PIECES = (
    ((0, 0, 0), (0, 0, 1), (1, 0, 0), (1, 0, 1), (0, 1, 0), (0, 1, 1), (0, 2, 1), (0, 2, 0))
    + ((1, 1, 0), (1, 1, 1), (1, 2, 1), (1, 2, 0), (0, 3, 0), (1, 3, 0), (0, 3, 1), (1, 3, 1))
)


def pack_kernel(tab_ref, sent_ref, got_ref, weight_ref, gain_ref, out_ref, *, devices):
    columns = sent_ref.shape[0]
    mine = (sent_ref[...].astype(jnp.float32) + got_ref[...].astype(jnp.float32)) / devices
    out_ref[:columns, :] = mine.astype(jnp.bfloat16)
    rows = pl.ds(pl.multiple_of(tab_ref[0] * TILE, TILE), TILE)
    weight = weight_ref[rows, :].astype(jnp.float32).T
    gain = gain_ref[:, pl.ds(pl.multiple_of(tab_ref[1] * TILE, TILE), TILE)]
    part = jnp.sum(weight * mine, axis=0, keepdims=True) / gain
    high = part.astype(jnp.bfloat16).astype(jnp.float32)
    tail = out_ref.shape[0] - columns
    row = lax.broadcasted_iota(jnp.int32, (tail, TILE), 0)
    ends = jnp.where(row == 0, high, jnp.where(row == 1, part - high, 0.0))
    out_ref[columns:, :] = ends.astype(jnp.bfloat16)


def pack(sent, got, weight, gain, table, devices):
    vmem = pl.BlockSpec(memory_space=pltpu.VMEM)
    return pl.pallas_call(
        functools.partial(pack_kernel, devices=devices),
        in_specs=[pl.BlockSpec(memory_space=pltpu.SMEM)] + [vmem] * 4,
        out_specs=vmem,
        out_shape=jax.ShapeDtypeStruct((sent.shape[0] + 16, TILE), jnp.bfloat16),
    )(table, sent, got, weight, gain)


def finish_kernel(tab_ref, near_ref, far_ref, weight_ref, gain_ref):
    columns = weight_ref.shape[1]
    for k in range(4):
        part = (near_ref, far_ref)[k // 2].at[k % 2]
        rows = pl.ds(pl.multiple_of(tab_ref[k] * TILE, TILE), TILE)
        weight_ref[rows, :] = part[:columns, :].astype(jnp.float32).T
        ends = part[columns:, :].astype(jnp.float32)
        gain_ref[pl.ds(tab_ref[k], 1), :] = ends[0:1] + ends[1:2]


def finish(parts, table):
    vmem = pl.BlockSpec(memory_space=pltpu.VMEM)
    columns = parts[0].shape[1] - 16
    return pl.pallas_call(
        finish_kernel,
        in_specs=[pl.BlockSpec(memory_space=pltpu.SMEM)] + [vmem] * 2,
        out_specs=[vmem] * 2,
        out_shape=[
            jax.ShapeDtypeStruct((4 * TILE, columns), jnp.float32),
            jax.ShapeDtypeStruct((4, TILE), jnp.float32),
        ],
    )(table, *parts)


def order_kernel(tab_ref, in_ref, out_ref):
    for node in range(in_ref.shape[0]):
        out_ref[node] = in_ref[tab_ref[node]]


def order(rows, table):
    vmem = pl.BlockSpec(memory_space=pltpu.VMEM)
    return pl.pallas_call(
        order_kernel,
        in_specs=[pl.BlockSpec(memory_space=pltpu.SMEM), vmem],
        out_specs=vmem,
        out_shape=jax.ShapeDtypeStruct(rows.shape, rows.dtype),
    )(table, rows)


def shards(tokens, norm_gain, weight_values, weight_scale, key_cotangent):
    y, zl, x, c = (lax.axis_index(a) for a in ("y", "zl", "x", "c"))
    width = tokens.shape[1]
    columns = weight_values.shape[1]
    gain = norm_gain.reshape(1, width)
    devices = 1
    for axis in EVERY:
        devices *= lax.axis_size(axis)

    def offset(core, first, second):
        masks = (1 + 2 * core, 3 - 2 * core)
        return first * masks[0] ^ second * masks[1]

    label = jnp.arange(32, dtype=jnp.int32)
    bits = [label // 16] + [label // k % 2 for k in (8, 4, 2, 1)]
    tables = []
    for core in (c, 1 - c):
        chip = (zl ^ bits[0]) * 4 + (x ^ offset(core, bits[3], bits[4]))
        tables.append((chip * 2 + core) * 4 + (y ^ offset(core, bits[1], bits[2])))
    shards_at = jnp.stack(
        [((zl ^ z) * 4 + (x ^ offset(c, k % 2, k // 2))) * 2 + (c ^ lane) for z, k, lane in PIECES]
    ).astype(jnp.int32)

    own = widen_weight(weight_values, weight_scale)
    own_c = swap(own, "c")
    up = pair_z(own)
    cot_own = key_cotangent.T
    cot_got = swap(cot_own, "c")
    mine, other, inverse = norm_tiles(tie(tokens, own, cot_own), gain, jnp.stack(tables))
    got = swap(other, "c")
    got, up = lax.optimization_barrier((got, up))
    base = jnp.stack([own, own_c])
    near = pair(base, "x", 0)
    up_c = swap(up, "c")
    sent, kept = grad_tiles(mine, got, cot_own, cot_got)

    first = sent[0]
    second, near, up_c = lax.optimization_barrier((sent[1], near, up_c))
    moved = (pair(first, "y", 0), pair_z(second))
    near_c = swap(near, "c")
    above = jnp.stack([up, up_c])
    above_near = pair(above, "x", 0)
    (first, kept_first), (second, kept_second) = (halve(add(k, m)) for k, m in zip(kept, moved))
    second, near_c, above_near = lax.optimization_barrier((second, near_c, above_near))
    moved = (pair_z(first), pair(second, "y", 0))
    above_near_c = swap(above_near, "c")
    far = pair(jnp.stack([near_c[1], above_near_c[1]]), "x", 0)
    (first, kept_first), (second, kept_second) = (
        halve(add(k, m)) for k, m in zip((kept_first, kept_second), moved)
    )
    moved = pair(jnp.stack([first, second]), "y", 1)
    total = jnp.stack([add(kept_first, moved[0]), add(kept_second, moved[1])], axis=1)
    send, kept = halve(total)
    send, far = lax.optimization_barrier((send, far))
    moved = pair(send, "x", 0)
    far_c = swap(far, "c")
    send, kept = halve(add(kept, moved))
    send, far_c = lax.optimization_barrier((send, far_c))
    weights = [base, above, near, near_c, above_near, above_near_c, far, far_c]

    moved = pair(send, "x", 1)
    projected, moment = forward(tokens, inverse, gain, key_cotangent, weights, shards_at)
    moved, moment = lax.optimization_barrier((moved, moment))
    send = add(kept, moved).astype(jnp.bfloat16).reshape(columns, TILE)
    moved = pair(send, "zh", 0)
    send = (send.astype(jnp.float32) + moved.astype(jnp.float32)).astype(jnp.bfloat16)
    moved = pair(send, "zh", 1)

    node = (zl * 4 + x) * 2 + c
    at = jnp.stack([y, node * 4 + y]).astype(jnp.int32)
    packed = pack(send, moved, own, gain, at, devices)[None]
    pieces = jnp.concatenate([packed, pair(packed, "y", 0)])
    pieces, moment = lax.optimization_barrier((pieces, moment))
    moved = pair(pieces, "y", 1)
    token_grads = backward(tokens, inverse, gain, key_cotangent, moment, weights, shards_at)
    moved = tie(moved, token_grads)
    quarters = jnp.stack([y ^ offset(c, k % 2, k // 2) for k in range(4)]).astype(jnp.int32)
    weight_grads, gains = finish((pieces, moved), quarters)
    gains = gains[None]
    for move in (
        lambda a: swap(a, "c"),
        lambda a: pair(a, "x", 0),
        lambda a: pair(a, "x", 1),
        lambda a: swap(a, "zl"),
    ):
        gains = jnp.concatenate([gains, move(gains)])
    nodes = jnp.arange(16, dtype=jnp.int32)
    across = nodes // 2 % 4 ^ x
    high, mixed = across // 2, across % 2 ^ across // 2
    step0, step1 = jnp.where(c == 0, mixed, high), jnp.where(c == 0, high, mixed)
    relative = (nodes // 8 ^ zl) * 8 + step1 * 4 + step0 * 2 + (nodes % 2 ^ c)
    gain_grads = order(gains, relative.astype(jnp.int32)).reshape(width)
    return (projected, token_grads, weight_grads, gain_grads)


def solution(mesh):
    fine = Mesh(mesh.devices.reshape(4, 4, 2, 4, 2), EVERY)
    rows = P(EVERY, None)
    return jax.shard_map(
        shards,
        mesh=fine,
        in_specs=(rows, P(), P(NODE, None), P(NODE, None), rows),
        out_specs=(rows, rows, P(NODE, None), P()),
        check_vma=False,
    )
```

```python
import functools

import jax
import jax.numpy as jnp
from jax import lax
from jax.experimental import pallas as pl
from jax.experimental.pallas import tpu as pltpu
from jax.sharding import Mesh, PartitionSpec as P

NODE = ("zl", "x", "c")
EVERY = ("y", "zh", "zl", "x", "c")
TILE = 128
EXTRA = 8
LIMIT = 16 * 2**20


def widen_kernel(values_ref, scales_ref, out_ref):
    blocks = scales_ref.shape[0]
    block = values_ref.shape[1] // blocks
    scales = scales_ref[...].astype(jnp.float32)
    scales = jnp.concatenate([scales] * (8 // blocks), axis=0).T
    for k in range(blocks):
        part = slice(k * block, (k + 1) * block)
        wide = values_ref[:, part].astype(jnp.float32)
        out_ref[:, part] = (wide * scales[:, k : k + 1]).astype(jnp.bfloat16)


def widen_weight(values, scales):
    return pl.pallas_call(
        widen_kernel, out_shape=jax.ShapeDtypeStruct(values.shape, jnp.bfloat16)
    )(values, scales.T)


def norm_kernel(tab_ref, tok_ref, gain_ref, own_ref, oth_ref, inv_ref):
    rows, width = tok_ref.shape
    total = jnp.zeros((rows, TILE), jnp.float32)
    for t in range(width // TILE):
        wide = tok_ref[:, t * TILE : (t + 1) * TILE].astype(jnp.float32)
        total = total + wide * wide
    mean = jnp.sum(total, axis=1, keepdims=True) / width
    inverse = lax.rsqrt(mean + 1e-05)
    inv_ref[...] = inverse
    for side, out_ref in enumerate((own_ref, oth_ref)):
        for r in range(width // TILE // 2):
            at = pl.multiple_of(tab_ref[side, r] * TILE, TILE)
            wide = tok_ref[:, pl.ds(at, TILE)].astype(jnp.float32)
            scaled = wide * inverse * gain_ref[:, pl.ds(at, TILE)]
            out_ref[:, r * TILE : (r + 1) * TILE] = scaled.astype(jnp.bfloat16)


def norm_tiles(tokens, gain, table):
    rows, width = tokens.shape
    step = 64 if rows % 64 == 0 else rows
    half = pl.BlockSpec((step, width // 2), lambda i, tab: (i, 0))
    return pl.pallas_call(
        norm_kernel,
        grid_spec=pltpu.PrefetchScalarGridSpec(
            num_scalar_prefetch=1,
            grid=(rows // step,),
            in_specs=[
                pl.BlockSpec((step, width), lambda i, tab: (i, 0)),
                pl.BlockSpec((1, width), lambda i, tab: (0, 0)),
            ],
            out_specs=[half, half, pl.BlockSpec((step, 1), lambda i, tab: (i, 0))],
        ),
        out_shape=[
            jax.ShapeDtypeStruct((rows, width // 2), jnp.bfloat16),
            jax.ShapeDtypeStruct((rows, width // 2), jnp.bfloat16),
            jax.ShapeDtypeStruct((rows, 1), jnp.float32),
        ],
        compiler_params=pltpu.CompilerParams(vmem_limit_bytes=LIMIT),
        cost_estimate=pl.CostEstimate(
            flops=6 * rows * width, bytes_accessed=4 * rows * width, transcendentals=rows
        ),
    )(table, tokens, gain)


def grad_kernel(own_ref, got_ref, cot_own_ref, cot_got_ref, *out_refs):
    span = 2 * TILE
    half = cot_own_ref.shape[0] // 2
    cot_own = cot_own_ref[...]
    cot_got = cot_got_ref[...]
    for pair in range(own_ref.shape[1] // span):
        part = slice(pair * span, (pair + 1) * span)
        grads = jnp.dot(cot_own, own_ref[:, part], preferred_element_type=jnp.float32)
        grads += jnp.dot(cot_got, got_ref[:, part], preferred_element_type=jnp.float32)
        for which in range(2):
            tile = pair * 2 + which
            z, y1, rest = tile // 16, tile // 8 % 2, tile % 8
            for side, (sent, at) in enumerate(((y1, z * 8 + rest), (z, y1 * 8 + rest))):
                piece = grads[side * half : (side + 1) * half, which * TILE : (which + 1) * TILE]
                if sent:
                    out_refs[side][at] = piece.astype(jnp.bfloat16)
                else:
                    out_refs[2 + side][at] = piece


def grad_tiles(own, got, cot_own, cot_got):
    rows, width = own.shape
    columns = cot_own.shape[0]
    tiles = width // TILE // 2
    shape = (tiles, columns // 2, TILE)
    outs = pl.pallas_call(
        grad_kernel,
        out_shape=[jax.ShapeDtypeStruct(shape, jnp.bfloat16)] * 2
        + [jax.ShapeDtypeStruct(shape, jnp.float32)] * 2,
        compiler_params=pltpu.CompilerParams(vmem_limit_bytes=LIMIT),
        cost_estimate=pl.CostEstimate(
            flops=4 * rows * width * columns,
            bytes_accessed=4 * rows * width + 6 * columns * tiles * TILE,
            transcendentals=0,
        ),
    )(own, got, cot_own, cot_got)
    return outs[:2], outs[2:]


def block_in(tab_ref, tok_ref, block, sem, k):
    span = block.shape[2]
    at = pl.multiple_of(tab_ref[k] * span, span)
    return pltpu.make_async_copy(tok_ref.at[:, pl.ds(at, span)], block.at[k], sem.at[k])


def forward_kernel(tab_ref, tok_ref, inv_ref, gain_ref, *refs):
    w_refs, acc_in, (acc, block, sem) = refs[:4], refs[4:-3], refs[-3:]
    count, _, span = block.shape
    for k in range(count):
        block_in(tab_ref, tok_ref, block, sem, k).start()
    inverse = inv_ref[...]
    acc[...] = acc_in[0][...] if acc_in else jnp.zeros_like(acc)
    for k in range(count):
        block_in(tab_ref, tok_ref, block, sem, k).wait()
        at = pl.multiple_of(tab_ref[k] * span, span)
        wide = block[k].astype(jnp.float32)
        normed = (wide * inverse * gain_ref[:, pl.ds(at, span)]).astype(jnp.bfloat16)
        acc[...] += jnp.dot(normed, w_refs[k // 2][k % 2], preferred_element_type=jnp.float32)


def forward_last_kernel(tab_ref, tok_ref, inv_ref, gain_ref, cot_ref, *refs):
    w_refs, acc_in, proj_ref, moment_ref, acc, block, sem = refs[:4], *refs[4:]
    forward_kernel(tab_ref, tok_ref, inv_ref, gain_ref, *w_refs, acc_in, acc, block, sem)
    keys = acc[...]
    inverse = inv_ref[...]
    proj_ref[...] = keys.astype(jnp.bfloat16)
    inner = jnp.sum(cot_ref[...].astype(jnp.float32) * keys, axis=1, keepdims=True)
    moment_ref[...] = inverse * inverse * inner / tok_ref.shape[1]


def backward_kernel(tab_ref, tok_ref, inv_ref, gain_ref, cot_ref, moment_ref, *refs):
    w_refs, (grads_ref, block, out, sem, out_sem) = refs[:4], refs[-5:]
    count, _, span = block.shape

    def block_out(k):
        at = pl.multiple_of(tab_ref[k] * span, span)
        return pltpu.make_async_copy(out.at[k], grads_ref.at[:, pl.ds(at, span)], out_sem.at[k])

    for k in range(count):
        block_in(tab_ref, tok_ref, block, sem, k).start()
    inverse, moment, cot = inv_ref[...], moment_ref[...], cot_ref[...]
    for k in range(count):
        partial = lax.dot_general(
            cot, w_refs[k // 2][k % 2], (((1,), (1,)), ((), ())), preferred_element_type=jnp.float32
        )
        block_in(tab_ref, tok_ref, block, sem, k).wait()
        at = pl.multiple_of(tab_ref[k] * span, span)
        wide = block[k].astype(jnp.float32)
        grads = inverse * gain_ref[:, pl.ds(at, span)] * partial - wide * moment
        out[k] = grads.astype(jnp.bfloat16)
        block_out(k).start()
    for k in range(count):
        block_out(k).wait()


VMEM = pl.BlockSpec(memory_space=pltpu.VMEM)
SMEM = pl.BlockSpec(memory_space=pltpu.SMEM)
ANY = pl.BlockSpec(memory_space=pl.ANY)


def costs(tokens, columns):
    rows, width = tokens.shape
    return dict(
        compiler_params=pltpu.CompilerParams(vmem_limit_bytes=LIMIT),
        cost_estimate=pl.CostEstimate(
            flops=rows * width * columns,
            bytes_accessed=2 * rows * width + width * columns,
            transcendentals=0,
        ),
    )


def forward(tokens, inverse, gain, weights, table):
    rows, span, columns = tokens.shape[0], *weights[0].shape[1:]
    return pl.pallas_call(
        forward_kernel,
        in_specs=[SMEM, ANY] + [VMEM] * 6,
        out_specs=VMEM,
        out_shape=jax.ShapeDtypeStruct((rows, columns), jnp.float32),
        scratch_shapes=[
            pltpu.VMEM((8, rows, span), jnp.bfloat16),
            pltpu.SemaphoreType.DMA((8,)),
        ],
        **costs(tokens, columns),
    )(table, tokens, inverse, gain, *weights)


def forward_last(tokens, inverse, gain, cotangent, weights, sums, table):
    rows, span, columns = tokens.shape[0], *weights[0].shape[1:]
    return pl.pallas_call(
        forward_last_kernel,
        in_specs=[SMEM, ANY] + [VMEM] * 8,
        out_specs=[VMEM] * 2,
        out_shape=[
            jax.ShapeDtypeStruct((rows, columns), jnp.bfloat16),
            jax.ShapeDtypeStruct((rows, 1), jnp.float32),
        ],
        scratch_shapes=[
            pltpu.VMEM((rows, columns), jnp.float32),
            pltpu.VMEM((8, rows, span), jnp.bfloat16),
            pltpu.SemaphoreType.DMA((8,)),
        ],
        **costs(tokens, columns),
    )(table, tokens, inverse, gain, cotangent, *weights, sums)


def backward(tokens, inverse, gain, cotangent, moment, weights, table, before=()):
    rows, span, columns = tokens.shape[0], *weights[0].shape[1:]
    return pl.pallas_call(
        backward_kernel,
        in_specs=[SMEM, ANY] + [VMEM] * 8 + [ANY] * len(before),
        out_specs=ANY,
        out_shape=jax.ShapeDtypeStruct(tokens.shape, jnp.bfloat16),
        scratch_shapes=[
            pltpu.VMEM((8, rows, span), jnp.bfloat16),
            pltpu.VMEM((8, rows, span), jnp.bfloat16),
            pltpu.SemaphoreType.DMA((8,)),
            pltpu.SemaphoreType.DMA((8,)),
        ],
        input_output_aliases={10: 0} if before else {},
        **costs(tokens, columns),
    )(table, tokens, inverse, gain, cotangent, moment, *weights, *before)


def swap(array, axis):
    last = lax.axis_size(axis) - 1
    return lax.ppermute(array, axis, [(a, last - a) for a in range(last + 1)])


def pair(array, axis, step):
    size = lax.axis_size(axis)
    masks = (1, 3) if step == 0 else (3, 1)
    moves = [(a * 2 + c, (a ^ masks[c]) * 2 + c) for a in range(size) for c in range(2)]
    return lax.ppermute(array, (axis, "c"), moves)


def across(array, axis):
    size = lax.axis_size(axis)
    return lax.ppermute(array, axis, [(a, a ^ 2) for a in range(size)])


def pair_z(array):
    size = lax.axis_size("zh") * lax.axis_size("zl")
    moves = []
    for z in range(size):
        moves.append((z * 2, (z ^ 1) * 2))
        moves.append((z * 2 + 1, (z + (1 if z % 2 else -1)) % size * 2 + 1))
    return lax.ppermute(array, ("zh", "zl", "c"), moves)


def halve(total):
    half = total.shape[0] // 2
    return total[half:].astype(jnp.bfloat16), total[:half]


def add(kept, got):
    return kept + got.astype(jnp.float32)


def tie(first, *others):
    return lax.optimization_barrier((first, *others))[0]


PIECES = (
    ((0, 0, 0), (0, 0, 1), (1, 0, 0), (1, 0, 1), (0, 1, 0), (0, 1, 1), (0, 2, 1), (0, 2, 0))
    + ((1, 1, 0), (1, 1, 1), (1, 2, 1), (1, 2, 0), (0, 3, 0), (1, 3, 0), (0, 3, 1), (1, 3, 1))
)


def write_ends(out_ref, rows):
    high = rows.astype(jnp.bfloat16).astype(jnp.float32)
    out_ref[-2 * EXTRA :, :] = jnp.concatenate([high, rows - high]).astype(jnp.bfloat16)


def read_ends(ref):
    ends = ref[-2 * EXTRA :, :].astype(jnp.float32)
    return ends[:EXTRA] + ends[EXTRA:]


def spread_kernel(tab_ref, total_ref, gain_ref, base_ref, near_ref, near_c_ref, far_ref, *refs, devices):
    out_refs, rows_ref = refs[:4], refs[4]
    columns = base_ref.shape[2]
    shards_ = (base_ref.at[0], near_c_ref.at[1], near_ref.at[0], far_ref.at[0])
    rows = pl.ds(pl.multiple_of(tab_ref[4] * TILE, TILE), TILE)
    rows_ref[...] = jnp.zeros_like(rows_ref)
    for k, shard in enumerate(shards_):
        total = total_ref[k].reshape(columns, TILE)
        out_refs[k][:columns, :] = total.astype(jnp.bfloat16)
        weight = shard[rows, :].astype(jnp.float32).T
        part = jnp.sum(weight * total, axis=0, keepdims=True)
        gain = gain_ref[:, pl.ds(pl.multiple_of(tab_ref[k] * TILE, TILE), TILE)]
        rows_ref[pl.ds(tab_ref[5 + k], 1), :] = part / (gain * devices)
    for out_ref in out_refs:
        write_ends(out_ref, rows_ref[...])


def spread(total, gain, base, near, near_c, far, table, devices):
    columns = base.shape[2]
    return pl.pallas_call(
        functools.partial(spread_kernel, devices=devices),
        in_specs=[SMEM] + [VMEM] * 6,
        out_specs=[VMEM] * 4,
        out_shape=[jax.ShapeDtypeStruct((columns + 2 * EXTRA, TILE), jnp.bfloat16)] * 4,
        scratch_shapes=[pltpu.VMEM((EXTRA, TILE), jnp.float32)],
        compiler_params=pltpu.CompilerParams(vmem_limit_bytes=LIMIT),
    )(table, total, gain, base, near, near_c, far)


def in_pairs(terms):
    while len(terms) > 1:
        terms = [a + b for a, b in zip(terms[::2], terms[1::2])]
    return terms[0]


def merge_kernel(*refs, scale):
    parts, out_ref = refs[:-1], refs[-1]
    columns = out_ref.shape[0] - 2 * EXTRA
    total = in_pairs([part[:columns, :].astype(jnp.float32) for part in parts])
    out_ref[:columns, :] = (total * scale).astype(jnp.bfloat16)
    write_ends(out_ref, in_pairs([read_ends(part) for part in parts]))


def merge(parts, scale=1.0):
    return pl.pallas_call(
        functools.partial(merge_kernel, scale=scale),
        in_specs=[VMEM] * len(parts),
        out_specs=VMEM,
        out_shape=jax.ShapeDtypeStruct(parts[0].shape, parts[0].dtype),
    )(*parts)


def finish_kernel(tab_ref, *refs):
    parts, (weight_ref, gain_ref) = refs[:4], refs[4:]
    columns = weight_ref.shape[1]
    for k, part in enumerate(parts):
        rows = pl.ds(pl.multiple_of(tab_ref[k] * TILE, TILE), TILE)
        weight_ref[rows, :] = part[:columns, :].astype(jnp.float32).T
        gain_ref[tab_ref[k]] = read_ends(part)


def finish(parts, table):
    columns = parts[0].shape[0] - 2 * EXTRA
    return pl.pallas_call(
        finish_kernel,
        in_specs=[SMEM] + [VMEM] * 4,
        out_specs=[VMEM] * 2,
        out_shape=[
            jax.ShapeDtypeStruct((4 * TILE, columns), jnp.float32),
            jax.ShapeDtypeStruct((4, EXTRA, TILE), jnp.float32),
        ],
    )(table, *parts)


def order_kernel(tab_ref, *refs):
    parts, out_ref = refs[:4], refs[4]
    for k, part in enumerate(parts):
        for x in range(4):
            for y in range(4):
                out_ref[tab_ref[k] + 2 * x, y : y + 1, :] = part[y, x : x + 1, :]


def order(parts, table):
    return pl.pallas_call(
        order_kernel,
        in_specs=[SMEM] + [VMEM] * 4,
        out_specs=VMEM,
        out_shape=jax.ShapeDtypeStruct((16, 4, TILE), jnp.float32),
    )(table, *parts)


def shards(tokens, norm_gain, weight_values, weight_scale, key_cotangent):
    y, zl, x, c = (lax.axis_index(a) for a in ("y", "zl", "x", "c"))
    width = tokens.shape[1]
    columns = weight_values.shape[1]
    gain = norm_gain.reshape(1, width)
    devices = 1
    for axis in EVERY:
        devices *= lax.axis_size(axis)

    def offset(core, first, second):
        masks = (1 + 2 * core, 3 - 2 * core)
        return first * masks[0] ^ second * masks[1]

    label = jnp.arange(32, dtype=jnp.int32)
    bits = [label // 16] + [label // k % 2 for k in (8, 4, 2, 1)]
    tables = []
    for core in (c, 1 - c):
        chip = (zl ^ bits[0]) * 4 + (x ^ offset(core, bits[3], bits[4]))
        tables.append((chip * 2 + core) * 4 + (y ^ offset(core, bits[1], bits[2])))
    shards_at = jnp.stack(
        [((zl ^ z) * 4 + (x ^ offset(c, k % 2, k // 2))) * 2 + (c ^ lane) for z, k, lane in PIECES]
    ).astype(jnp.int32)

    own = widen_weight(weight_values, weight_scale)
    own_c = swap(own, "c")
    up = pair_z(own)
    cot_own = key_cotangent.T
    base = jnp.stack([own, own_c])
    cot_got = swap(cot_own, "c")
    mine, other, inverse = norm_tiles(tie(tokens, base, cot_own), gain, jnp.stack(tables))
    got = swap(other, "c")
    got, up = lax.optimization_barrier((got, up))
    near = pair(base, "x", 0)
    up_c = swap(up, "c")
    sent, kept = grad_tiles(mine, got, cot_own, cot_got)

    first = sent[0]
    second, near, up_c = lax.optimization_barrier((sent[1], near, up_c))
    moved = (pair(first, "y", 0), pair_z(second))
    near_c = swap(near, "c")
    above = jnp.stack([up, up_c])
    above_near = pair(above, "x", 0)
    (first, kept_first), (second, kept_second) = (halve(add(k, m)) for k, m in zip(kept, moved))
    second, near_c, above_near = lax.optimization_barrier((second, near_c, above_near))
    moved = (pair_z(first), pair(second, "y", 0))
    above_near_c = swap(above_near, "c")
    far = pair(jnp.stack([near_c[1], above_near_c[1]]), "x", 0)
    (first, kept_first), (second, kept_second) = (
        halve(add(k, m)) for k, m in zip((kept_first, kept_second), moved)
    )
    send, near_c = lax.optimization_barrier((jnp.stack([first, second]), near_c))
    moved = pair(send, "y", 1)
    early, late_at = [base, above, near, near_c], shards_at[8:]
    sums = forward(tokens, inverse, gain, early, shards_at[:8])
    moved, sums = lax.optimization_barrier((moved, sums))
    total = jnp.stack([add(kept_first, moved[0]), add(kept_second, moved[1])], axis=1)
    total, far, sums = lax.optimization_barrier((total, far, sums))

    peer = x ^ offset(c, jnp.arange(4) // 2, jnp.arange(4) % 2)
    node_tile = ((zl * 4 + peer) * 2 + c) * 4 + y
    at = jnp.concatenate([node_tile, y[None], peer]).astype(jnp.int32)
    parts = spread(total, gain, base, near, near_c, far, at, devices)
    moved = [parts[0], pair(parts[2], "x", 0), pair(parts[1], "x", 1), across(parts[3], "x")]
    far_c = swap(far, "c")
    late = [above_near, above_near_c, far, far_c]
    projected, moment = forward_last(tokens, inverse, gain, key_cotangent, late, sums, late_at)
    moved[3], moment = lax.optimization_barrier((moved[3], moment))
    send = merge(moved)

    send, moment = lax.optimization_barrier((send, moment))
    moved = pair(send, "zh", 0)
    token_grads = backward(tokens, inverse, gain, key_cotangent, moment, early, shards_at[:8])
    moved, token_grads = lax.optimization_barrier((moved, token_grads))
    send = merge((send, moved))
    send, token_grads = lax.optimization_barrier((send, token_grads))
    moved = pair(send, "zh", 1)
    token_grads = backward(
        tokens, inverse, gain, key_cotangent, moment, late, late_at, before=(token_grads,)
    )
    moved, token_grads = lax.optimization_barrier((moved, token_grads))
    send = merge((send, moved), 1.0 / devices)

    parts = (send, pair(send, "y", 0), pair(send, "y", 1), across(send, "y"))
    quarters = jnp.stack([y ^ offset(c, k % 2, k // 2) for k in range(4)]).astype(jnp.int32)
    weight_grads, gains = finish(parts, quarters)
    gains = (gains, swap(gains, "c"), swap(gains, "zl"), swap(gains, ("zl", "c")))
    nodes = jnp.stack([(zl ^ k // 2) * 8 + (c ^ k % 2) for k in range(4)]).astype(jnp.int32)
    gain_grads = order(gains, nodes).reshape(width)
    return (projected, token_grads, weight_grads, gain_grads)


def solution(mesh):
    fine = Mesh(mesh.devices.reshape(4, 4, 2, 4, 2), EVERY)
    rows = P(EVERY, None)
    return jax.shard_map(
        shards,
        mesh=fine,
        in_specs=(rows, P(), P(NODE, None), P(NODE, None), rows),
        out_specs=(rows, rows, P(NODE, None), P()),
        check_vma=False,
    )
```

```python
import functools

import jax
import jax.numpy as jnp
from jax import lax
from jax.experimental import pallas as pl
from jax.experimental.pallas import tpu as pltpu
from jax.sharding import Mesh, PartitionSpec as P

NODE = ("zl", "x", "c")
EVERY = ("y", "zh", "zl", "x", "c")
TILE = 128
EXTRA = 8
LIMIT = 16 * 2**20
SMALL = 8 * 2**20
QUICK = pl.CostEstimate(flops=1, bytes_accessed=1, transcendentals=0)


def widen_kernel(values_ref, scales_ref, out_ref):
    blocks = scales_ref.shape[0]
    block = values_ref.shape[1] // blocks
    scales = scales_ref[...].astype(jnp.float32)
    scales = jnp.concatenate([scales] * (8 // blocks), axis=0).T
    for k in range(blocks):
        part = slice(k * block, (k + 1) * block)
        wide = values_ref[:, part].astype(jnp.float32)
        out_ref[:, part] = (wide * scales[:, k : k + 1]).astype(jnp.bfloat16)


def widen_weight(values, scales):
    return pl.pallas_call(
        widen_kernel,
        out_shape=jax.ShapeDtypeStruct(values.shape, jnp.bfloat16),
        compiler_params=pltpu.CompilerParams(vmem_limit_bytes=SMALL),
    )(values, scales.T)


def norm_kernel(tab_ref, tok_ref, gain_ref, own_ref, oth_ref, inv_ref):
    rows, width = tok_ref.shape
    total = jnp.zeros((rows, TILE), jnp.float32)
    for t in range(width // TILE):
        wide = tok_ref[:, t * TILE : (t + 1) * TILE].astype(jnp.float32)
        total = total + wide * wide
    mean = jnp.sum(total, axis=1, keepdims=True) / width
    inverse = lax.rsqrt(mean + 1e-05)
    inv_ref[...] = inverse
    for side, out_ref in enumerate((own_ref, oth_ref)):
        for r in range(width // TILE // 2):
            at = pl.multiple_of(tab_ref[side, r] * TILE, TILE)
            wide = tok_ref[:, pl.ds(at, TILE)].astype(jnp.float32)
            scaled = wide * inverse * gain_ref[:, pl.ds(at, TILE)]
            out_ref[:, r * TILE : (r + 1) * TILE] = scaled.astype(jnp.bfloat16)


def norm_tiles(tokens, gain, table):
    rows, width = tokens.shape
    step = 64 if rows % 64 == 0 else rows
    half = pl.BlockSpec((step, width // 2), lambda i, tab: (i, 0))
    return pl.pallas_call(
        norm_kernel,
        grid_spec=pltpu.PrefetchScalarGridSpec(
            num_scalar_prefetch=1,
            grid=(rows // step,),
            in_specs=[
                pl.BlockSpec((step, width), lambda i, tab: (i, 0)),
                pl.BlockSpec((1, width), lambda i, tab: (0, 0)),
            ],
            out_specs=[half, half, pl.BlockSpec((step, 1), lambda i, tab: (i, 0))],
        ),
        out_shape=[
            jax.ShapeDtypeStruct((rows, width // 2), jnp.bfloat16),
            jax.ShapeDtypeStruct((rows, width // 2), jnp.bfloat16),
            jax.ShapeDtypeStruct((rows, 1), jnp.float32),
        ],
        compiler_params=pltpu.CompilerParams(vmem_limit_bytes=LIMIT),
        cost_estimate=QUICK,
    )(table, tokens, gain)


def grad_kernel(own_ref, got_ref, cot_own_ref, cot_got_ref, *out_refs):
    span = 2 * TILE
    half = cot_own_ref.shape[0] // 2
    cot_own = cot_own_ref[...]
    cot_got = cot_got_ref[...]
    for pair in range(own_ref.shape[1] // span):
        part = slice(pair * span, (pair + 1) * span)
        grads = jnp.dot(cot_own, own_ref[:, part], preferred_element_type=jnp.float32)
        grads += jnp.dot(cot_got, got_ref[:, part], preferred_element_type=jnp.float32)
        for which in range(2):
            tile = pair * 2 + which
            z, y1, rest = tile // 16, tile // 8 % 2, tile % 8
            for side, (sent, at) in enumerate(((y1, z * 8 + rest), (z, y1 * 8 + rest))):
                piece = grads[side * half : (side + 1) * half, which * TILE : (which + 1) * TILE]
                if sent:
                    out_refs[side][at] = piece.astype(jnp.bfloat16)
                else:
                    out_refs[2 + side][at] = piece


def grad_tiles(own, got, cot_own, cot_got):
    rows, width = own.shape
    columns = cot_own.shape[0]
    tiles = width // TILE // 2
    shape = (tiles, columns // 2, TILE)
    outs = pl.pallas_call(
        grad_kernel,
        out_shape=[jax.ShapeDtypeStruct(shape, jnp.bfloat16)] * 2
        + [jax.ShapeDtypeStruct(shape, jnp.float32)] * 2,
        compiler_params=pltpu.CompilerParams(vmem_limit_bytes=LIMIT),
        cost_estimate=QUICK,
    )(own, got, cot_own, cot_got)
    return outs[:2], outs[2:]


def block_in(tab_ref, tok_ref, block, sem, k):
    span = block.shape[2]
    at = pl.multiple_of(tab_ref[k] * span, span)
    return pltpu.make_async_copy(tok_ref.at[:, pl.ds(at, span)], block.at[k], sem.at[k])


def shards_of(refs):
    return [ref.at[k] for ref in refs for k in range(ref.shape[0])]


def forward_kernel(tab_ref, tok_ref, inv_ref, gain_ref, *refs):
    w_refs, acc_in, (acc, block, sem) = refs[:4], refs[4:-3], refs[-3:]
    forward_steps(tab_ref, tok_ref, inv_ref, gain_ref, shards_of(w_refs), acc_in, acc, block, sem)


def forward_steps(tab_ref, tok_ref, inv_ref, gain_ref, weights, acc_in, acc, block, sem):
    count, _, span = block.shape
    for k in range(count):
        block_in(tab_ref, tok_ref, block, sem, k).start()
    inverse = inv_ref[...]
    acc[...] = acc_in[0][...] if acc_in else jnp.zeros_like(acc)
    for k in range(count):
        block_in(tab_ref, tok_ref, block, sem, k).wait()
        at = pl.multiple_of(tab_ref[k] * span, span)
        wide = block[k].astype(jnp.float32)
        normed = (wide * inverse * gain_ref[:, pl.ds(at, span)]).astype(jnp.bfloat16)
        acc[...] += jnp.dot(normed, weights[k][...], preferred_element_type=jnp.float32)


def forward_last_kernel(tab_ref, tok_ref, inv_ref, gain_ref, cot_ref, *refs):
    w_refs, (acc_in, proj_ref, moment_ref, acc, block, sem) = refs[:-6], refs[-6:]
    weights = shards_of(w_refs)
    forward_steps(tab_ref, tok_ref, inv_ref, gain_ref, weights, (acc_in,), acc, block, sem)
    keys = acc[...]
    inverse = inv_ref[...]
    proj_ref[...] = keys.astype(jnp.bfloat16)
    inner = jnp.sum(cot_ref[...].astype(jnp.float32) * keys, axis=1, keepdims=True)
    moment_ref[...] = inverse * inverse * inner / tok_ref.shape[1]


def backward_kernel(tab_ref, tok_ref, inv_ref, gain_ref, cot_ref, moment_ref, *refs, count):
    weights, (grads_ref, block, out, sem, out_sem) = shards_of(refs[:count]), refs[-5:]
    count, _, span = block.shape

    def block_out(k):
        at = pl.multiple_of(tab_ref[k] * span, span)
        return pltpu.make_async_copy(out.at[k], grads_ref.at[:, pl.ds(at, span)], out_sem.at[k])

    for k in range(count):
        block_in(tab_ref, tok_ref, block, sem, k).start()
    inverse, moment, cot = inv_ref[...], moment_ref[...], cot_ref[...]
    for k in range(count):
        partial = lax.dot_general(
            cot, weights[k][...], (((1,), (1,)), ((), ())), preferred_element_type=jnp.float32
        )
        block_in(tab_ref, tok_ref, block, sem, k).wait()
        at = pl.multiple_of(tab_ref[k] * span, span)
        wide = block[k].astype(jnp.float32)
        grads = inverse * gain_ref[:, pl.ds(at, span)] * partial - wide * moment
        out[k] = grads.astype(jnp.bfloat16)
        block_out(k).start()
    for k in range(count):
        block_out(k).wait()


VMEM = pl.BlockSpec(memory_space=pltpu.VMEM)
SMEM = pl.BlockSpec(memory_space=pltpu.SMEM)
ANY = pl.BlockSpec(memory_space=pl.ANY)


def costs(tokens, columns):
    rows, width = tokens.shape
    return dict(
        compiler_params=pltpu.CompilerParams(vmem_limit_bytes=LIMIT),
        cost_estimate=pl.CostEstimate(
            flops=rows * width * columns,
            bytes_accessed=2 * rows * width + width * columns,
            transcendentals=0,
        ),
    )


def forward(tokens, inverse, gain, weights, table):
    rows, span, columns = tokens.shape[0], *weights[0].shape[1:]
    return pl.pallas_call(
        forward_kernel,
        in_specs=[SMEM, ANY] + [VMEM] * 6,
        out_specs=VMEM,
        out_shape=jax.ShapeDtypeStruct((rows, columns), jnp.float32),
        scratch_shapes=[
            pltpu.VMEM((8, rows, span), jnp.bfloat16),
            pltpu.SemaphoreType.DMA((8,)),
        ],
        **costs(tokens, columns),
    )(table, tokens, inverse, gain, *weights)


def forward_last(tokens, inverse, gain, cotangent, weights, sums, table):
    rows, span, columns = tokens.shape[0], *weights[0].shape[1:]
    return pl.pallas_call(
        forward_last_kernel,
        in_specs=[SMEM, ANY] + [VMEM] * (4 + len(weights)),
        out_specs=[VMEM] * 2,
        out_shape=[
            jax.ShapeDtypeStruct((rows, columns), jnp.bfloat16),
            jax.ShapeDtypeStruct((rows, 1), jnp.float32),
        ],
        scratch_shapes=[
            pltpu.VMEM((rows, columns), jnp.float32),
            pltpu.VMEM((8, rows, span), jnp.bfloat16),
            pltpu.SemaphoreType.DMA((8,)),
        ],
        **costs(tokens, columns),
    )(table, tokens, inverse, gain, cotangent, *weights, sums)


def backward(tokens, inverse, gain, cotangent, moment, weights, table, before=()):
    rows, span, columns = tokens.shape[0], *weights[0].shape[1:]
    return pl.pallas_call(
        functools.partial(backward_kernel, count=len(weights)),
        in_specs=[SMEM, ANY] + [VMEM] * (4 + len(weights)) + [ANY] * len(before),
        out_specs=ANY,
        out_shape=jax.ShapeDtypeStruct(tokens.shape, jnp.bfloat16),
        scratch_shapes=[
            pltpu.VMEM((8, rows, span), jnp.bfloat16),
            pltpu.VMEM((8, rows, span), jnp.bfloat16),
            pltpu.SemaphoreType.DMA((8,)),
            pltpu.SemaphoreType.DMA((8,)),
        ],
        input_output_aliases={6 + len(weights): 0} if before else {},
        **costs(tokens, columns),
    )(table, tokens, inverse, gain, cotangent, moment, *weights, *before)


def swap(array, axis):
    last = lax.axis_size(axis) - 1
    return lax.ppermute(array, axis, [(a, last - a) for a in range(last + 1)])


def pair(array, axis, step):
    size = lax.axis_size(axis)
    masks = (1, 3) if step == 0 else (3, 1)
    moves = [(a * 2 + c, (a ^ masks[c]) * 2 + c) for a in range(size) for c in range(2)]
    return lax.ppermute(array, (axis, "c"), moves)


def across(array, axis):
    size = lax.axis_size(axis)
    return lax.ppermute(array, axis, [(a, a ^ 2) for a in range(size)])


def pair_z(array):
    size = lax.axis_size("zh") * lax.axis_size("zl")
    moves = []
    for z in range(size):
        moves.append((z * 2, (z ^ 1) * 2))
        moves.append((z * 2 + 1, (z + (1 if z % 2 else -1)) % size * 2 + 1))
    return lax.ppermute(array, ("zh", "zl", "c"), moves)


def halve(total):
    half = total.shape[0] // 2
    return total[half:].astype(jnp.bfloat16), total[:half]


def add(kept, got):
    return kept + got.astype(jnp.float32)


def tie(first, *others):
    return lax.optimization_barrier((first, *others))[0]


PIECES = (
    ((0, 0, 0), (0, 0, 1), (1, 0, 0), (1, 0, 1), (0, 1, 0), (0, 1, 1), (0, 2, 1), (0, 2, 0))
    + ((1, 1, 0), (1, 1, 1), (1, 2, 1), (1, 2, 0), (0, 3, 0), (1, 3, 0), (0, 3, 1), (1, 3, 1))
)


def write_ends(out_ref, rows):
    high = rows.astype(jnp.bfloat16).astype(jnp.float32)
    out_ref[-2 * EXTRA :, :] = jnp.concatenate([high, rows - high]).astype(jnp.bfloat16)


def read_ends(ref):
    ends = ref[-2 * EXTRA :, :].astype(jnp.float32)
    return ends[:EXTRA] + ends[EXTRA:]


def spread_kernel(tab_ref, total_ref, gain_ref, base_ref, near_ref, near_c_ref, far_ref, *refs, devices):
    out_refs, rows_ref = refs[:4], refs[4]
    columns = base_ref.shape[2]
    shards_ = (base_ref.at[0], near_c_ref.at[1], near_ref.at[0], far_ref.at[0])
    rows = pl.ds(pl.multiple_of(tab_ref[4] * TILE, TILE), TILE)
    rows_ref[...] = jnp.zeros_like(rows_ref)
    for k, shard in enumerate(shards_):
        total = total_ref[k].reshape(columns, TILE)
        out_refs[k][:columns, :] = total.astype(jnp.bfloat16)
        weight = shard[rows, :].astype(jnp.float32).T
        part = jnp.sum(weight * total, axis=0, keepdims=True)
        gain = gain_ref[:, pl.ds(pl.multiple_of(tab_ref[k] * TILE, TILE), TILE)]
        rows_ref[pl.ds(tab_ref[5 + k], 1), :] = part / (gain * devices)
    for out_ref in out_refs:
        write_ends(out_ref, rows_ref[...])


def spread(total, gain, base, near, near_c, far, table, devices):
    columns = base.shape[2]
    return pl.pallas_call(
        functools.partial(spread_kernel, devices=devices),
        in_specs=[SMEM] + [VMEM] * 6,
        out_specs=[VMEM] * 4,
        out_shape=[jax.ShapeDtypeStruct((columns + 2 * EXTRA, TILE), jnp.bfloat16)] * 4,
        scratch_shapes=[pltpu.VMEM((EXTRA, TILE), jnp.float32)],
        compiler_params=pltpu.CompilerParams(vmem_limit_bytes=LIMIT),
    )(table, total, gain, base, near, near_c, far)


def in_pairs(terms):
    while len(terms) > 1:
        terms = [a + b for a, b in zip(terms[::2], terms[1::2])]
    return terms[0]


def merge_kernel(*refs, scale):
    parts, out_ref = refs[:-1], refs[-1]
    columns = out_ref.shape[0] - 2 * EXTRA
    total = in_pairs([part[:columns, :].astype(jnp.float32) for part in parts])
    out_ref[:columns, :] = (total * scale).astype(jnp.bfloat16)
    write_ends(out_ref, in_pairs([read_ends(part) for part in parts]))


def merge(parts, scale=1.0):
    return pl.pallas_call(
        functools.partial(merge_kernel, scale=scale),
        in_specs=[VMEM] * len(parts),
        out_specs=VMEM,
        out_shape=jax.ShapeDtypeStruct(parts[0].shape, parts[0].dtype),
        compiler_params=pltpu.CompilerParams(vmem_limit_bytes=SMALL),
    )(*parts)


def finish_kernel(tab_ref, *refs):
    parts, (weight_ref, gain_ref) = refs[:4], refs[4:]
    columns = weight_ref.shape[1]
    for k, part in enumerate(parts):
        rows = pl.ds(pl.multiple_of(tab_ref[k] * TILE, TILE), TILE)
        weight_ref[rows, :] = part[:columns, :].astype(jnp.float32).T
        gain_ref[tab_ref[k]] = read_ends(part)


def finish(parts, table):
    columns = parts[0].shape[0] - 2 * EXTRA
    return pl.pallas_call(
        finish_kernel,
        in_specs=[SMEM] + [VMEM] * 4,
        out_specs=[VMEM] * 2,
        out_shape=[
            jax.ShapeDtypeStruct((4 * TILE, columns), jnp.float32),
            jax.ShapeDtypeStruct((4, EXTRA, TILE), jnp.float32),
        ],
        compiler_params=pltpu.CompilerParams(vmem_limit_bytes=SMALL),
    )(table, *parts)


def order_kernel(tab_ref, *refs):
    parts, out_ref = refs[:4], refs[4]
    for k, part in enumerate(parts):
        for x in range(4):
            for y in range(4):
                out_ref[tab_ref[k] + 2 * x, y : y + 1, :] = part[y, x : x + 1, :]


def order(parts, table):
    return pl.pallas_call(
        order_kernel,
        in_specs=[SMEM] + [VMEM] * 4,
        out_specs=VMEM,
        out_shape=jax.ShapeDtypeStruct((16, 4, TILE), jnp.float32),
        compiler_params=pltpu.CompilerParams(vmem_limit_bytes=SMALL),
    )(table, *parts)


def shards(tokens, norm_gain, weight_values, weight_scale, key_cotangent):
    y, zl, x, c = (lax.axis_index(a) for a in ("y", "zl", "x", "c"))
    width = tokens.shape[1]
    columns = weight_values.shape[1]
    gain = norm_gain.reshape(1, width)
    devices = 1
    for axis in EVERY:
        devices *= lax.axis_size(axis)

    def offset(core, first, second):
        masks = (1 + 2 * core, 3 - 2 * core)
        return first * masks[0] ^ second * masks[1]

    label = jnp.arange(32, dtype=jnp.int32)
    bits = [label // 16] + [label // k % 2 for k in (8, 4, 2, 1)]
    tables = []
    for core in (c, 1 - c):
        chip = (zl ^ bits[0]) * 4 + (x ^ offset(core, bits[3], bits[4]))
        tables.append((chip * 2 + core) * 4 + (y ^ offset(core, bits[1], bits[2])))
    shards_at = jnp.stack(
        [((zl ^ z) * 4 + (x ^ offset(c, k % 2, k // 2))) * 2 + (c ^ lane) for z, k, lane in PIECES]
    ).astype(jnp.int32)

    own = widen_weight(weight_values, weight_scale)
    own_c = swap(own, "c")
    up = pair_z(own)
    cot_own = key_cotangent.T
    base = jnp.stack([own, own_c])
    cot_got = swap(cot_own, "c")
    mine, other, inverse = norm_tiles(tokens, gain, tie(jnp.stack(tables), base, cot_own))
    got = swap(other, "c")
    near = pair(base, "x", 0)
    sent, kept = grad_tiles(mine, got, cot_own, cot_got)

    first = sent[0]
    second, near, up = lax.optimization_barrier((sent[1], near, up))
    moved = [pair(first, "y", 0), pair_z(second)]
    near_c = swap(near, "c")
    above = jnp.stack([up, swap(up, "c")])
    above_near = pair(above, "x", 0)
    far = pair(near_c[1:], "x", 0)
    (first, kept_first), (second, kept_second) = (halve(add(k, m)) for k, m in zip(kept, moved))

    second, near_c, above = lax.optimization_barrier((second, near_c, above))
    moved = [pair_z(first), pair(second, "y", 0)]
    early, late_at = [base, above, near, near_c], shards_at[8:]
    sums = forward(tokens, inverse, gain, early, shards_at[:8])
    moved[1], sums, above_near, far = lax.optimization_barrier((moved[1], sums, above_near, far))
    above_near_c = swap(above_near, "c")
    above_far = pair(above_near_c[1:], "x", 0)
    (first, kept_first), (second, kept_second) = (
        halve(add(k, m)) for k, m in zip((kept_first, kept_second), moved)
    )

    moved = pair(jnp.stack([first, second]), "y", 1)
    far_c = swap(far, "c")
    moved, above_far, far_c = lax.optimization_barrier((moved, above_far, far_c))
    total = jnp.stack([add(kept_first, moved[0]), add(kept_second, moved[1])], axis=1)

    peer = x ^ offset(c, jnp.arange(4) // 2, jnp.arange(4) % 2)
    node_tile = ((zl * 4 + peer) * 2 + c) * 4 + y
    at = jnp.concatenate([node_tile, y[None], peer]).astype(jnp.int32)
    parts = list(spread(total, gain, base, near, near_c, far, at, devices))
    parts[0], above_far = lax.optimization_barrier((parts[0], above_far))
    moved = [parts[0], pair(parts[2], "x", 0), pair(parts[1], "x", 1), across(parts[3], "x")]
    late = [above_near, above_near_c, far, above_far, far_c, swap(above_far, "c")]
    projected, moment = forward_last(tokens, inverse, gain, key_cotangent, late, sums, late_at)
    moved[3], moment = lax.optimization_barrier((moved[3], moment))
    send = merge(moved)

    send, moment = lax.optimization_barrier((send, moment))
    moved = pair(send, "zh", 0)
    token_grads = backward(tokens, inverse, gain, key_cotangent, moment, early, shards_at[:8])
    moved, token_grads = lax.optimization_barrier((moved, token_grads))
    send = merge((send, moved))
    send, token_grads = lax.optimization_barrier((send, token_grads))
    moved = pair(send, "zh", 1)
    token_grads = backward(
        tokens, inverse, gain, key_cotangent, moment, late, late_at, before=(token_grads,)
    )
    moved, token_grads = lax.optimization_barrier((moved, token_grads))
    send = merge((send, moved), 1.0 / devices)

    parts = (send, pair(send, "y", 0), pair(send, "y", 1), across(send, "y"))
    quarters = jnp.stack([y ^ offset(c, k % 2, k // 2) for k in range(4)]).astype(jnp.int32)
    weight_grads, gains = finish(parts, quarters)
    gains = (gains, swap(gains, "c"), swap(gains, "zl"), swap(gains, ("zl", "c")))
    nodes = jnp.stack([(zl ^ k // 2) * 8 + (c ^ k % 2) for k in range(4)]).astype(jnp.int32)
    gain_grads = order(gains, nodes).reshape(width)
    return (projected, token_grads, weight_grads, gain_grads)


def solution(mesh):
    fine = Mesh(mesh.devices.reshape(4, 4, 2, 4, 2), EVERY)
    rows = P(EVERY, None)
    return jax.shard_map(
        shards,
        mesh=fine,
        in_specs=(rows, P(), P(NODE, None), P(NODE, None), rows),
        out_specs=(rows, rows, P(NODE, None), P()),
        check_vma=False,
    )
```

```python
import functools

import jax
import jax.numpy as jnp
from jax import lax
from jax.experimental import pallas as pl
from jax.experimental.pallas import tpu as pltpu
from jax.sharding import Mesh, PartitionSpec as P

NODE = ("zl", "x", "c")
EVERY = ("y", "zh", "zl", "x", "c")
TILE = 128
EXTRA = 8
LIMIT = 16 * 2**20
SMALL = 8 * 2**20
QUICK = pl.CostEstimate(flops=1, bytes_accessed=1, transcendentals=0)
VMEM = pl.BlockSpec(memory_space=pltpu.VMEM)
SMEM = pl.BlockSpec(memory_space=pltpu.SMEM)
HBM = pl.BlockSpec(memory_space=pltpu.HBM)


def widen_kernel(values_ref, scales_ref, out_ref):
    blocks = scales_ref.shape[0]
    block = values_ref.shape[1] // blocks
    scales = scales_ref[...].astype(jnp.float32)
    scales = jnp.concatenate([scales] * (8 // blocks), axis=0).T
    for k in range(blocks):
        part = slice(k * block, (k + 1) * block)
        wide = values_ref[:, part].astype(jnp.float32)
        out_ref[:, part] = (wide * scales[:, k : k + 1]).astype(jnp.bfloat16)


def widen_weight(values, scales):
    return pl.pallas_call(
        widen_kernel,
        out_shape=jax.ShapeDtypeStruct(values.shape, jnp.bfloat16),
        compiler_params=pltpu.CompilerParams(vmem_limit_bytes=SMALL),
    )(values, scales.T)


def norm_kernel(tab_ref, tok_ref, gain_ref, own_ref, oth_ref, inv_ref, block, sem):
    count, rows, width = block.shape

    def block_in(k):
        return pltpu.make_async_copy(tok_ref.at[pl.ds(k * rows, rows)], block.at[k], sem.at[k])

    for k in range(count):
        block_in(k).start()
    for k in range(count):
        block_in(k).wait()
        part = slice(k * rows, (k + 1) * rows)
        total = jnp.zeros((rows, TILE), jnp.float32)
        for t in range(width // TILE):
            wide = block[k, :, t * TILE : (t + 1) * TILE].astype(jnp.float32)
            total = total + wide * wide
        mean = jnp.sum(total, axis=1, keepdims=True) / width
        inverse = lax.rsqrt(mean + 1e-05)
        inv_ref[part, :] = inverse
        for side, out_ref in enumerate((own_ref, oth_ref)):
            for r in range(width // TILE // 2):
                at = pl.multiple_of(tab_ref[side, r] * TILE, TILE)
                wide = block[k, :, pl.ds(at, TILE)].astype(jnp.float32)
                scaled = wide * inverse * gain_ref[:, pl.ds(at, TILE)]
                out_ref[part, r * TILE : (r + 1) * TILE] = scaled.astype(jnp.bfloat16)


def norm_tiles(tokens, gain, table):
    rows, width = tokens.shape
    step = 64 if rows % 64 == 0 else rows
    return pl.pallas_call(
        norm_kernel,
        in_specs=[SMEM, HBM, VMEM],
        out_specs=[VMEM] * 3,
        out_shape=[
            jax.ShapeDtypeStruct((rows, width // 2), jnp.bfloat16),
            jax.ShapeDtypeStruct((rows, width // 2), jnp.bfloat16),
            jax.ShapeDtypeStruct((rows, 1), jnp.float32),
        ],
        scratch_shapes=[
            pltpu.VMEM((rows // step, step, width), jnp.bfloat16),
            pltpu.SemaphoreType.DMA((rows // step,)),
        ],
        compiler_params=pltpu.CompilerParams(vmem_limit_bytes=LIMIT),
        cost_estimate=QUICK,
    )(table, tokens, gain)


def grad_kernel(own_ref, got_ref, cot_own_ref, cot_got_ref, *out_refs):
    span = 2 * TILE
    half = cot_own_ref.shape[0] // 2
    cot_own = cot_own_ref[...]
    cot_got = cot_got_ref[...]
    for pair in range(own_ref.shape[1] // span):
        part = slice(pair * span, (pair + 1) * span)
        grads = jnp.dot(cot_own, own_ref[:, part], preferred_element_type=jnp.float32)
        grads += jnp.dot(cot_got, got_ref[:, part], preferred_element_type=jnp.float32)
        for which in range(2):
            tile = pair * 2 + which
            z, y1, rest = tile // 16, tile // 8 % 2, tile % 8
            for side, (sent, at) in enumerate(((y1, z * 8 + rest), (z, y1 * 8 + rest))):
                piece = grads[side * half : (side + 1) * half, which * TILE : (which + 1) * TILE]
                if sent:
                    out_refs[side][at] = piece.astype(jnp.bfloat16)
                else:
                    out_refs[2 + side][at] = piece


def grad_tiles(own, got, cot_own, cot_got):
    rows, width = own.shape
    columns = cot_own.shape[0]
    tiles = width // TILE // 2
    shape = (tiles, columns // 2, TILE)
    outs = pl.pallas_call(
        grad_kernel,
        out_shape=[jax.ShapeDtypeStruct(shape, jnp.bfloat16)] * 2
        + [jax.ShapeDtypeStruct(shape, jnp.float32)] * 2,
        compiler_params=pltpu.CompilerParams(vmem_limit_bytes=LIMIT),
        cost_estimate=QUICK,
    )(own, got, cot_own, cot_got)
    return outs[:2], outs[2:]


class Inputs:
    def __init__(self, tab_ref, tok_ref, w_refs, block, weight, sem, weight_sem):
        shards_ = [ref.at[k] for ref in w_refs for k in range(ref.shape[0])]
        self.count, _, self.span = block.shape
        self.tab_ref, self.block, self.weight = tab_ref, block, weight
        self.copies = []
        for k in range(self.count):
            self.copies.append(
                (
                    pltpu.make_async_copy(tok_ref.at[:, self.columns(k)], block.at[k], sem.at[k]),
                    pltpu.make_async_copy(shards_[k], weight.at[k], weight_sem.at[k]),
                )
            )
        for pair_ in self.copies:
            for copy in pair_:
                copy.start()

    def columns(self, k):
        return pl.ds(pl.multiple_of(self.tab_ref[k] * self.span, self.span), self.span)

    def wait(self, k):
        for copy in self.copies[k]:
            copy.wait()

    @staticmethod
    def scratch(rows, span, columns, count):
        return [
            pltpu.VMEM((count, rows, span), jnp.bfloat16),
            pltpu.VMEM((count, span, columns), jnp.bfloat16),
            pltpu.SemaphoreType.DMA((count,)),
            pltpu.SemaphoreType.DMA((count,)),
        ]


def forward_steps(inputs, inv_ref, gain_ref, acc):
    inverse = inv_ref[...]
    for k in range(inputs.count):
        inputs.wait(k)
        wide = inputs.block[k].astype(jnp.float32)
        normed = (wide * inverse * gain_ref[:, inputs.columns(k)]).astype(jnp.bfloat16)
        acc[...] += jnp.dot(normed, inputs.weight[k], preferred_element_type=jnp.float32)


def forward_kernel(tab_ref, tok_ref, inv_ref, gain_ref, *refs):
    w_refs, (acc, *scratch) = refs[:-5], refs[-5:]
    inputs = Inputs(tab_ref, tok_ref, w_refs, *scratch)
    acc[...] = jnp.zeros_like(acc)
    forward_steps(inputs, inv_ref, gain_ref, acc)


def forward_last_kernel(tab_ref, tok_ref, inv_ref, gain_ref, cot_ref, acc_in, *refs):
    w_refs, (proj_ref, moment_ref, acc, *scratch) = refs[:-7], refs[-7:]
    inputs = Inputs(tab_ref, tok_ref, w_refs, *scratch)
    acc[...] = acc_in[...]
    forward_steps(inputs, inv_ref, gain_ref, acc)
    keys = acc[...]
    inverse = inv_ref[...]
    proj_ref[...] = keys.astype(jnp.bfloat16)
    inner = jnp.sum(cot_ref[...].astype(jnp.float32) * keys, axis=1, keepdims=True)
    moment_ref[...] = inverse * inverse * inner / tok_ref.shape[1]


def backward_kernel(tab_ref, tok_ref, inv_ref, gain_ref, cot_ref, moment_ref, *refs, count):
    w_refs, (grads_ref, out, out_sem, *scratch) = refs[:count], refs[-7:]
    inputs = Inputs(tab_ref, tok_ref, w_refs, *scratch)

    def block_out(k):
        return pltpu.make_async_copy(
            out.at[k], grads_ref.at[:, inputs.columns(k)], out_sem.at[k]
        )

    inverse, moment, cot = inv_ref[...], moment_ref[...], cot_ref[...]
    for k in range(inputs.count):
        inputs.wait(k)
        partial = lax.dot_general(
            cot, inputs.weight[k], (((1,), (1,)), ((), ())), preferred_element_type=jnp.float32
        )
        wide = inputs.block[k].astype(jnp.float32)
        grads = inverse * gain_ref[:, inputs.columns(k)] * partial - wide * moment
        out[k] = grads.astype(jnp.bfloat16)
        block_out(k).start()
    for k in range(inputs.count):
        block_out(k).wait()


def costs(tokens, columns):
    rows, width = tokens.shape
    return dict(
        compiler_params=pltpu.CompilerParams(vmem_limit_bytes=LIMIT),
        cost_estimate=pl.CostEstimate(
            flops=rows * width * columns,
            bytes_accessed=2 * rows * width + width * columns,
            transcendentals=0,
        ),
    )


def forward(tokens, inverse, gain, weights, table):
    rows, span, columns = tokens.shape[0], *weights[0].shape[1:]
    return pl.pallas_call(
        forward_kernel,
        in_specs=[SMEM, HBM] + [VMEM] * 2 + [HBM] * len(weights),
        out_specs=VMEM,
        out_shape=jax.ShapeDtypeStruct((rows, columns), jnp.float32),
        scratch_shapes=Inputs.scratch(rows, span, columns, table.shape[0]),
        **costs(tokens, columns),
    )(table, tokens, inverse, gain, *weights)


def forward_last(tokens, inverse, gain, cotangent, weights, sums, table):
    rows, span, columns = tokens.shape[0], *weights[0].shape[1:]
    return pl.pallas_call(
        forward_last_kernel,
        in_specs=[SMEM, HBM] + [VMEM] * 4 + [HBM] * len(weights),
        out_specs=[VMEM] * 2,
        out_shape=[
            jax.ShapeDtypeStruct((rows, columns), jnp.bfloat16),
            jax.ShapeDtypeStruct((rows, 1), jnp.float32),
        ],
        scratch_shapes=[pltpu.VMEM((rows, columns), jnp.float32)]
        + Inputs.scratch(rows, span, columns, table.shape[0]),
        **costs(tokens, columns),
    )(table, tokens, inverse, gain, cotangent, sums, *weights)


def backward(tokens, inverse, gain, cotangent, moment, weights, table, before=()):
    rows, span, columns = tokens.shape[0], *weights[0].shape[1:]
    count = table.shape[0]
    return pl.pallas_call(
        functools.partial(backward_kernel, count=len(weights)),
        in_specs=[SMEM, HBM] + [VMEM] * 4 + [HBM] * (len(weights) + len(before)),
        out_specs=HBM,
        out_shape=jax.ShapeDtypeStruct(tokens.shape, jnp.bfloat16),
        scratch_shapes=[
            pltpu.VMEM((count, rows, span), jnp.bfloat16),
            pltpu.SemaphoreType.DMA((count,)),
        ]
        + Inputs.scratch(rows, span, columns, count),
        input_output_aliases={6 + len(weights): 0} if before else {},
        **costs(tokens, columns),
    )(table, tokens, inverse, gain, cotangent, moment, *weights, *before)


def swap(array, axis):
    last = lax.axis_size(axis) - 1
    return lax.ppermute(array, axis, [(a, last - a) for a in range(last + 1)])


def pair(array, axis, step):
    size = lax.axis_size(axis)
    masks = (1, 3) if step == 0 else (3, 1)
    moves = [(a * 2 + c, (a ^ masks[c]) * 2 + c) for a in range(size) for c in range(2)]
    return lax.ppermute(array, (axis, "c"), moves)


def across(array, axis):
    size = lax.axis_size(axis)
    return lax.ppermute(array, axis, [(a, a ^ 2) for a in range(size)])


def pair_z(array):
    size = lax.axis_size("zh") * lax.axis_size("zl")
    moves = []
    for z in range(size):
        moves.append((z * 2, (z ^ 1) * 2))
        moves.append((z * 2 + 1, (z + (1 if z % 2 else -1)) % size * 2 + 1))
    return lax.ppermute(array, ("zh", "zl", "c"), moves)


def halve(total):
    half = total.shape[0] // 2
    return total[half:].astype(jnp.bfloat16), total[:half]


def add(kept, got):
    return kept + got.astype(jnp.float32)


def tie(first, *others):
    return lax.optimization_barrier((first, *others))[0]


BASE, ABOVE = (((z, 0, 0), (z, 0, 1)) for z in (0, 1))
NEAR, ABOVE_NEAR = (((z, 1, 0), (z, 1, 1)) for z in (0, 1))
NEAR_C, ABOVE_NEAR_C = (((z, 2, 1), (z, 2, 0)) for z in (0, 1))
FAR, ABOVE_FAR = (((z, 3, 0),) for z in (0, 1))
FAR_C, ABOVE_FAR_C = (((z, 3, 1),) for z in (0, 1))


def write_ends(out_ref, rows):
    high = rows.astype(jnp.bfloat16).astype(jnp.float32)
    out_ref[-2 * EXTRA :, :] = jnp.concatenate([high, rows - high]).astype(jnp.bfloat16)


def read_ends(ref):
    ends = ref[-2 * EXTRA :, :].astype(jnp.float32)
    return ends[:EXTRA] + ends[EXTRA:]


def spread_kernel(tab_ref, total_ref, gain_ref, base_ref, near_ref, near_c_ref, far_ref, *refs, devices):
    out_refs, (rows_ref, weight, sem) = refs[:4], refs[4:]
    columns = base_ref.shape[2]
    rows = pl.ds(pl.multiple_of(tab_ref[4] * TILE, TILE), TILE)
    copies = [
        pltpu.make_async_copy(shard.at[rows], weight.at[k], sem.at[k])
        for k, shard in enumerate((base_ref.at[0], near_c_ref.at[1], near_ref.at[0], far_ref.at[0]))
    ]
    for copy in copies:
        copy.start()
    rows_ref[...] = jnp.zeros_like(rows_ref)
    for k in range(4):
        out_refs[k][:columns, :] = total_ref[k].reshape(columns, TILE).astype(jnp.bfloat16)
    for k in range(4):
        copies[k].wait()
        total = total_ref[k].reshape(columns, TILE)
        part = jnp.sum(weight[k].astype(jnp.float32).T * total, axis=0, keepdims=True)
        gain = gain_ref[:, pl.ds(pl.multiple_of(tab_ref[k] * TILE, TILE), TILE)]
        rows_ref[pl.ds(tab_ref[5 + k], 1), :] = part / (gain * devices)
    for out_ref in out_refs:
        write_ends(out_ref, rows_ref[...])


def spread(total, gain, base, near, near_c, far, table, devices):
    columns = base.shape[2]
    return pl.pallas_call(
        functools.partial(spread_kernel, devices=devices),
        in_specs=[SMEM] + [VMEM] * 2 + [HBM] * 4,
        out_specs=[VMEM] * 4,
        out_shape=[jax.ShapeDtypeStruct((columns + 2 * EXTRA, TILE), jnp.bfloat16)] * 4,
        scratch_shapes=[
            pltpu.VMEM((EXTRA, TILE), jnp.float32),
            pltpu.VMEM((4, TILE, columns), jnp.bfloat16),
            pltpu.SemaphoreType.DMA((4,)),
        ],
        compiler_params=pltpu.CompilerParams(vmem_limit_bytes=LIMIT),
    )(table, total, gain, base, near, near_c, far)


def in_pairs(terms):
    while len(terms) > 1:
        terms = [a + b for a, b in zip(terms[::2], terms[1::2])]
    return terms[0]


def merge_kernel(*refs, scale):
    parts, out_ref = refs[:-1], refs[-1]
    columns = out_ref.shape[0] - 2 * EXTRA
    total = in_pairs([part[:columns, :].astype(jnp.float32) for part in parts])
    out_ref[:columns, :] = (total * scale).astype(jnp.bfloat16)
    write_ends(out_ref, in_pairs([read_ends(part) for part in parts]))


def merge(parts, scale=1.0):
    return pl.pallas_call(
        functools.partial(merge_kernel, scale=scale),
        in_specs=[VMEM] * len(parts),
        out_specs=VMEM,
        out_shape=jax.ShapeDtypeStruct(parts[0].shape, parts[0].dtype),
        compiler_params=pltpu.CompilerParams(vmem_limit_bytes=SMALL),
    )(*parts)


def finish_kernel(tab_ref, *refs):
    parts, (weight_ref, gain_ref) = refs[:4], refs[4:]
    columns = weight_ref.shape[1]
    for k, part in enumerate(parts):
        rows = pl.ds(pl.multiple_of(tab_ref[k] * TILE, TILE), TILE)
        weight_ref[rows, :] = part[:columns, :].astype(jnp.float32).T
        gain_ref[tab_ref[k]] = read_ends(part)


def finish(parts, table):
    columns = parts[0].shape[0] - 2 * EXTRA
    return pl.pallas_call(
        finish_kernel,
        in_specs=[SMEM] + [VMEM] * 4,
        out_specs=[VMEM] * 2,
        out_shape=[
            jax.ShapeDtypeStruct((4 * TILE, columns), jnp.float32),
            jax.ShapeDtypeStruct((4, EXTRA, TILE), jnp.float32),
        ],
        compiler_params=pltpu.CompilerParams(vmem_limit_bytes=SMALL),
    )(table, *parts)


def order_kernel(tab_ref, *refs):
    parts, out_ref = refs[:4], refs[4]
    for k, part in enumerate(parts):
        for x in range(4):
            for y in range(4):
                out_ref[tab_ref[k] + 2 * x, y : y + 1, :] = part[y, x : x + 1, :]


def order(parts, table):
    return pl.pallas_call(
        order_kernel,
        in_specs=[SMEM] + [VMEM] * 4,
        out_specs=VMEM,
        out_shape=jax.ShapeDtypeStruct((16, 4, TILE), jnp.float32),
        compiler_params=pltpu.CompilerParams(vmem_limit_bytes=SMALL),
    )(table, *parts)


def shards(tokens, norm_gain, weight_values, weight_scale, key_cotangent):
    y, zl, x, c = (lax.axis_index(a) for a in ("y", "zl", "x", "c"))
    width = tokens.shape[1]
    columns = weight_values.shape[1]
    gain = norm_gain.reshape(1, width)
    devices = 1
    for axis in EVERY:
        devices *= lax.axis_size(axis)

    def offset(core, first, second):
        masks = (1 + 2 * core, 3 - 2 * core)
        return first * masks[0] ^ second * masks[1]

    label = jnp.arange(32, dtype=jnp.int32)
    bits = [label // 16] + [label // k % 2 for k in (8, 4, 2, 1)]
    tables = []
    for core in (c, 1 - c):
        chip = (zl ^ bits[0]) * 4 + (x ^ offset(core, bits[3], bits[4]))
        tables.append((chip * 2 + core) * 4 + (y ^ offset(core, bits[1], bits[2])))

    def nodes_of(pieces):
        at = [((zl ^ z) * 4 + (x ^ offset(c, k % 2, k // 2))) * 2 + (c ^ lane) for z, k, lane in pieces]
        return jnp.stack(at).astype(jnp.int32)

    own = widen_weight(weight_values, weight_scale)
    own_c = swap(own, "c")
    up = pair_z(own)
    cot_own = key_cotangent.T
    base = jnp.stack([own, own_c])
    cot_got = swap(cot_own, "c")
    mine, other, inverse = norm_tiles(tokens, gain, tie(jnp.stack(tables), base, cot_own))
    got = swap(other, "c")
    near = pair(base, "x", 0)
    sent, kept = grad_tiles(mine, got, cot_own, cot_got)

    moved = [pair(sent[0], "y", 0), pair_z(sent[1])]
    (first, kept_first), (second, kept_second) = (halve(add(k, m)) for k, m in zip(kept, moved))

    first, near, up = lax.optimization_barrier((first, near, up))
    moved = [pair_z(first), pair(second, "y", 0)]
    near_c = swap(near, "c")
    above = jnp.stack([up, swap(up, "c")])
    above_near = pair(above, "x", 0)
    far = pair(near_c[1:], "x", 0)
    early = [base, above, near, near_c]
    sums = forward(tokens, inverse, gain, early, nodes_of(BASE + ABOVE + NEAR + NEAR_C))
    moved[1], sums, above_near, far = lax.optimization_barrier((moved[1], sums, above_near, far))
    above_near_c = swap(above_near, "c")
    above_far = pair(above_near_c[1:], "x", 0)
    (first, kept_first), (second, kept_second) = (
        halve(add(k, m)) for k, m in zip((kept_first, kept_second), moved)
    )

    moved = pair(jnp.stack([first, second]), "y", 1)
    far_c = swap(far, "c")
    moved, above_far, far_c = lax.optimization_barrier((moved, above_far, far_c))
    total = jnp.stack([add(kept_first, moved[0]), add(kept_second, moved[1])], axis=1)

    peer = x ^ offset(c, jnp.arange(4) // 2, jnp.arange(4) % 2)
    node_tile = ((zl * 4 + peer) * 2 + c) * 4 + y
    at = jnp.concatenate([node_tile, y[None], peer]).astype(jnp.int32)
    parts = list(spread(total, gain, base, near, near_c, far, at, devices))
    parts[0], above_far = lax.optimization_barrier((parts[0], above_far))
    moved = [parts[0], pair(parts[2], "x", 0), pair(parts[1], "x", 1), across(parts[3], "x")]
    above_far_c = swap(above_far, "c")
    late = [above_near, above_near_c, far, above_far, far_c, above_far_c]
    late_at = nodes_of(ABOVE_NEAR + ABOVE_NEAR_C + FAR + ABOVE_FAR + FAR_C + ABOVE_FAR_C)
    projected, moment = forward_last(tokens, inverse, gain, key_cotangent, late, sums, late_at)
    moved[3], moment = lax.optimization_barrier((moved[3], moment))
    send = merge(moved)

    def part_of_grads(before, weights, pieces):
        return backward(
            tokens, inverse, gain, key_cotangent, moment, weights, nodes_of(pieces), before
        )

    send, moment = lax.optimization_barrier((send, moment))
    moved = pair(send, "zh", 0)
    token_grads = part_of_grads((), [base, above, near], BASE + ABOVE + NEAR)
    moved, token_grads = lax.optimization_barrier((moved, token_grads))
    send = merge((send, moved))
    send, token_grads = lax.optimization_barrier((send, token_grads))
    moved = pair(send, "zh", 1)
    token_grads = part_of_grads(
        (token_grads,), [near_c, above_near, far], NEAR_C + ABOVE_NEAR + FAR
    )
    moved, token_grads = lax.optimization_barrier((moved, token_grads))
    send = merge((send, moved), 1.0 / devices)

    parts = (send, pair(send, "y", 0), pair(send, "y", 1), across(send, "y"))
    quarters = jnp.stack([y ^ offset(c, k % 2, k // 2) for k in range(4)]).astype(jnp.int32)
    token_grads = part_of_grads(
        (tie(token_grads, send),),
        [above_near_c, above_far, far_c, above_far_c],
        ABOVE_NEAR_C + ABOVE_FAR + FAR_C + ABOVE_FAR_C,
    )
    parts, token_grads = lax.optimization_barrier((parts, token_grads))
    weight_grads, gains = finish(parts, quarters)
    gains = (gains, swap(gains, "c"), swap(gains, "zl"), swap(gains, ("zl", "c")))
    nodes = jnp.stack([(zl ^ k // 2) * 8 + (c ^ k % 2) for k in range(4)]).astype(jnp.int32)
    gain_grads = order(gains, nodes).reshape(width)
    return (projected, token_grads, weight_grads, gain_grads)


def solution(mesh):
    fine = Mesh(mesh.devices.reshape(4, 4, 2, 4, 2), EVERY)
    rows = P(EVERY, None)
    return jax.shard_map(
        shards,
        mesh=fine,
        in_specs=(rows, P(), P(NODE, None), P(NODE, None), rows),
        out_specs=(rows, rows, P(NODE, None), P()),
        check_vma=False,
    )
```

```python
import functools

import jax
import jax.numpy as jnp
from jax import lax
from jax.experimental import pallas as pl
from jax.experimental.pallas import tpu as pltpu
from jax.sharding import Mesh, PartitionSpec as P

NODE = ("zl", "x", "c")
EVERY = ("y", "zh", "zl", "x", "c")
TILE = 128
EXTRA = 8
LIMIT = 16 * 2**20
SMALL = 8 * 2**20
QUICK = pl.CostEstimate(flops=1, bytes_accessed=1, transcendentals=0)
VMEM = pl.BlockSpec(memory_space=pltpu.VMEM)
SMEM = pl.BlockSpec(memory_space=pltpu.SMEM)
HBM = pl.BlockSpec(memory_space=pltpu.HBM)


def widen_kernel(values_ref, scales_ref, out_ref):
    blocks = scales_ref.shape[0]
    block = values_ref.shape[1] // blocks
    scales = scales_ref[...].astype(jnp.float32)
    scales = jnp.concatenate([scales] * (8 // blocks), axis=0).T
    for k in range(blocks):
        part = slice(k * block, (k + 1) * block)
        wide = values_ref[:, part].astype(jnp.float32)
        out_ref[:, part] = (wide * scales[:, k : k + 1]).astype(jnp.bfloat16)


def widen_weight(values, scales):
    return pl.pallas_call(
        widen_kernel,
        out_shape=jax.ShapeDtypeStruct(values.shape, jnp.bfloat16),
        compiler_params=pltpu.CompilerParams(vmem_limit_bytes=SMALL),
    )(values, scales.T)


def norm_kernel(tab_ref, tok_ref, gain_ref, own_ref, oth_ref, inv_ref, block, sem):
    count, rows, width = block.shape

    def block_in(k):
        return pltpu.make_async_copy(tok_ref.at[pl.ds(k * rows, rows)], block.at[k], sem.at[k])

    for k in range(count):
        block_in(k).start()
    for k in range(count):
        block_in(k).wait()
        part = slice(k * rows, (k + 1) * rows)
        total = jnp.zeros((rows, TILE), jnp.float32)
        for t in range(width // TILE):
            wide = block[k, :, t * TILE : (t + 1) * TILE].astype(jnp.float32)
            total = total + wide * wide
        mean = jnp.sum(total, axis=1, keepdims=True) / width
        inverse = lax.rsqrt(mean + 1e-05)
        inv_ref[part, :] = inverse
        for side, out_ref in enumerate((own_ref, oth_ref)):
            for r in range(width // TILE // 2):
                at = pl.multiple_of(tab_ref[side, r] * TILE, TILE)
                wide = block[k, :, pl.ds(at, TILE)].astype(jnp.float32)
                scaled = wide * inverse * gain_ref[:, pl.ds(at, TILE)]
                out_ref[part, r * TILE : (r + 1) * TILE] = scaled.astype(jnp.bfloat16)


def norm_tiles(tokens, gain, table):
    rows, width = tokens.shape
    step = 64 if rows % 64 == 0 else rows
    return pl.pallas_call(
        norm_kernel,
        in_specs=[SMEM, HBM, VMEM],
        out_specs=[VMEM] * 3,
        out_shape=[
            jax.ShapeDtypeStruct((rows, width // 2), jnp.bfloat16),
            jax.ShapeDtypeStruct((rows, width // 2), jnp.bfloat16),
            jax.ShapeDtypeStruct((rows, 1), jnp.float32),
        ],
        scratch_shapes=[
            pltpu.VMEM((rows // step, step, width), jnp.bfloat16),
            pltpu.SemaphoreType.DMA((rows // step,)),
        ],
        compiler_params=pltpu.CompilerParams(vmem_limit_bytes=LIMIT),
        cost_estimate=QUICK,
    )(table, *in_hbm(tokens), gain)


def grad_kernel(own_ref, got_ref, cot_own_ref, cot_got_ref, sent_ref, kept_ref, *, side):
    span = 2 * TILE
    half = cot_own_ref.shape[0] // 2
    rows = slice(side * half, (side + 1) * half)
    cot_own = cot_own_ref[rows, :]
    cot_got = cot_got_ref[rows, :]
    for pair in range(own_ref.shape[1] // span):
        part = slice(pair * span, (pair + 1) * span)
        grads = jnp.dot(cot_own, own_ref[:, part], preferred_element_type=jnp.float32)
        grads += jnp.dot(cot_got, got_ref[:, part], preferred_element_type=jnp.float32)
        for which in range(2):
            tile = pair * 2 + which
            z, y1, rest = tile // 16, tile // 8 % 2, tile % 8
            sent, at = ((y1, z * 8 + rest), (z, y1 * 8 + rest))[side]
            piece = grads[:, which * TILE : (which + 1) * TILE]
            if sent:
                sent_ref[at] = piece.astype(jnp.bfloat16)
            else:
                kept_ref[at] = piece


def grad_tiles(own, got, cot_own, cot_got, side):
    width = own.shape[1]
    shape = (width // TILE // 2, cot_own.shape[0] // 2, TILE)
    return pl.pallas_call(
        functools.partial(grad_kernel, side=side),
        out_shape=[
            jax.ShapeDtypeStruct(shape, jnp.bfloat16),
            jax.ShapeDtypeStruct(shape, jnp.float32),
        ],
        compiler_params=pltpu.CompilerParams(vmem_limit_bytes=LIMIT),
        cost_estimate=QUICK,
    )(own, got, cot_own, cot_got)


class Inputs:
    def __init__(self, tab_ref, tok_ref, w_refs, block, weight, sem, weight_sem):
        shards_ = [ref.at[k] for ref in w_refs for k in range(ref.shape[0])]
        self.count, _, self.span = block.shape
        self.tab_ref, self.block, self.weight = tab_ref, block, weight
        self.copies = []
        for k in range(self.count):
            self.copies.append(
                (
                    pltpu.make_async_copy(tok_ref.at[:, self.columns(k)], block.at[k], sem.at[k]),
                    pltpu.make_async_copy(shards_[k], weight.at[k], weight_sem.at[k]),
                )
            )
        for pair_ in self.copies:
            for copy in pair_:
                copy.start()

    def columns(self, k):
        return pl.ds(pl.multiple_of(self.tab_ref[k] * self.span, self.span), self.span)

    def wait(self, k):
        for copy in self.copies[k]:
            copy.wait()

    @staticmethod
    def scratch(rows, span, columns, count):
        return [
            pltpu.VMEM((count, rows, span), jnp.bfloat16),
            pltpu.VMEM((count, span, columns), jnp.bfloat16),
            pltpu.SemaphoreType.DMA((count,)),
            pltpu.SemaphoreType.DMA((count,)),
        ]


def forward_steps(inputs, inv_ref, gain_ref, acc):
    inverse = inv_ref[...]
    for k in range(inputs.count):
        inputs.wait(k)
        wide = inputs.block[k].astype(jnp.float32)
        normed = (wide * inverse * gain_ref[:, inputs.columns(k)]).astype(jnp.bfloat16)
        acc[...] += jnp.dot(normed, inputs.weight[k], preferred_element_type=jnp.float32)


def forward_kernel(tab_ref, tok_ref, inv_ref, gain_ref, *refs):
    w_refs, (acc, *scratch) = refs[:-5], refs[-5:]
    inputs = Inputs(tab_ref, tok_ref, w_refs, *scratch)
    acc[...] = jnp.zeros_like(acc)
    forward_steps(inputs, inv_ref, gain_ref, acc)


def forward_last_kernel(tab_ref, tok_ref, inv_ref, gain_ref, cot_ref, acc_in, *refs):
    w_refs, (proj_ref, moment_ref, acc, *scratch) = refs[:-7], refs[-7:]
    inputs = Inputs(tab_ref, tok_ref, w_refs, *scratch)
    acc[...] = acc_in[...]
    forward_steps(inputs, inv_ref, gain_ref, acc)
    keys = acc[...]
    inverse = inv_ref[...]
    proj_ref[...] = keys.astype(jnp.bfloat16)
    inner = jnp.sum(cot_ref[...].astype(jnp.float32) * keys, axis=1, keepdims=True)
    moment_ref[...] = inverse * inverse * inner / tok_ref.shape[1]


def backward_kernel(tab_ref, tok_ref, inv_ref, gain_ref, cot_ref, moment_ref, *refs, count):
    w_refs, (grads_ref, out, out_sem, *scratch) = refs[:count], refs[-7:]
    inputs = Inputs(tab_ref, tok_ref, w_refs, *scratch)

    def block_out(k):
        return pltpu.make_async_copy(
            out.at[k], grads_ref.at[:, inputs.columns(k)], out_sem.at[k]
        )

    inverse, moment, cot = inv_ref[...], moment_ref[...], cot_ref[...]
    for k in range(inputs.count):
        inputs.wait(k)
        partial = lax.dot_general(
            cot, inputs.weight[k], (((1,), (1,)), ((), ())), preferred_element_type=jnp.float32
        )
        wide = inputs.block[k].astype(jnp.float32)
        grads = inverse * gain_ref[:, inputs.columns(k)] * partial - wide * moment
        out[k] = grads.astype(jnp.bfloat16)
        block_out(k).start()
    for k in range(inputs.count):
        block_out(k).wait()


def in_hbm(*arrays):
    return [pltpu.with_memory_space_constraint(array, pltpu.HBM) for array in arrays]


def costs(tokens, columns):
    rows, width = tokens.shape
    return dict(
        compiler_params=pltpu.CompilerParams(vmem_limit_bytes=LIMIT),
        cost_estimate=pl.CostEstimate(
            flops=rows * width * columns,
            bytes_accessed=2 * rows * width + width * columns,
            transcendentals=0,
        ),
    )


def forward(tokens, inverse, gain, weights, table):
    rows, span, columns = tokens.shape[0], *weights[0].shape[1:]
    return pl.pallas_call(
        forward_kernel,
        in_specs=[SMEM, HBM] + [VMEM] * 2 + [HBM] * len(weights),
        out_specs=VMEM,
        out_shape=jax.ShapeDtypeStruct((rows, columns), jnp.float32),
        scratch_shapes=Inputs.scratch(rows, span, columns, table.shape[0]),
        **costs(tokens, columns),
    )(table, *in_hbm(tokens), inverse, gain, *in_hbm(*weights))


def forward_last(tokens, inverse, gain, cotangent, weights, sums, table):
    rows, span, columns = tokens.shape[0], *weights[0].shape[1:]
    return pl.pallas_call(
        forward_last_kernel,
        in_specs=[SMEM, HBM] + [VMEM] * 4 + [HBM] * len(weights),
        out_specs=[VMEM] * 2,
        out_shape=[
            jax.ShapeDtypeStruct((rows, columns), jnp.bfloat16),
            jax.ShapeDtypeStruct((rows, 1), jnp.float32),
        ],
        scratch_shapes=[pltpu.VMEM((rows, columns), jnp.float32)]
        + Inputs.scratch(rows, span, columns, table.shape[0]),
        **costs(tokens, columns),
    )(table, *in_hbm(tokens), inverse, gain, cotangent, sums, *in_hbm(*weights))


def backward(tokens, inverse, gain, cotangent, moment, weights, table, before=()):
    rows, span, columns = tokens.shape[0], *weights[0].shape[1:]
    count = table.shape[0]
    return pl.pallas_call(
        functools.partial(backward_kernel, count=len(weights)),
        in_specs=[SMEM, HBM] + [VMEM] * 4 + [HBM] * (len(weights) + len(before)),
        out_specs=HBM,
        out_shape=jax.ShapeDtypeStruct(tokens.shape, jnp.bfloat16),
        scratch_shapes=[
            pltpu.VMEM((count, rows, span), jnp.bfloat16),
            pltpu.SemaphoreType.DMA((count,)),
        ]
        + Inputs.scratch(rows, span, columns, count),
        input_output_aliases={6 + len(weights): 0} if before else {},
        **costs(tokens, columns),
    )(table, *in_hbm(tokens), inverse, gain, cotangent, moment, *in_hbm(*weights, *before))


def swap(array, axis):
    last = lax.axis_size(axis) - 1
    return lax.ppermute(array, axis, [(a, last - a) for a in range(last + 1)])


def pair(array, axis, step):
    size = lax.axis_size(axis)
    masks = (1, 3) if step == 0 else (3, 1)
    moves = [(a * 2 + c, (a ^ masks[c]) * 2 + c) for a in range(size) for c in range(2)]
    return lax.ppermute(array, (axis, "c"), moves)


def across(array, axis):
    size = lax.axis_size(axis)
    return lax.ppermute(array, axis, [(a, a ^ 2) for a in range(size)])


def pair_z(array):
    size = lax.axis_size("zh") * lax.axis_size("zl")
    moves = []
    for z in range(size):
        moves.append((z * 2, (z ^ 1) * 2))
        moves.append((z * 2 + 1, (z + (1 if z % 2 else -1)) % size * 2 + 1))
    return lax.ppermute(array, ("zh", "zl", "c"), moves)


def add(kept, got):
    return kept + got.astype(jnp.float32)


def add_halves(kept, got):
    half = kept.shape[0] // 2
    return add(kept[half:], got[half:]).astype(jnp.bfloat16), add(kept[:half], got[:half])


def tie(first, *others):
    return lax.optimization_barrier((first, *others))[0]


BASE, ABOVE = (((z, 0, 0), (z, 0, 1)) for z in (0, 1))
NEAR, ABOVE_NEAR = (((z, 1, 0), (z, 1, 1)) for z in (0, 1))
NEAR_C, ABOVE_NEAR_C = (((z, 2, 1), (z, 2, 0)) for z in (0, 1))
FAR, ABOVE_FAR = (((z, 3, 0),) for z in (0, 1))
FAR_C, ABOVE_FAR_C = (((z, 3, 1),) for z in (0, 1))


def write_ends(out_ref, rows):
    high = rows.astype(jnp.bfloat16).astype(jnp.float32)
    out_ref[-2 * EXTRA :, :] = jnp.concatenate([high, rows - high]).astype(jnp.bfloat16)


def read_ends(ref):
    ends = ref[-2 * EXTRA :, :].astype(jnp.float32)
    return ends[:EXTRA] + ends[EXTRA:]


def spread_kernel(tab_ref, total_ref, gain_ref, base_ref, near_ref, near_c_ref, far_ref, *refs, devices):
    out_refs, (rows_ref, weight, sem) = refs[:4], refs[4:]
    columns = base_ref.shape[2]
    rows = pl.ds(pl.multiple_of(tab_ref[4] * TILE, TILE), TILE)
    copies = [
        pltpu.make_async_copy(shard.at[rows], weight.at[k], sem.at[k])
        for k, shard in enumerate((base_ref.at[0], near_c_ref.at[1], near_ref.at[0], far_ref.at[0]))
    ]
    for copy in copies:
        copy.start()
    rows_ref[...] = jnp.zeros_like(rows_ref)
    for k in range(4):
        out_refs[k][:columns, :] = total_ref[k].reshape(columns, TILE).astype(jnp.bfloat16)
    for k in range(4):
        copies[k].wait()
        total = total_ref[k].reshape(columns, TILE)
        part = jnp.sum(weight[k].astype(jnp.float32).T * total, axis=0, keepdims=True)
        gain = gain_ref[:, pl.ds(pl.multiple_of(tab_ref[k] * TILE, TILE), TILE)]
        rows_ref[pl.ds(tab_ref[5 + k], 1), :] = part / (gain * devices)
    for out_ref in out_refs:
        write_ends(out_ref, rows_ref[...])


def spread(total, gain, base, near, near_c, far, table, devices):
    columns = base.shape[2]
    return pl.pallas_call(
        functools.partial(spread_kernel, devices=devices),
        in_specs=[SMEM] + [VMEM] * 2 + [HBM] * 4,
        out_specs=[VMEM] * 4,
        out_shape=[jax.ShapeDtypeStruct((columns + 2 * EXTRA, TILE), jnp.bfloat16)] * 4,
        scratch_shapes=[
            pltpu.VMEM((EXTRA, TILE), jnp.float32),
            pltpu.VMEM((4, TILE, columns), jnp.bfloat16),
            pltpu.SemaphoreType.DMA((4,)),
        ],
        compiler_params=pltpu.CompilerParams(vmem_limit_bytes=LIMIT),
    )(table, total, gain, *in_hbm(base, near, near_c, far))


def in_pairs(terms):
    while len(terms) > 1:
        terms = [a + b for a, b in zip(terms[::2], terms[1::2])]
    return terms[0]


def merge_kernel(*refs, scale):
    parts, out_ref = refs[:-1], refs[-1]
    columns = out_ref.shape[0] - 2 * EXTRA
    total = in_pairs([part[:columns, :].astype(jnp.float32) for part in parts])
    out_ref[:columns, :] = (total * scale).astype(jnp.bfloat16)
    write_ends(out_ref, in_pairs([read_ends(part) for part in parts]))


def merge(parts, scale=1.0):
    return pl.pallas_call(
        functools.partial(merge_kernel, scale=scale),
        in_specs=[VMEM] * len(parts),
        out_specs=VMEM,
        out_shape=jax.ShapeDtypeStruct(parts[0].shape, parts[0].dtype),
        compiler_params=pltpu.CompilerParams(vmem_limit_bytes=SMALL),
    )(*parts)


def finish_kernel(tab_ref, *refs):
    parts, (weight_ref, gain_ref) = refs[:4], refs[4:]
    columns = weight_ref.shape[1]
    for k, part in enumerate(parts):
        rows = pl.ds(pl.multiple_of(tab_ref[k] * TILE, TILE), TILE)
        weight_ref[rows, :] = part[:columns, :].astype(jnp.float32).T
        gain_ref[tab_ref[k]] = read_ends(part)


def finish(parts, table):
    columns = parts[0].shape[0] - 2 * EXTRA
    return pl.pallas_call(
        finish_kernel,
        in_specs=[SMEM] + [VMEM] * 4,
        out_specs=[VMEM] * 2,
        out_shape=[
            jax.ShapeDtypeStruct((4 * TILE, columns), jnp.float32),
            jax.ShapeDtypeStruct((4, EXTRA, TILE), jnp.float32),
        ],
        compiler_params=pltpu.CompilerParams(vmem_limit_bytes=SMALL),
    )(table, *parts)


def order_kernel(tab_ref, *refs):
    parts, out_ref = refs[:4], refs[4]
    for k, part in enumerate(parts):
        for x in range(4):
            for y in range(4):
                out_ref[tab_ref[k] + 2 * x, y : y + 1, :] = part[y, x : x + 1, :]


def order(parts, table):
    return pl.pallas_call(
        order_kernel,
        in_specs=[SMEM] + [VMEM] * 4,
        out_specs=VMEM,
        out_shape=jax.ShapeDtypeStruct((16, 4, TILE), jnp.float32),
        compiler_params=pltpu.CompilerParams(vmem_limit_bytes=SMALL),
    )(table, *parts)


def shards(tokens, norm_gain, weight_values, weight_scale, key_cotangent):
    y, zl, x, c = (lax.axis_index(a) for a in ("y", "zl", "x", "c"))
    width = tokens.shape[1]
    columns = weight_values.shape[1]
    gain = norm_gain.reshape(1, width)
    devices = 1
    for axis in EVERY:
        devices *= lax.axis_size(axis)

    def offset(core, first, second):
        masks = (1 + 2 * core, 3 - 2 * core)
        return first * masks[0] ^ second * masks[1]

    label = jnp.arange(32, dtype=jnp.int32)
    bits = [label // 16] + [label // k % 2 for k in (8, 4, 2, 1)]
    tables = []
    for core in (c, 1 - c):
        chip = (zl ^ bits[0]) * 4 + (x ^ offset(core, bits[3], bits[4]))
        tables.append((chip * 2 + core) * 4 + (y ^ offset(core, bits[1], bits[2])))

    def nodes_of(pieces):
        at = [((zl ^ z) * 4 + (x ^ offset(c, k % 2, k // 2))) * 2 + (c ^ lane) for z, k, lane in pieces]
        return jnp.stack(at).astype(jnp.int32)

    own = widen_weight(weight_values, weight_scale)
    own_c = swap(own, "c")
    up = pair_z(own)
    cot_own = key_cotangent.T
    base = jnp.stack([own, own_c])
    cot_got = swap(cot_own, "c")
    mine, other, inverse = norm_tiles(tokens, gain, tie(jnp.stack(tables), base, cot_own))
    got = swap(other, "c")
    near = pair(base, "x", 0)

    first, kept_first = grad_tiles(mine, got, cot_own, cot_got, 0)
    mine, up, first = lax.optimization_barrier((mine, up, first))
    second, kept_second = grad_tiles(mine, got, cot_own, cot_got, 1)
    moved = [pair(first, "y", 0), pair_z(second)]
    above = jnp.stack([up, swap(up, "c")])
    above_near = pair(above, "x", 0)
    (first, kept_first), (second, kept_second) = map(
        add_halves, (kept_first, kept_second), moved
    )

    first, near = lax.optimization_barrier((first, near))
    moved = [pair_z(first), pair(second, "y", 0)]
    near_c = swap(near, "c")
    far = pair(near_c[1:], "x", 0)
    early = [base, above, near, near_c]
    sums = forward(tokens, inverse, gain, early, nodes_of(BASE + ABOVE + NEAR + NEAR_C))
    moved[1], sums, above_near = lax.optimization_barrier((moved[1], sums, above_near))
    above_near_c = swap(above_near, "c")
    above_far = pair(above_near_c[1:], "x", 0)
    (first, kept_first), (second, kept_second) = map(
        add_halves, (kept_first, kept_second), moved
    )

    moved = pair(jnp.stack([first, second]), "y", 1)
    far_c = swap(far, "c")
    moved, above_far, far_c = lax.optimization_barrier((moved, above_far, far_c))
    total = jnp.stack([add(kept_first, moved[0]), add(kept_second, moved[1])], axis=1)

    peer = x ^ offset(c, jnp.arange(4) // 2, jnp.arange(4) % 2)
    node_tile = ((zl * 4 + peer) * 2 + c) * 4 + y
    at = jnp.concatenate([node_tile, y[None], peer]).astype(jnp.int32)
    parts = list(spread(total, gain, base, near, near_c, far, at, devices))
    parts[0], above_far = lax.optimization_barrier((parts[0], above_far))
    moved = [parts[0], pair(parts[2], "x", 0), pair(parts[1], "x", 1), across(parts[3], "x")]
    above_far_c = swap(above_far, "c")
    late = [above_near, above_near_c, far, above_far, far_c, above_far_c]
    late_at = nodes_of(ABOVE_NEAR + ABOVE_NEAR_C + FAR + ABOVE_FAR + FAR_C + ABOVE_FAR_C)
    projected, moment = forward_last(tokens, inverse, gain, key_cotangent, late, sums, late_at)
    moved[3], moment = lax.optimization_barrier((moved[3], moment))
    send = merge(moved)

    def part_of_grads(before, weights, pieces):
        return backward(
            tokens, inverse, gain, key_cotangent, moment, weights, nodes_of(pieces), before
        )

    send, moment = lax.optimization_barrier((send, moment))
    moved = pair(send, "zh", 0)
    token_grads = part_of_grads((), [base, above, near], BASE + ABOVE + NEAR)
    moved, token_grads = lax.optimization_barrier((moved, token_grads))
    send = merge((send, moved))
    send, token_grads = lax.optimization_barrier((send, token_grads))
    moved = pair(send, "zh", 1)
    token_grads = part_of_grads(
        (token_grads,), [near_c, above_near, far], NEAR_C + ABOVE_NEAR + FAR
    )
    moved, token_grads = lax.optimization_barrier((moved, token_grads))
    send = merge((send, moved), 1.0 / devices)

    parts = (send, pair(send, "y", 0), pair(send, "y", 1), across(send, "y"))
    quarters = jnp.stack([y ^ offset(c, k % 2, k // 2) for k in range(4)]).astype(jnp.int32)
    token_grads = part_of_grads(
        (tie(token_grads, send),),
        [above_near_c, above_far, far_c, above_far_c],
        ABOVE_NEAR_C + ABOVE_FAR + FAR_C + ABOVE_FAR_C,
    )
    parts, token_grads = lax.optimization_barrier((parts, token_grads))
    weight_grads, gains = finish(parts, quarters)
    gains = (gains, swap(gains, "c"), swap(gains, "zl"), swap(gains, ("zl", "c")))
    nodes = jnp.stack([(zl ^ k // 2) * 8 + (c ^ k % 2) for k in range(4)]).astype(jnp.int32)
    gain_grads = order(gains, nodes).reshape(width)
    return (projected, token_grads, weight_grads, gain_grads)


def solution(mesh):
    fine = Mesh(mesh.devices.reshape(4, 4, 2, 4, 2), EVERY)
    rows = P(EVERY, None)
    return jax.shard_map(
        shards,
        mesh=fine,
        in_specs=(rows, P(), P(NODE, None), P(NODE, None), rows),
        out_specs=(rows, rows, P(NODE, None), P()),
        check_vma=False,
    )
```

```python
import functools

import jax
import jax.numpy as jnp
from jax import lax
from jax.experimental import pallas as pl
from jax.experimental.pallas import tpu as pltpu
from jax.sharding import Mesh, PartitionSpec as P

NODE = ("zl", "x", "c")
EVERY = ("y", "zh", "zl", "x", "c")
TILE = 128
EXTRA = 8
LIMIT = 16 * 2**20
SMALL = 8 * 2**20
QUICK = pl.CostEstimate(flops=1, bytes_accessed=1, transcendentals=0)
VMEM = pl.BlockSpec(memory_space=pltpu.VMEM)
SMEM = pl.BlockSpec(memory_space=pltpu.SMEM)
HBM = pl.BlockSpec(memory_space=pltpu.HBM)


def widen_kernel(values_ref, scales_ref, out_ref):
    blocks = scales_ref.shape[0]
    block = values_ref.shape[1] // blocks
    scales = scales_ref[...].astype(jnp.float32)
    scales = jnp.concatenate([scales] * (8 // blocks), axis=0).T
    for k in range(blocks):
        part = slice(k * block, (k + 1) * block)
        wide = values_ref[:, part].astype(jnp.float32)
        out_ref[:, part] = (wide * scales[:, k : k + 1]).astype(jnp.bfloat16)


def widen_weight(values, scales):
    return pl.pallas_call(
        widen_kernel,
        out_shape=jax.ShapeDtypeStruct(values.shape, jnp.bfloat16),
        compiler_params=pltpu.CompilerParams(vmem_limit_bytes=SMALL),
    )(values, scales.T)


def norm_kernel(tab_ref, tok_ref, gain_ref, own_ref, oth_ref, inv_ref, block, sem):
    count, rows, width = block.shape

    def block_in(k):
        return pltpu.make_async_copy(tok_ref.at[pl.ds(k * rows, rows)], block.at[k], sem.at[k])

    for k in range(count):
        block_in(k).start()
    for k in range(count):
        block_in(k).wait()
        part = slice(k * rows, (k + 1) * rows)
        total = jnp.zeros((rows, TILE), jnp.float32)
        for t in range(width // TILE):
            wide = block[k, :, t * TILE : (t + 1) * TILE].astype(jnp.float32)
            total = total + wide * wide
        mean = jnp.sum(total, axis=1, keepdims=True) / width
        inverse = lax.rsqrt(mean + 1e-05)
        inv_ref[part, :] = inverse
        for side, out_ref in enumerate((own_ref, oth_ref)):
            for r in range(width // TILE // 2):
                at = pl.multiple_of(tab_ref[side, r] * TILE, TILE)
                wide = block[k, :, pl.ds(at, TILE)].astype(jnp.float32)
                scaled = wide * inverse * gain_ref[:, pl.ds(at, TILE)]
                out_ref[part, r * TILE : (r + 1) * TILE] = scaled.astype(jnp.bfloat16)


def norm_tiles(tokens, gain, table):
    rows, width = tokens.shape
    step = 64 if rows % 64 == 0 else rows
    return pl.pallas_call(
        norm_kernel,
        in_specs=[SMEM, HBM, VMEM],
        out_specs=[VMEM] * 3,
        out_shape=[
            jax.ShapeDtypeStruct((rows, width // 2), jnp.bfloat16),
            jax.ShapeDtypeStruct((rows, width // 2), jnp.bfloat16),
            jax.ShapeDtypeStruct((rows, 1), jnp.float32),
        ],
        scratch_shapes=[
            pltpu.VMEM((rows // step, step, width), jnp.bfloat16),
            pltpu.SemaphoreType.DMA((rows // step,)),
        ],
        compiler_params=pltpu.CompilerParams(vmem_limit_bytes=LIMIT),
        cost_estimate=QUICK,
    )(table, *in_hbm(tokens), gain)


def grad_kernel(own_ref, got_ref, cot_own_ref, cot_got_ref, sent_ref, kept_ref, *, side):
    span = 2 * TILE
    half = cot_own_ref.shape[0] // 2
    rows = slice(side * half, (side + 1) * half)
    cot_own = cot_own_ref[rows, :]
    cot_got = cot_got_ref[rows, :]
    for pair in range(own_ref.shape[1] // span):
        part = slice(pair * span, (pair + 1) * span)
        grads = jnp.dot(cot_own, own_ref[:, part], preferred_element_type=jnp.float32)
        grads += jnp.dot(cot_got, got_ref[:, part], preferred_element_type=jnp.float32)
        for which in range(2):
            tile = pair * 2 + which
            z, y1, rest = tile // 16, tile // 8 % 2, tile % 8
            sent, at = ((y1, z * 8 + rest), (z, y1 * 8 + rest))[side]
            piece = grads[:, which * TILE : (which + 1) * TILE]
            if sent:
                sent_ref[at] = piece.astype(jnp.bfloat16)
            else:
                kept_ref[at] = piece


def grad_tiles(own, got, cot_own, cot_got, side):
    width = own.shape[1]
    shape = (width // TILE // 2, cot_own.shape[0] // 2, TILE)
    return pl.pallas_call(
        functools.partial(grad_kernel, side=side),
        out_shape=[
            jax.ShapeDtypeStruct(shape, jnp.bfloat16),
            jax.ShapeDtypeStruct(shape, jnp.float32),
        ],
        compiler_params=pltpu.CompilerParams(vmem_limit_bytes=LIMIT),
        cost_estimate=QUICK,
    )(own, got, cot_own, cot_got)


class Inputs:
    def __init__(self, tab_ref, tok_ref, w_refs, block, weight, sem, weight_sem):
        shards_ = [ref.at[k] for ref in w_refs for k in range(ref.shape[0])]
        self.count, _, self.span = block.shape
        self.tab_ref, self.block, self.weight = tab_ref, block, weight
        self.copies = []
        for k in range(self.count):
            self.copies.append(
                (
                    pltpu.make_async_copy(tok_ref.at[:, self.columns(k)], block.at[k], sem.at[k]),
                    pltpu.make_async_copy(shards_[k], weight.at[k], weight_sem.at[k]),
                )
            )
        for pair_ in self.copies:
            for copy in pair_:
                copy.start()

    def columns(self, k):
        return pl.ds(pl.multiple_of(self.tab_ref[k] * self.span, self.span), self.span)

    def wait(self, k):
        for copy in self.copies[k]:
            copy.wait()

    @staticmethod
    def scratch(rows, span, columns, count):
        return [
            pltpu.VMEM((count, rows, span), jnp.bfloat16),
            pltpu.VMEM((count, span, columns), jnp.bfloat16),
            pltpu.SemaphoreType.DMA((count,)),
            pltpu.SemaphoreType.DMA((count,)),
        ]


def forward_steps(inputs, inv_ref, gain_ref, acc):
    inverse = inv_ref[...]
    for k in range(inputs.count):
        inputs.wait(k)
        wide = inputs.block[k].astype(jnp.float32)
        normed = (wide * inverse * gain_ref[:, inputs.columns(k)]).astype(jnp.bfloat16)
        acc[...] += jnp.dot(normed, inputs.weight[k], preferred_element_type=jnp.float32)


def forward_kernel(tab_ref, tok_ref, inv_ref, gain_ref, *refs):
    w_refs, (acc, *scratch) = refs[:-5], refs[-5:]
    inputs = Inputs(tab_ref, tok_ref, w_refs, *scratch)
    acc[...] = jnp.zeros_like(acc)
    forward_steps(inputs, inv_ref, gain_ref, acc)


def forward_last_kernel(tab_ref, tok_ref, inv_ref, gain_ref, cot_ref, acc_in, *refs):
    w_refs, (proj_ref, moment_ref, acc, *scratch) = refs[:-7], refs[-7:]
    inputs = Inputs(tab_ref, tok_ref, w_refs, *scratch)
    acc[...] = acc_in[...]
    forward_steps(inputs, inv_ref, gain_ref, acc)
    keys = acc[...]
    inverse = inv_ref[...]
    proj_ref[...] = keys.astype(jnp.bfloat16)
    inner = jnp.sum(cot_ref[...].astype(jnp.float32) * keys, axis=1, keepdims=True)
    moment_ref[...] = inverse * inverse * inner / tok_ref.shape[1]


def backward_kernel(tab_ref, tok_ref, inv_ref, gain_ref, cot_ref, moment_ref, *refs, count):
    w_refs, (grads_ref, out, out_sem, *scratch) = refs[:count], refs[-7:]
    inputs = Inputs(tab_ref, tok_ref, w_refs, *scratch)

    def block_out(k):
        return pltpu.make_async_copy(
            out.at[k], grads_ref.at[:, inputs.columns(k)], out_sem.at[k]
        )

    inverse, moment, cot = inv_ref[...], moment_ref[...], cot_ref[...]
    for k in range(inputs.count):
        inputs.wait(k)
        partial = lax.dot_general(
            cot, inputs.weight[k], (((1,), (1,)), ((), ())), preferred_element_type=jnp.float32
        )
        wide = inputs.block[k].astype(jnp.float32)
        grads = inverse * gain_ref[:, inputs.columns(k)] * partial - wide * moment
        out[k] = grads.astype(jnp.bfloat16)
        block_out(k).start()
    for k in range(inputs.count):
        block_out(k).wait()


def in_hbm(*arrays):
    return [pltpu.with_memory_space_constraint(array, pltpu.HBM) for array in arrays]


def costs(tokens, columns):
    rows, width = tokens.shape
    return dict(
        compiler_params=pltpu.CompilerParams(vmem_limit_bytes=LIMIT),
        cost_estimate=pl.CostEstimate(
            flops=rows * width * columns,
            bytes_accessed=2 * rows * width + width * columns,
            transcendentals=0,
        ),
    )


def forward(tokens, inverse, gain, weights, table):
    rows, span, columns = tokens.shape[0], *weights[0].shape[1:]
    return pl.pallas_call(
        forward_kernel,
        in_specs=[SMEM, HBM] + [VMEM] * 2 + [HBM] * len(weights),
        out_specs=VMEM,
        out_shape=jax.ShapeDtypeStruct((rows, columns), jnp.float32),
        scratch_shapes=Inputs.scratch(rows, span, columns, table.shape[0]),
        **costs(tokens, columns),
    )(table, *in_hbm(tokens), inverse, gain, *in_hbm(*weights))


def forward_last(tokens, inverse, gain, cotangent, weights, sums, table):
    rows, span, columns = tokens.shape[0], *weights[0].shape[1:]
    return pl.pallas_call(
        forward_last_kernel,
        in_specs=[SMEM, HBM] + [VMEM] * 4 + [HBM] * len(weights),
        out_specs=[VMEM] * 2,
        out_shape=[
            jax.ShapeDtypeStruct((rows, columns), jnp.bfloat16),
            jax.ShapeDtypeStruct((rows, 1), jnp.float32),
        ],
        scratch_shapes=[pltpu.VMEM((rows, columns), jnp.float32)]
        + Inputs.scratch(rows, span, columns, table.shape[0]),
        **costs(tokens, columns),
    )(table, *in_hbm(tokens), inverse, gain, cotangent, sums, *in_hbm(*weights))


def backward(tokens, inverse, gain, cotangent, moment, weights, table, before=()):
    rows, span, columns = tokens.shape[0], *weights[0].shape[1:]
    count = table.shape[0]
    return pl.pallas_call(
        functools.partial(backward_kernel, count=len(weights)),
        in_specs=[SMEM, HBM] + [VMEM] * 4 + [HBM] * (len(weights) + len(before)),
        out_specs=HBM,
        out_shape=jax.ShapeDtypeStruct(tokens.shape, jnp.bfloat16),
        scratch_shapes=[
            pltpu.VMEM((count, rows, span), jnp.bfloat16),
            pltpu.SemaphoreType.DMA((count,)),
        ]
        + Inputs.scratch(rows, span, columns, count),
        input_output_aliases={6 + len(weights): 0} if before else {},
        **costs(tokens, columns),
    )(table, *in_hbm(tokens), inverse, gain, cotangent, moment, *in_hbm(*weights, *before))


def swap(array, axis):
    last = lax.axis_size(axis) - 1
    return lax.ppermute(array, axis, [(a, last - a) for a in range(last + 1)])


def pair(array, axis, step):
    size = lax.axis_size(axis)
    masks = (1, 3) if step == 0 else (3, 1)
    moves = [(a * 2 + c, (a ^ masks[c]) * 2 + c) for a in range(size) for c in range(2)]
    return lax.ppermute(array, (axis, "c"), moves)


def across(array, axis):
    size = lax.axis_size(axis)
    return lax.ppermute(array, axis, [(a, a ^ 2) for a in range(size)])


def pair_z(array):
    size = lax.axis_size("zh") * lax.axis_size("zl")
    moves = []
    for z in range(size):
        moves.append((z * 2, (z ^ 1) * 2))
        moves.append((z * 2 + 1, (z + (1 if z % 2 else -1)) % size * 2 + 1))
    return lax.ppermute(array, ("zh", "zl", "c"), moves)


def add(kept, got):
    return kept + got.astype(jnp.float32)


def add_halves(kept, got):
    half = kept.shape[0] // 2
    return add(kept[half:], got[half:]).astype(jnp.bfloat16), add(kept[:half], got[:half])


def tie(first, *others):
    return lax.optimization_barrier((first, *others))[0]


BASE, ABOVE = (((z, 0, 0), (z, 0, 1)) for z in (0, 1))
NEAR, ABOVE_NEAR = (((z, 1, 0), (z, 1, 1)) for z in (0, 1))
NEAR_C, ABOVE_NEAR_C = (((z, 2, 1), (z, 2, 0)) for z in (0, 1))
FAR, ABOVE_FAR = (((z, 3, 0),) for z in (0, 1))
FAR_C, ABOVE_FAR_C = (((z, 3, 1),) for z in (0, 1))


def write_ends(out_ref, rows):
    high = rows.astype(jnp.bfloat16).astype(jnp.float32)
    out_ref[-2 * EXTRA :, :] = jnp.concatenate([high, rows - high]).astype(jnp.bfloat16)


def read_ends(ref):
    ends = ref[-2 * EXTRA :, :].astype(jnp.float32)
    return ends[:EXTRA] + ends[EXTRA:]


def spread_kernel(tab_ref, total_ref, gain_ref, base_ref, near_ref, near_c_ref, far_ref, *refs, devices):
    out_refs, (rows_ref, weight, sem) = refs[:4], refs[4:]
    columns = base_ref.shape[2]
    rows = pl.ds(pl.multiple_of(tab_ref[4] * TILE, TILE), TILE)
    copies = [
        pltpu.make_async_copy(shard.at[rows], weight.at[k], sem.at[k])
        for k, shard in enumerate((base_ref.at[0], near_c_ref.at[1], near_ref.at[0], far_ref.at[0]))
    ]
    for copy in copies:
        copy.start()
    rows_ref[...] = jnp.zeros_like(rows_ref)
    for k in range(4):
        out_refs[k][:columns, :] = total_ref[k].reshape(columns, TILE).astype(jnp.bfloat16)
    for k in range(4):
        copies[k].wait()
        total = total_ref[k].reshape(columns, TILE)
        part = jnp.sum(weight[k].astype(jnp.float32).T * total, axis=0, keepdims=True)
        gain = gain_ref[:, pl.ds(pl.multiple_of(tab_ref[k] * TILE, TILE), TILE)]
        rows_ref[pl.ds(tab_ref[5 + k], 1), :] = part / (gain * devices)
    for out_ref in out_refs:
        write_ends(out_ref, rows_ref[...])


def spread(total, gain, base, near, near_c, far, table, devices):
    columns = base.shape[2]
    return pl.pallas_call(
        functools.partial(spread_kernel, devices=devices),
        in_specs=[SMEM] + [VMEM] * 2 + [HBM] * 4,
        out_specs=[VMEM] * 4,
        out_shape=[jax.ShapeDtypeStruct((columns + 2 * EXTRA, TILE), jnp.bfloat16)] * 4,
        scratch_shapes=[
            pltpu.VMEM((EXTRA, TILE), jnp.float32),
            pltpu.VMEM((4, TILE, columns), jnp.bfloat16),
            pltpu.SemaphoreType.DMA((4,)),
        ],
        compiler_params=pltpu.CompilerParams(vmem_limit_bytes=LIMIT),
    )(table, total, gain, *in_hbm(base, near, near_c, far))


def in_pairs(terms):
    while len(terms) > 1:
        terms = [a + b for a, b in zip(terms[::2], terms[1::2])]
    return terms[0]


def merge_kernel(*refs, scale):
    parts, out_ref = refs[:-1], refs[-1]
    columns = out_ref.shape[0] - 2 * EXTRA
    total = in_pairs([part[:columns, :].astype(jnp.float32) for part in parts])
    out_ref[:columns, :] = (total * scale).astype(jnp.bfloat16)
    write_ends(out_ref, in_pairs([read_ends(part) for part in parts]))


def merge(parts, scale=1.0):
    return pl.pallas_call(
        functools.partial(merge_kernel, scale=scale),
        in_specs=[VMEM] * len(parts),
        out_specs=VMEM,
        out_shape=jax.ShapeDtypeStruct(parts[0].shape, parts[0].dtype),
        compiler_params=pltpu.CompilerParams(vmem_limit_bytes=SMALL),
    )(*parts)


def finish_kernel(tab_ref, *refs):
    parts, (weight_ref, gain_ref) = refs[:4], refs[4:]
    columns = weight_ref.shape[1]
    for k, part in enumerate(parts):
        rows = pl.ds(pl.multiple_of(tab_ref[k] * TILE, TILE), TILE)
        weight_ref[rows, :] = part[:columns, :].astype(jnp.float32).T
        gain_ref[tab_ref[k]] = read_ends(part)


def finish(parts, table):
    columns = parts[0].shape[0] - 2 * EXTRA
    return pl.pallas_call(
        finish_kernel,
        in_specs=[SMEM] + [VMEM] * 4,
        out_specs=[VMEM] * 2,
        out_shape=[
            jax.ShapeDtypeStruct((4 * TILE, columns), jnp.float32),
            jax.ShapeDtypeStruct((4, EXTRA, TILE), jnp.float32),
        ],
        compiler_params=pltpu.CompilerParams(vmem_limit_bytes=SMALL),
    )(table, *parts)


def order_kernel(tab_ref, *refs):
    parts, out_ref = refs[:4], refs[4]
    for k, part in enumerate(parts):
        for x in range(4):
            for y in range(4):
                out_ref[tab_ref[k] + 2 * x, y : y + 1, :] = part[y, x : x + 1, :]


def order(parts, table):
    return pl.pallas_call(
        order_kernel,
        in_specs=[SMEM] + [VMEM] * 4,
        out_specs=VMEM,
        out_shape=jax.ShapeDtypeStruct((16, 4, TILE), jnp.float32),
        compiler_params=pltpu.CompilerParams(vmem_limit_bytes=SMALL),
    )(table, *parts)


def shards(tokens, norm_gain, weight_values, weight_scale, key_cotangent):
    y, zl, x, c = (lax.axis_index(a) for a in ("y", "zl", "x", "c"))
    width = tokens.shape[1]
    columns = weight_values.shape[1]
    gain = norm_gain.reshape(1, width)
    devices = 1
    for axis in EVERY:
        devices *= lax.axis_size(axis)

    def offset(core, first, second):
        masks = (1 + 2 * core, 3 - 2 * core)
        return first * masks[0] ^ second * masks[1]

    label = jnp.arange(32, dtype=jnp.int32)
    bits = [label // 16] + [label // k % 2 for k in (8, 4, 2, 1)]
    tables = []
    for core in (c, 1 - c):
        chip = (zl ^ bits[0]) * 4 + (x ^ offset(core, bits[3], bits[4]))
        tables.append((chip * 2 + core) * 4 + (y ^ offset(core, bits[1], bits[2])))

    def nodes_of(pieces):
        at = [((zl ^ z) * 4 + (x ^ offset(c, k % 2, k // 2))) * 2 + (c ^ lane) for z, k, lane in pieces]
        return jnp.stack(at).astype(jnp.int32)

    own = widen_weight(weight_values, weight_scale)
    own_c = swap(own, "c")
    up = pair_z(own)
    cot_own = key_cotangent.T
    base = jnp.stack([own, own_c])
    cot_got = swap(cot_own, "c")
    mine, other, inverse = norm_tiles(tokens, gain, tie(jnp.stack(tables), base, cot_own))
    got = swap(other, "c")
    near = pair(base, "x", 0)

    first, kept_first = grad_tiles(mine, got, cot_own, cot_got, 0)
    mine, up, first = lax.optimization_barrier((mine, up, first))
    second, kept_second = grad_tiles(mine, got, cot_own, cot_got, 1)
    moved = [pair(first, "y", 0), pair_z(second)]
    above = jnp.stack([up, swap(up, "c")])
    above_near = pair(above, "x", 0)
    (first, kept_first), (second, kept_second) = map(
        add_halves, (kept_first, kept_second), moved
    )

    first, near = lax.optimization_barrier((first, near))
    moved = [pair_z(first), pair(second, "y", 0)]
    near_c = swap(near, "c")
    far = pair(near_c[1:], "x", 0)
    early = [base, above, near, near_c]
    sums = forward(tokens, inverse, gain, early, nodes_of(BASE + ABOVE + NEAR + NEAR_C))
    moved[1], sums, above_near, far = lax.optimization_barrier((moved[1], sums, above_near, far))
    (first, kept_first), (second, kept_second) = map(
        add_halves, (kept_first, kept_second), moved
    )

    send, above_near, far = lax.optimization_barrier((jnp.stack([first, second]), above_near, far))
    moved = pair(send, "y", 1)
    above_near_c = swap(above_near, "c")
    above_far = pair(above_near_c[1:], "x", 0)
    far_c = swap(far, "c")
    moved, far_c, above_near_c = lax.optimization_barrier((moved, far_c, above_near_c))
    total = jnp.stack([add(kept_first, moved[0]), add(kept_second, moved[1])], axis=1)

    peer = x ^ offset(c, jnp.arange(4) // 2, jnp.arange(4) % 2)
    node_tile = ((zl * 4 + peer) * 2 + c) * 4 + y
    at = jnp.concatenate([node_tile, y[None], peer]).astype(jnp.int32)
    parts = list(spread(total, gain, base, near, near_c, far, at, devices))
    parts[0], above_far = lax.optimization_barrier((parts[0], above_far))
    moved = [parts[0], pair(parts[2], "x", 0), pair(parts[1], "x", 1), across(parts[3], "x")]
    above_far_c = swap(above_far, "c")
    late = [above_near, above_near_c, far, above_far, far_c, above_far_c]
    late_at = nodes_of(ABOVE_NEAR + ABOVE_NEAR_C + FAR + ABOVE_FAR + FAR_C + ABOVE_FAR_C)
    projected, moment = forward_last(tokens, inverse, gain, key_cotangent, late, sums, late_at)
    moved[3], moment = lax.optimization_barrier((moved[3], moment))
    send = merge(moved)

    def part_of_grads(before, weights, pieces):
        return backward(
            tokens, inverse, gain, key_cotangent, moment, weights, nodes_of(pieces), before
        )

    send, moment = lax.optimization_barrier((send, moment))
    moved = pair(send, "zh", 0)
    token_grads = part_of_grads((), [base, above, near], BASE + ABOVE + NEAR)
    moved, token_grads = lax.optimization_barrier((moved, token_grads))
    send = merge((send, moved))
    send, token_grads = lax.optimization_barrier((send, token_grads))
    moved = pair(send, "zh", 1)
    token_grads = part_of_grads(
        (token_grads,), [near_c, above_near, far], NEAR_C + ABOVE_NEAR + FAR
    )
    moved, token_grads = lax.optimization_barrier((moved, token_grads))
    send = merge((send, moved), 1.0 / devices)

    parts = (send, pair(send, "y", 0), pair(send, "y", 1), across(send, "y"))
    quarters = jnp.stack([y ^ offset(c, k % 2, k // 2) for k in range(4)]).astype(jnp.int32)
    token_grads = part_of_grads(
        (tie(token_grads, send),),
        [above_near_c, above_far, far_c, above_far_c],
        ABOVE_NEAR_C + ABOVE_FAR + FAR_C + ABOVE_FAR_C,
    )
    parts, token_grads = lax.optimization_barrier((parts, token_grads))
    weight_grads, gains = finish(parts, quarters)
    gains = (gains, swap(gains, "c"), swap(gains, "zl"), swap(gains, ("zl", "c")))
    nodes = jnp.stack([(zl ^ k // 2) * 8 + (c ^ k % 2) for k in range(4)]).astype(jnp.int32)
    gain_grads = order(gains, nodes).reshape(width)
    return (projected, token_grads, weight_grads, gain_grads)


def solution(mesh):
    fine = Mesh(mesh.devices.reshape(4, 4, 2, 4, 2), EVERY)
    rows = P(EVERY, None)
    return jax.shard_map(
        shards,
        mesh=fine,
        in_specs=(rows, P(), P(NODE, None), P(NODE, None), rows),
        out_specs=(rows, rows, P(NODE, None), P()),
        check_vma=False,
    )
```

```python
import functools

import jax
import jax.numpy as jnp
from jax import lax
from jax.experimental import pallas as pl
from jax.experimental.pallas import tpu as pltpu
from jax.sharding import Mesh, PartitionSpec as P

NODE = ("zl", "x", "c")
EVERY = ("y", "zh", "zl", "x", "c")
TILE = 128
EXTRA = 8
LIMIT = 16 * 2**20
SMALL = 8 * 2**20
QUICK = pl.CostEstimate(flops=1, bytes_accessed=1, transcendentals=0)
VMEM = pl.BlockSpec(memory_space=pltpu.VMEM)
SMEM = pl.BlockSpec(memory_space=pltpu.SMEM)
HBM = pl.BlockSpec(memory_space=pltpu.HBM)


def widen_kernel(values_ref, scales_ref, out_ref):
    blocks = scales_ref.shape[0]
    block = values_ref.shape[1] // blocks
    scales = scales_ref[...].astype(jnp.float32)
    scales = jnp.concatenate([scales] * (8 // blocks), axis=0).T
    for k in range(blocks):
        part = slice(k * block, (k + 1) * block)
        wide = values_ref[:, part].astype(jnp.float32)
        out_ref[:, part] = (wide * scales[:, k : k + 1]).astype(jnp.bfloat16)


def widen_weight(values, scales):
    return pl.pallas_call(
        widen_kernel,
        out_shape=jax.ShapeDtypeStruct(values.shape, jnp.bfloat16),
        compiler_params=pltpu.CompilerParams(vmem_limit_bytes=SMALL),
    )(values, scales.T)


def norm_kernel(tab_ref, tok_ref, gain_ref, own_ref, oth_ref, inv_ref, block, sem):
    count, rows, width = block.shape

    def block_in(k):
        return pltpu.make_async_copy(tok_ref.at[pl.ds(k * rows, rows)], block.at[k], sem.at[k])

    for k in range(count):
        block_in(k).start()
    for k in range(count):
        block_in(k).wait()
        part = slice(k * rows, (k + 1) * rows)
        total = jnp.zeros((rows, TILE), jnp.float32)
        for t in range(width // TILE):
            wide = block[k, :, t * TILE : (t + 1) * TILE].astype(jnp.float32)
            total = total + wide * wide
        mean = jnp.sum(total, axis=1, keepdims=True) / width
        inverse = lax.rsqrt(mean + 1e-05)
        inv_ref[part, :] = inverse
        for side, out_ref in enumerate((own_ref, oth_ref)):
            for r in range(width // TILE // 2):
                at = pl.multiple_of(tab_ref[side, r] * TILE, TILE)
                wide = block[k, :, pl.ds(at, TILE)].astype(jnp.float32)
                scaled = wide * inverse * gain_ref[:, pl.ds(at, TILE)]
                out_ref[part, r * TILE : (r + 1) * TILE] = scaled.astype(jnp.bfloat16)


def norm_tiles(tokens, gain, table):
    rows, width = tokens.shape
    step = 64 if rows % 64 == 0 else rows
    return pl.pallas_call(
        norm_kernel,
        in_specs=[SMEM, HBM, VMEM],
        out_specs=[VMEM] * 3,
        out_shape=[
            jax.ShapeDtypeStruct((rows, width // 2), jnp.bfloat16),
            jax.ShapeDtypeStruct((rows, width // 2), jnp.bfloat16),
            jax.ShapeDtypeStruct((rows, 1), jnp.float32),
        ],
        scratch_shapes=[
            pltpu.VMEM((rows // step, step, width), jnp.bfloat16),
            pltpu.SemaphoreType.DMA((rows // step,)),
        ],
        compiler_params=pltpu.CompilerParams(vmem_limit_bytes=LIMIT),
        cost_estimate=QUICK,
    )(table, *in_hbm(tokens), gain)


def grad_kernel(own_ref, got_ref, cot_own_ref, cot_got_ref, sent_ref, kept_ref, *, side):
    span = 2 * TILE
    half = cot_own_ref.shape[0] // 2
    rows = slice(side * half, (side + 1) * half)
    cot_own = cot_own_ref[rows, :]
    cot_got = cot_got_ref[rows, :]
    for pair in range(own_ref.shape[1] // span):
        part = slice(pair * span, (pair + 1) * span)
        grads = jnp.dot(cot_own, own_ref[:, part], preferred_element_type=jnp.float32)
        grads += jnp.dot(cot_got, got_ref[:, part], preferred_element_type=jnp.float32)
        for which in range(2):
            tile = pair * 2 + which
            z, y1, rest = tile // 16, tile // 8 % 2, tile % 8
            sent, at = ((y1, z * 8 + rest), (z, y1 * 8 + rest))[side]
            piece = grads[:, which * TILE : (which + 1) * TILE]
            if sent:
                sent_ref[at] = piece.astype(jnp.bfloat16)
            else:
                kept_ref[at] = piece


def grad_tiles(own, got, cot_own, cot_got, side):
    width = own.shape[1]
    shape = (width // TILE // 2, cot_own.shape[0] // 2, TILE)
    return pl.pallas_call(
        functools.partial(grad_kernel, side=side),
        out_shape=[
            jax.ShapeDtypeStruct(shape, jnp.bfloat16),
            jax.ShapeDtypeStruct(shape, jnp.float32),
        ],
        compiler_params=pltpu.CompilerParams(vmem_limit_bytes=LIMIT),
        cost_estimate=QUICK,
    )(own, got, cot_own, cot_got)


class Inputs:
    def __init__(self, tab_ref, tok_ref, w_refs, block, weight, sem, weight_sem):
        shards_ = [ref.at[k] for ref in w_refs for k in range(ref.shape[0])]
        self.count, _, self.span = block.shape
        self.tab_ref, self.block, self.weight = tab_ref, block, weight
        self.copies = []
        for k in range(self.count):
            self.copies.append(
                (
                    pltpu.make_async_copy(tok_ref.at[:, self.columns(k)], block.at[k], sem.at[k]),
                    pltpu.make_async_copy(shards_[k], weight.at[k], weight_sem.at[k]),
                )
            )
        for pair_ in self.copies:
            for copy in pair_:
                copy.start()

    def columns(self, k):
        return pl.ds(pl.multiple_of(self.tab_ref[k] * self.span, self.span), self.span)

    def wait(self, k):
        for copy in self.copies[k]:
            copy.wait()

    @staticmethod
    def scratch(rows, span, columns, count):
        return [
            pltpu.VMEM((count, rows, span), jnp.bfloat16),
            pltpu.VMEM((count, span, columns), jnp.bfloat16),
            pltpu.SemaphoreType.DMA((count,)),
            pltpu.SemaphoreType.DMA((count,)),
        ]


def forward_steps(inputs, inv_ref, gain_ref, acc):
    inverse = inv_ref[...]
    for k in range(inputs.count):
        inputs.wait(k)
        wide = inputs.block[k].astype(jnp.float32)
        normed = (wide * inverse * gain_ref[:, inputs.columns(k)]).astype(jnp.bfloat16)
        acc[...] += jnp.dot(normed, inputs.weight[k], preferred_element_type=jnp.float32)


def forward_kernel(tab_ref, tok_ref, inv_ref, gain_ref, *refs):
    w_refs, (acc, *scratch) = refs[:-5], refs[-5:]
    inputs = Inputs(tab_ref, tok_ref, w_refs, *scratch)
    acc[...] = jnp.zeros_like(acc)
    forward_steps(inputs, inv_ref, gain_ref, acc)


def forward_last_kernel(tab_ref, tok_ref, inv_ref, gain_ref, cot_ref, acc_in, *refs):
    w_refs, (proj_ref, moment_ref, acc, *scratch) = refs[:-7], refs[-7:]
    inputs = Inputs(tab_ref, tok_ref, w_refs, *scratch)
    acc[...] = acc_in[...]
    forward_steps(inputs, inv_ref, gain_ref, acc)
    keys = acc[...]
    inverse = inv_ref[...]
    proj_ref[...] = keys.astype(jnp.bfloat16)
    inner = jnp.sum(cot_ref[...].astype(jnp.float32) * keys, axis=1, keepdims=True)
    moment_ref[...] = inverse * inverse * inner / tok_ref.shape[1]


def backward_kernel(tab_ref, tok_ref, inv_ref, gain_ref, cot_ref, moment_ref, *refs, count):
    w_refs, (grads_ref, out, out_sem, *scratch) = refs[:count], refs[-7:]
    inputs = Inputs(tab_ref, tok_ref, w_refs, *scratch)

    def block_out(k):
        return pltpu.make_async_copy(
            out.at[k], grads_ref.at[:, inputs.columns(k)], out_sem.at[k]
        )

    inverse, moment, cot = inv_ref[...], moment_ref[...], cot_ref[...]
    for k in range(inputs.count):
        inputs.wait(k)
        partial = lax.dot_general(
            cot, inputs.weight[k], (((1,), (1,)), ((), ())), preferred_element_type=jnp.float32
        )
        wide = inputs.block[k].astype(jnp.float32)
        grads = inverse * gain_ref[:, inputs.columns(k)] * partial - wide * moment
        out[k] = grads.astype(jnp.bfloat16)
        block_out(k).start()
    for k in range(inputs.count):
        block_out(k).wait()


def in_hbm(*arrays):
    return [pltpu.with_memory_space_constraint(array, pltpu.HBM) for array in arrays]


def costs(tokens, columns):
    rows, width = tokens.shape
    return dict(
        compiler_params=pltpu.CompilerParams(vmem_limit_bytes=LIMIT),
        cost_estimate=pl.CostEstimate(
            flops=rows * width * columns,
            bytes_accessed=2 * rows * width + width * columns,
            transcendentals=0,
        ),
    )


def forward(tokens, inverse, gain, weights, table):
    rows, span, columns = tokens.shape[0], *weights[0].shape[1:]
    return pl.pallas_call(
        forward_kernel,
        in_specs=[SMEM, HBM] + [VMEM] * 2 + [HBM] * len(weights),
        out_specs=VMEM,
        out_shape=jax.ShapeDtypeStruct((rows, columns), jnp.float32),
        scratch_shapes=Inputs.scratch(rows, span, columns, table.shape[0]),
        **costs(tokens, columns),
    )(table, *in_hbm(tokens), inverse, gain, *in_hbm(*weights))


def forward_last(tokens, inverse, gain, cotangent, weights, sums, table):
    rows, span, columns = tokens.shape[0], *weights[0].shape[1:]
    return pl.pallas_call(
        forward_last_kernel,
        in_specs=[SMEM, HBM] + [VMEM] * 4 + [HBM] * len(weights),
        out_specs=[VMEM] * 2,
        out_shape=[
            jax.ShapeDtypeStruct((rows, columns), jnp.bfloat16),
            jax.ShapeDtypeStruct((rows, 1), jnp.float32),
        ],
        scratch_shapes=[pltpu.VMEM((rows, columns), jnp.float32)]
        + Inputs.scratch(rows, span, columns, table.shape[0]),
        **costs(tokens, columns),
    )(table, *in_hbm(tokens), inverse, gain, cotangent, sums, *in_hbm(*weights))


def backward(tokens, inverse, gain, cotangent, moment, weights, table, before=()):
    rows, span, columns = tokens.shape[0], *weights[0].shape[1:]
    count = table.shape[0]
    return pl.pallas_call(
        functools.partial(backward_kernel, count=len(weights)),
        in_specs=[SMEM, HBM] + [VMEM] * 4 + [HBM] * (len(weights) + len(before)),
        out_specs=HBM,
        out_shape=jax.ShapeDtypeStruct(tokens.shape, jnp.bfloat16),
        scratch_shapes=[
            pltpu.VMEM((count, rows, span), jnp.bfloat16),
            pltpu.SemaphoreType.DMA((count,)),
        ]
        + Inputs.scratch(rows, span, columns, count),
        input_output_aliases={6 + len(weights): 0} if before else {},
        **costs(tokens, columns),
    )(table, *in_hbm(tokens), inverse, gain, cotangent, moment, *in_hbm(*weights, *before))


def swap(array, axis):
    last = lax.axis_size(axis) - 1
    return lax.ppermute(array, axis, [(a, last - a) for a in range(last + 1)])


def pair(array, axis, step):
    size = lax.axis_size(axis)
    masks = (1, 3) if step == 0 else (3, 1)
    moves = [(a * 2 + c, (a ^ masks[c]) * 2 + c) for a in range(size) for c in range(2)]
    return lax.ppermute(array, (axis, "c"), moves)


def across(array, axis):
    size = lax.axis_size(axis)
    return lax.ppermute(array, axis, [(a, a ^ 2) for a in range(size)])


def pair_z(array):
    size = lax.axis_size("zh") * lax.axis_size("zl")
    moves = []
    for z in range(size):
        moves.append((z * 2, (z ^ 1) * 2))
        moves.append((z * 2 + 1, (z + (1 if z % 2 else -1)) % size * 2 + 1))
    return lax.ppermute(array, ("zh", "zl", "c"), moves)


def add(kept, got):
    return kept + got.astype(jnp.float32)


def add_halves(kept, got):
    half = kept.shape[0] // 2
    return add(kept[half:], got[half:]).astype(jnp.bfloat16), add(kept[:half], got[:half])


def tie(first, *others):
    return lax.optimization_barrier((first, *others))[0]


BASE, ABOVE = (((z, 0, 0), (z, 0, 1)) for z in (0, 1))
NEAR, ABOVE_NEAR = (((z, 1, 0), (z, 1, 1)) for z in (0, 1))
NEAR_C, ABOVE_NEAR_C = (((z, 2, 1), (z, 2, 0)) for z in (0, 1))
FAR, ABOVE_FAR = (((z, 3, 0),) for z in (0, 1))
FAR_C, ABOVE_FAR_C = (((z, 3, 1),) for z in (0, 1))


def write_ends(out_ref, rows):
    high = rows.astype(jnp.bfloat16).astype(jnp.float32)
    out_ref[-2 * EXTRA :, :] = jnp.concatenate([high, rows - high]).astype(jnp.bfloat16)


def read_ends(ref):
    ends = ref[-2 * EXTRA :, :].astype(jnp.float32)
    return ends[:EXTRA] + ends[EXTRA:]


def spread_kernel(tab_ref, total_ref, gain_ref, base_ref, near_ref, near_c_ref, far_ref, *refs, devices):
    out_refs, (rows_ref, weight, sem) = refs[:4], refs[4:]
    columns = base_ref.shape[2]
    rows = pl.ds(pl.multiple_of(tab_ref[4] * TILE, TILE), TILE)
    copies = [
        pltpu.make_async_copy(shard.at[rows], weight.at[k], sem.at[k])
        for k, shard in enumerate((base_ref.at[0], near_c_ref.at[1], near_ref.at[0], far_ref.at[0]))
    ]
    for copy in copies:
        copy.start()
    rows_ref[...] = jnp.zeros_like(rows_ref)
    for k in range(4):
        out_refs[k][:columns, :] = total_ref[k].reshape(columns, TILE).astype(jnp.bfloat16)
    for k in range(4):
        copies[k].wait()
        total = total_ref[k].reshape(columns, TILE)
        part = jnp.sum(weight[k].astype(jnp.float32).T * total, axis=0, keepdims=True)
        gain = gain_ref[:, pl.ds(pl.multiple_of(tab_ref[k] * TILE, TILE), TILE)]
        rows_ref[pl.ds(tab_ref[5 + k], 1), :] = part / (gain * devices)
    for out_ref in out_refs:
        write_ends(out_ref, rows_ref[...])


def spread(total, gain, base, near, near_c, far, table, devices):
    columns = base.shape[2]
    return pl.pallas_call(
        functools.partial(spread_kernel, devices=devices),
        in_specs=[SMEM] + [VMEM] * 2 + [HBM] * 4,
        out_specs=[VMEM] * 4,
        out_shape=[jax.ShapeDtypeStruct((columns + 2 * EXTRA, TILE), jnp.bfloat16)] * 4,
        scratch_shapes=[
            pltpu.VMEM((EXTRA, TILE), jnp.float32),
            pltpu.VMEM((4, TILE, columns), jnp.bfloat16),
            pltpu.SemaphoreType.DMA((4,)),
        ],
        compiler_params=pltpu.CompilerParams(vmem_limit_bytes=LIMIT),
    )(table, total, gain, *in_hbm(base, near, near_c, far))


def in_pairs(terms):
    while len(terms) > 1:
        terms = [a + b for a, b in zip(terms[::2], terms[1::2])]
    return terms[0]


def merge_kernel(*refs, scale):
    parts, out_ref = refs[:-1], refs[-1]
    columns = out_ref.shape[0] - 2 * EXTRA
    total = in_pairs([part[:columns, :].astype(jnp.float32) for part in parts])
    out_ref[:columns, :] = (total * scale).astype(jnp.bfloat16)
    write_ends(out_ref, in_pairs([read_ends(part) for part in parts]))


def merge(parts, scale=1.0):
    return pl.pallas_call(
        functools.partial(merge_kernel, scale=scale),
        in_specs=[VMEM] * len(parts),
        out_specs=VMEM,
        out_shape=jax.ShapeDtypeStruct(parts[0].shape, parts[0].dtype),
        compiler_params=pltpu.CompilerParams(vmem_limit_bytes=SMALL),
    )(*parts)


def finish_kernel(tab_ref, *refs):
    parts, (weight_ref, gain_ref) = refs[:4], refs[4:]
    columns = weight_ref.shape[1]
    for k, part in enumerate(parts):
        rows = pl.ds(pl.multiple_of(tab_ref[k] * TILE, TILE), TILE)
        weight_ref[rows, :] = part[:columns, :].astype(jnp.float32).T
        gain_ref[tab_ref[k]] = read_ends(part)


def finish(parts, table):
    columns = parts[0].shape[0] - 2 * EXTRA
    return pl.pallas_call(
        finish_kernel,
        in_specs=[SMEM] + [VMEM] * 4,
        out_specs=[VMEM] * 2,
        out_shape=[
            jax.ShapeDtypeStruct((4 * TILE, columns), jnp.float32),
            jax.ShapeDtypeStruct((4, EXTRA, TILE), jnp.float32),
        ],
        compiler_params=pltpu.CompilerParams(vmem_limit_bytes=SMALL),
    )(table, *parts)


def order_kernel(tab_ref, *refs):
    parts, out_ref = refs[:4], refs[4]
    for k, part in enumerate(parts):
        for x in range(4):
            for y in range(4):
                out_ref[tab_ref[k] + 2 * x, y : y + 1, :] = part[y, x : x + 1, :]


def order(parts, table):
    return pl.pallas_call(
        order_kernel,
        in_specs=[SMEM] + [VMEM] * 4,
        out_specs=VMEM,
        out_shape=jax.ShapeDtypeStruct((16, 4, TILE), jnp.float32),
        compiler_params=pltpu.CompilerParams(vmem_limit_bytes=SMALL),
    )(table, *parts)


def shards(tokens, norm_gain, weight_values, weight_scale, key_cotangent):
    y, zl, x, c = (lax.axis_index(a) for a in ("y", "zl", "x", "c"))
    width = tokens.shape[1]
    columns = weight_values.shape[1]
    gain = norm_gain.reshape(1, width)
    devices = 1
    for axis in EVERY:
        devices *= lax.axis_size(axis)

    def offset(core, first, second):
        masks = (1 + 2 * core, 3 - 2 * core)
        return first * masks[0] ^ second * masks[1]

    label = jnp.arange(32, dtype=jnp.int32)
    bits = [label // 16] + [label // k % 2 for k in (8, 4, 2, 1)]
    tables = []
    for core in (c, 1 - c):
        chip = (zl ^ bits[0]) * 4 + (x ^ offset(core, bits[3], bits[4]))
        tables.append((chip * 2 + core) * 4 + (y ^ offset(core, bits[1], bits[2])))

    def nodes_of(pieces):
        at = [((zl ^ z) * 4 + (x ^ offset(c, k % 2, k // 2))) * 2 + (c ^ lane) for z, k, lane in pieces]
        return jnp.stack(at).astype(jnp.int32)

    mine, other, inverse = norm_tiles(tokens, gain, jnp.stack(tables))
    got = swap(other, "c")

    own = widen_weight(tie(weight_values, inverse), weight_scale)
    own_c = swap(own, "c")
    up = pair_z(own)
    cot_own = tie(key_cotangent, inverse).T
    base = jnp.stack([own, own_c])
    cot_got = swap(cot_own, "c")
    near = pair(base, "x", 0)

    first, kept_first = grad_tiles(mine, got, cot_own, cot_got, 0)
    mine, up, first = lax.optimization_barrier((mine, up, first))
    second, kept_second = grad_tiles(mine, got, cot_own, cot_got, 1)
    moved = [pair(first, "y", 0), pair_z(second)]
    above = jnp.stack([up, swap(up, "c")])
    above_near = pair(above, "x", 0)
    (first, kept_first), (second, kept_second) = map(
        add_halves, (kept_first, kept_second), moved
    )

    first, near = lax.optimization_barrier((first, near))
    moved = [pair_z(first), pair(second, "y", 0)]
    near_c = swap(near, "c")
    far = pair(near_c[1:], "x", 0)
    early = [base, above, near, near_c]
    sums = forward(tokens, inverse, gain, early, nodes_of(BASE + ABOVE + NEAR + NEAR_C))
    moved[1], sums, above_near = lax.optimization_barrier((moved[1], sums, above_near))
    (first, kept_first), (second, kept_second) = map(
        add_halves, (kept_first, kept_second), moved
    )

    send, above_near = lax.optimization_barrier((jnp.stack([first, second]), above_near))
    moved = pair(send, "y", 1)
    above_near_c = swap(above_near, "c")
    above_far = pair(above_near_c[1:], "x", 0)
    far_c = swap(far, "c")
    moved, far_c, above_near_c = lax.optimization_barrier((moved, far_c, above_near_c))
    total = jnp.stack([add(kept_first, moved[0]), add(kept_second, moved[1])], axis=1)

    peer = x ^ offset(c, jnp.arange(4) // 2, jnp.arange(4) % 2)
    node_tile = ((zl * 4 + peer) * 2 + c) * 4 + y
    at = jnp.concatenate([node_tile, y[None], peer]).astype(jnp.int32)
    parts = list(spread(total, gain, base, near, near_c, far, at, devices))
    parts[0], above_far = lax.optimization_barrier((parts[0], above_far))
    moved = [parts[0], pair(parts[2], "x", 0), pair(parts[1], "x", 1), across(parts[3], "x")]
    above_far_c = swap(above_far, "c")
    late = [above_near, above_near_c, far, above_far, far_c, above_far_c]
    late_at = nodes_of(ABOVE_NEAR + ABOVE_NEAR_C + FAR + ABOVE_FAR + FAR_C + ABOVE_FAR_C)
    projected, moment = forward_last(tokens, inverse, gain, key_cotangent, late, sums, late_at)
    moved[3], moment = lax.optimization_barrier((moved[3], moment))
    send = merge(moved)

    def part_of_grads(before, weights, pieces):
        return backward(
            tokens, inverse, gain, key_cotangent, moment, weights, nodes_of(pieces), before
        )

    send, moment = lax.optimization_barrier((send, moment))
    moved = pair(send, "zh", 0)
    token_grads = part_of_grads((), [base, above, near], BASE + ABOVE + NEAR)
    moved, token_grads = lax.optimization_barrier((moved, token_grads))
    send = merge((send, moved))
    send, token_grads = lax.optimization_barrier((send, token_grads))
    moved = pair(send, "zh", 1)
    token_grads = part_of_grads(
        (token_grads,), [near_c, above_near, far], NEAR_C + ABOVE_NEAR + FAR
    )
    moved, token_grads = lax.optimization_barrier((moved, token_grads))
    send = merge((send, moved), 1.0 / devices)

    parts = (send, pair(send, "y", 0), pair(send, "y", 1), across(send, "y"))
    quarters = jnp.stack([y ^ offset(c, k % 2, k // 2) for k in range(4)]).astype(jnp.int32)
    token_grads = part_of_grads(
        (tie(token_grads, send),),
        [above_near_c, above_far, far_c, above_far_c],
        ABOVE_NEAR_C + ABOVE_FAR + FAR_C + ABOVE_FAR_C,
    )
    parts, token_grads = lax.optimization_barrier((parts, token_grads))
    weight_grads, gains = finish(parts, quarters)
    gains = (gains, swap(gains, "c"), swap(gains, "zl"), swap(gains, ("zl", "c")))
    nodes = jnp.stack([(zl ^ k // 2) * 8 + (c ^ k % 2) for k in range(4)]).astype(jnp.int32)
    gain_grads = order(gains, nodes).reshape(width)
    return (projected, token_grads, weight_grads, gain_grads)


def solution(mesh):
    fine = Mesh(mesh.devices.reshape(4, 4, 2, 4, 2), EVERY)
    rows = P(EVERY, None)
    return jax.shard_map(
        shards,
        mesh=fine,
        in_specs=(rows, P(), P(NODE, None), P(NODE, None), rows),
        out_specs=(rows, rows, P(NODE, None), P()),
        check_vma=False,
    )
```

```python
import functools

import jax
import jax.numpy as jnp
from jax import lax
from jax.experimental import pallas as pl
from jax.experimental.pallas import tpu as pltpu
from jax.sharding import Mesh, PartitionSpec as P

NODE = ("zl", "x", "c")
EVERY = ("y", "zh", "zl", "x", "c")
TILE = 128
EXTRA = 8
LIMIT = 16 * 2**20
SMALL = 8 * 2**20
QUICK = pl.CostEstimate(flops=1, bytes_accessed=1, transcendentals=0)
VMEM = pl.BlockSpec(memory_space=pltpu.VMEM)
SMEM = pl.BlockSpec(memory_space=pltpu.SMEM)
HBM = pl.BlockSpec(memory_space=pltpu.HBM)


def widen_kernel(values_ref, scales_ref, out_ref):
    blocks = scales_ref.shape[0]
    block = values_ref.shape[1] // blocks
    scales = scales_ref[...].astype(jnp.float32)
    scales = jnp.concatenate([scales] * (8 // blocks), axis=0).T
    for k in range(blocks):
        part = slice(k * block, (k + 1) * block)
        wide = values_ref[:, part].astype(jnp.float32)
        out_ref[:, part] = (wide * scales[:, k : k + 1]).astype(jnp.bfloat16)


def widen_weight(values, scales):
    return pl.pallas_call(
        widen_kernel,
        out_shape=jax.ShapeDtypeStruct(values.shape, jnp.bfloat16),
        compiler_params=pltpu.CompilerParams(vmem_limit_bytes=SMALL),
    )(values, scales.T)


def norm_kernel(tab_ref, tok_ref, gain_ref, own_ref, oth_ref, inv_ref, block, sem):
    count, rows, width = block.shape

    def block_in(k):
        return pltpu.make_async_copy(tok_ref.at[pl.ds(k * rows, rows)], block.at[k], sem.at[k])

    for k in range(count):
        block_in(k).start()
    for k in range(count):
        block_in(k).wait()
        part = slice(k * rows, (k + 1) * rows)
        total = jnp.zeros((rows, TILE), jnp.float32)
        for t in range(width // TILE):
            wide = block[k, :, t * TILE : (t + 1) * TILE].astype(jnp.float32)
            total = total + wide * wide
        mean = jnp.sum(total, axis=1, keepdims=True) / width
        inverse = lax.rsqrt(mean + 1e-05)
        inv_ref[part, :] = inverse
        for side, out_ref in enumerate((own_ref, oth_ref)):
            for r in range(width // TILE // 2):
                at = pl.multiple_of(tab_ref[side, r] * TILE, TILE)
                wide = block[k, :, pl.ds(at, TILE)].astype(jnp.float32)
                scaled = wide * inverse * gain_ref[:, pl.ds(at, TILE)]
                out_ref[part, r * TILE : (r + 1) * TILE] = scaled.astype(jnp.bfloat16)


def norm_tiles(tokens, gain, table):
    rows, width = tokens.shape
    step = 64 if rows % 64 == 0 else rows
    return pl.pallas_call(
        norm_kernel,
        in_specs=[SMEM, HBM, VMEM],
        out_specs=[VMEM] * 3,
        out_shape=[
            jax.ShapeDtypeStruct((rows, width // 2), jnp.bfloat16),
            jax.ShapeDtypeStruct((rows, width // 2), jnp.bfloat16),
            jax.ShapeDtypeStruct((rows, 1), jnp.float32),
        ],
        scratch_shapes=[
            pltpu.VMEM((rows // step, step, width), jnp.bfloat16),
            pltpu.SemaphoreType.DMA((rows // step,)),
        ],
        compiler_params=pltpu.CompilerParams(vmem_limit_bytes=LIMIT),
        cost_estimate=QUICK,
    )(table, *in_hbm(tokens), gain)


def grad_kernel(own_ref, got_ref, cot_own_ref, cot_got_ref, sent_ref, kept_ref, *, side):
    span = 2 * TILE
    half = cot_own_ref.shape[0] // 2
    rows = slice(side * half, (side + 1) * half)
    cot_own = cot_own_ref[rows, :]
    cot_got = cot_got_ref[rows, :]
    for pair in range(own_ref.shape[1] // span):
        part = slice(pair * span, (pair + 1) * span)
        grads = jnp.dot(cot_own, own_ref[:, part], preferred_element_type=jnp.float32)
        grads += jnp.dot(cot_got, got_ref[:, part], preferred_element_type=jnp.float32)
        for which in range(2):
            tile = pair * 2 + which
            z, y1, rest = tile // 16, tile // 8 % 2, tile % 8
            sent, at = ((y1, z * 8 + rest), (z, y1 * 8 + rest))[side]
            piece = grads[:, which * TILE : (which + 1) * TILE]
            if sent:
                sent_ref[at] = piece.astype(jnp.bfloat16)
            else:
                kept_ref[at] = piece


def grad_tiles(own, got, cot_own, cot_got, side):
    width = own.shape[1]
    shape = (width // TILE // 2, cot_own.shape[0] // 2, TILE)
    return pl.pallas_call(
        functools.partial(grad_kernel, side=side),
        out_shape=[
            jax.ShapeDtypeStruct(shape, jnp.bfloat16),
            jax.ShapeDtypeStruct(shape, jnp.float32),
        ],
        compiler_params=pltpu.CompilerParams(vmem_limit_bytes=LIMIT),
        cost_estimate=QUICK,
    )(own, got, cot_own, cot_got)


class Inputs:
    def __init__(self, tab_ref, tok_ref, w_refs, block, weight, sem, weight_sem):
        shards_ = [ref.at[k] for ref in w_refs for k in range(ref.shape[0])]
        self.count, _, self.span = block.shape
        self.tab_ref, self.block, self.weight = tab_ref, block, weight
        self.copies = []
        for k in range(self.count):
            self.copies.append(
                (
                    pltpu.make_async_copy(tok_ref.at[:, self.columns(k)], block.at[k], sem.at[k]),
                    pltpu.make_async_copy(shards_[k], weight.at[k], weight_sem.at[k]),
                )
            )
        for pair_ in self.copies:
            for copy in pair_:
                copy.start()

    def columns(self, k):
        return pl.ds(pl.multiple_of(self.tab_ref[k] * self.span, self.span), self.span)

    def wait(self, k):
        for copy in self.copies[k]:
            copy.wait()

    @staticmethod
    def scratch(rows, span, columns, count):
        return [
            pltpu.VMEM((count, rows, span), jnp.bfloat16),
            pltpu.VMEM((count, span, columns), jnp.bfloat16),
            pltpu.SemaphoreType.DMA((count,)),
            pltpu.SemaphoreType.DMA((count,)),
        ]


def forward_steps(inputs, inv_ref, gain_ref, acc):
    inverse = inv_ref[...]
    for k in range(inputs.count):
        inputs.wait(k)
        wide = inputs.block[k].astype(jnp.float32)
        normed = (wide * inverse * gain_ref[:, inputs.columns(k)]).astype(jnp.bfloat16)
        acc[...] += jnp.dot(normed, inputs.weight[k], preferred_element_type=jnp.float32)


def forward_kernel(tab_ref, tok_ref, inv_ref, gain_ref, *refs):
    w_refs, (acc, *scratch) = refs[:-5], refs[-5:]
    inputs = Inputs(tab_ref, tok_ref, w_refs, *scratch)
    acc[...] = jnp.zeros_like(acc)
    forward_steps(inputs, inv_ref, gain_ref, acc)


def forward_last_kernel(tab_ref, tok_ref, inv_ref, gain_ref, cot_ref, acc_in, *refs):
    w_refs, (proj_ref, moment_ref, acc, *scratch) = refs[:-7], refs[-7:]
    inputs = Inputs(tab_ref, tok_ref, w_refs, *scratch)
    acc[...] = acc_in[...]
    forward_steps(inputs, inv_ref, gain_ref, acc)
    keys = acc[...]
    inverse = inv_ref[...]
    proj_ref[...] = keys.astype(jnp.bfloat16)
    inner = jnp.sum(cot_ref[...].astype(jnp.float32) * keys, axis=1, keepdims=True)
    moment_ref[...] = inverse * inverse * inner / tok_ref.shape[1]


def backward_kernel(tab_ref, tok_ref, inv_ref, gain_ref, cot_ref, moment_ref, *refs, count):
    w_refs, (grads_ref, out, out_sem, *scratch) = refs[:count], refs[-7:]
    inputs = Inputs(tab_ref, tok_ref, w_refs, *scratch)

    def block_out(k):
        return pltpu.make_async_copy(
            out.at[k], grads_ref.at[:, inputs.columns(k)], out_sem.at[k]
        )

    inverse, moment, cot = inv_ref[...], moment_ref[...], cot_ref[...]
    for k in range(inputs.count):
        inputs.wait(k)
        partial = lax.dot_general(
            cot, inputs.weight[k], (((1,), (1,)), ((), ())), preferred_element_type=jnp.float32
        )
        wide = inputs.block[k].astype(jnp.float32)
        grads = inverse * gain_ref[:, inputs.columns(k)] * partial - wide * moment
        out[k] = grads.astype(jnp.bfloat16)
        block_out(k).start()
    for k in range(inputs.count):
        block_out(k).wait()


def in_hbm(*arrays):
    return [pltpu.with_memory_space_constraint(array, pltpu.HBM) for array in arrays]


def costs(tokens, columns):
    rows, width = tokens.shape
    return dict(
        compiler_params=pltpu.CompilerParams(vmem_limit_bytes=LIMIT),
        cost_estimate=pl.CostEstimate(
            flops=rows * width * columns,
            bytes_accessed=2 * rows * width + width * columns,
            transcendentals=0,
        ),
    )


def forward(tokens, inverse, gain, weights, table):
    rows, span, columns = tokens.shape[0], *weights[0].shape[1:]
    return pl.pallas_call(
        forward_kernel,
        in_specs=[SMEM, HBM] + [VMEM] * 2 + [HBM] * len(weights),
        out_specs=VMEM,
        out_shape=jax.ShapeDtypeStruct((rows, columns), jnp.float32),
        scratch_shapes=Inputs.scratch(rows, span, columns, table.shape[0]),
        **costs(tokens, columns),
    )(table, *in_hbm(tokens), inverse, gain, *in_hbm(*weights))


def forward_last(tokens, inverse, gain, cotangent, weights, sums, table):
    rows, span, columns = tokens.shape[0], *weights[0].shape[1:]
    return pl.pallas_call(
        forward_last_kernel,
        in_specs=[SMEM, HBM] + [VMEM] * 4 + [HBM] * len(weights),
        out_specs=[VMEM] * 2,
        out_shape=[
            jax.ShapeDtypeStruct((rows, columns), jnp.bfloat16),
            jax.ShapeDtypeStruct((rows, 1), jnp.float32),
        ],
        scratch_shapes=[pltpu.VMEM((rows, columns), jnp.float32)]
        + Inputs.scratch(rows, span, columns, table.shape[0]),
        **costs(tokens, columns),
    )(table, *in_hbm(tokens), inverse, gain, cotangent, sums, *in_hbm(*weights))


def backward(tokens, inverse, gain, cotangent, moment, weights, table, before=()):
    rows, span, columns = tokens.shape[0], *weights[0].shape[1:]
    count = table.shape[0]
    return pl.pallas_call(
        functools.partial(backward_kernel, count=len(weights)),
        in_specs=[SMEM, HBM] + [VMEM] * 4 + [HBM] * (len(weights) + len(before)),
        out_specs=HBM,
        out_shape=jax.ShapeDtypeStruct(tokens.shape, jnp.bfloat16),
        scratch_shapes=[
            pltpu.VMEM((count, rows, span), jnp.bfloat16),
            pltpu.SemaphoreType.DMA((count,)),
        ]
        + Inputs.scratch(rows, span, columns, count),
        input_output_aliases={6 + len(weights): 0} if before else {},
        **costs(tokens, columns),
    )(table, *in_hbm(tokens), inverse, gain, cotangent, moment, *in_hbm(*weights, *before))


def swap(array, axis):
    last = lax.axis_size(axis) - 1
    return lax.ppermute(array, axis, [(a, last - a) for a in range(last + 1)])


def pair(array, axis, step):
    size = lax.axis_size(axis)
    masks = (1, 3) if step == 0 else (3, 1)
    moves = [(a * 2 + c, (a ^ masks[c]) * 2 + c) for a in range(size) for c in range(2)]
    return lax.ppermute(array, (axis, "c"), moves)


def across(array, axis):
    size = lax.axis_size(axis)
    return lax.ppermute(array, axis, [(a, a ^ 2) for a in range(size)])


def pair_z(array):
    size = lax.axis_size("zh") * lax.axis_size("zl")
    moves = []
    for z in range(size):
        moves.append((z * 2, (z ^ 1) * 2))
        moves.append((z * 2 + 1, (z + (1 if z % 2 else -1)) % size * 2 + 1))
    return lax.ppermute(array, ("zh", "zl", "c"), moves)


def add(kept, got):
    return kept + got.astype(jnp.float32)


def add_halves(kept, got):
    half = kept.shape[0] // 2
    return add(kept[half:], got[half:]).astype(jnp.bfloat16), add(kept[:half], got[:half])


def tie(first, *others):
    return lax.optimization_barrier((first, *others))[0]


BASE, ABOVE = (((z, 0, 0), (z, 0, 1)) for z in (0, 1))
NEAR, ABOVE_NEAR = (((z, 1, 0), (z, 1, 1)) for z in (0, 1))
NEAR_C, ABOVE_NEAR_C = (((z, 2, 1), (z, 2, 0)) for z in (0, 1))
FAR, ABOVE_FAR = (((z, 3, 0),) for z in (0, 1))
FAR_C, ABOVE_FAR_C = (((z, 3, 1),) for z in (0, 1))


def write_ends(out_ref, rows):
    high = rows.astype(jnp.bfloat16).astype(jnp.float32)
    out_ref[-2 * EXTRA :, :] = jnp.concatenate([high, rows - high]).astype(jnp.bfloat16)


def read_ends(ref):
    ends = ref[-2 * EXTRA :, :].astype(jnp.float32)
    return ends[:EXTRA] + ends[EXTRA:]


def spread_kernel(tab_ref, total_ref, gain_ref, base_ref, near_ref, near_c_ref, far_ref, *refs, devices):
    out_refs, (rows_ref, weight, sem) = refs[:4], refs[4:]
    columns = base_ref.shape[2]
    rows = pl.ds(pl.multiple_of(tab_ref[4] * TILE, TILE), TILE)
    copies = [
        pltpu.make_async_copy(shard.at[rows], weight.at[k], sem.at[k])
        for k, shard in enumerate((base_ref.at[0], near_c_ref.at[1], near_ref.at[0], far_ref.at[0]))
    ]
    for copy in copies:
        copy.start()
    rows_ref[...] = jnp.zeros_like(rows_ref)
    for k in range(4):
        out_refs[k][:columns, :] = total_ref[k].reshape(columns, TILE).astype(jnp.bfloat16)
    for k in range(4):
        copies[k].wait()
        total = total_ref[k].reshape(columns, TILE)
        part = jnp.sum(weight[k].astype(jnp.float32).T * total, axis=0, keepdims=True)
        gain = gain_ref[:, pl.ds(pl.multiple_of(tab_ref[k] * TILE, TILE), TILE)]
        rows_ref[pl.ds(tab_ref[5 + k], 1), :] = part / (gain * devices)
    for out_ref in out_refs:
        write_ends(out_ref, rows_ref[...])


def spread(total, gain, base, near, near_c, far, table, devices):
    columns = base.shape[2]
    return pl.pallas_call(
        functools.partial(spread_kernel, devices=devices),
        in_specs=[SMEM] + [VMEM] * 2 + [HBM] * 4,
        out_specs=[VMEM] * 4,
        out_shape=[jax.ShapeDtypeStruct((columns + 2 * EXTRA, TILE), jnp.bfloat16)] * 4,
        scratch_shapes=[
            pltpu.VMEM((EXTRA, TILE), jnp.float32),
            pltpu.VMEM((4, TILE, columns), jnp.bfloat16),
            pltpu.SemaphoreType.DMA((4,)),
        ],
        compiler_params=pltpu.CompilerParams(vmem_limit_bytes=LIMIT),
    )(table, total, gain, *in_hbm(base, near, near_c, far))


def in_pairs(terms):
    while len(terms) > 1:
        terms = [a + b for a, b in zip(terms[::2], terms[1::2])]
    return terms[0]


def merge_kernel(*refs, scale):
    parts, out_ref = refs[:-1], refs[-1]
    columns = out_ref.shape[0] - 2 * EXTRA
    total = in_pairs([part[:columns, :].astype(jnp.float32) for part in parts])
    out_ref[:columns, :] = (total * scale).astype(jnp.bfloat16)
    write_ends(out_ref, in_pairs([read_ends(part) for part in parts]))


def merge(parts, scale=1.0):
    return pl.pallas_call(
        functools.partial(merge_kernel, scale=scale),
        in_specs=[VMEM] * len(parts),
        out_specs=VMEM,
        out_shape=jax.ShapeDtypeStruct(parts[0].shape, parts[0].dtype),
        compiler_params=pltpu.CompilerParams(vmem_limit_bytes=SMALL),
    )(*parts)


def finish_kernel(tab_ref, *refs):
    parts, (weight_ref, gain_ref) = refs[:4], refs[4:]
    columns = weight_ref.shape[1]
    for k, part in enumerate(parts):
        rows = pl.ds(pl.multiple_of(tab_ref[k] * TILE, TILE), TILE)
        weight_ref[rows, :] = part[:columns, :].astype(jnp.float32).T
        gain_ref[tab_ref[k]] = read_ends(part)


def finish(parts, table):
    columns = parts[0].shape[0] - 2 * EXTRA
    return pl.pallas_call(
        finish_kernel,
        in_specs=[SMEM] + [VMEM] * 4,
        out_specs=[VMEM] * 2,
        out_shape=[
            jax.ShapeDtypeStruct((4 * TILE, columns), jnp.float32),
            jax.ShapeDtypeStruct((4, EXTRA, TILE), jnp.float32),
        ],
        compiler_params=pltpu.CompilerParams(vmem_limit_bytes=SMALL),
    )(table, *parts)


def order_kernel(tab_ref, *refs):
    parts, out_ref = refs[:4], refs[4]
    for k, part in enumerate(parts):
        for x in range(4):
            for y in range(4):
                out_ref[tab_ref[k] + 2 * x, y : y + 1, :] = part[y, x : x + 1, :]


def order(parts, table):
    return pl.pallas_call(
        order_kernel,
        in_specs=[SMEM] + [VMEM] * 4,
        out_specs=VMEM,
        out_shape=jax.ShapeDtypeStruct((16, 4, TILE), jnp.float32),
        compiler_params=pltpu.CompilerParams(vmem_limit_bytes=SMALL),
    )(table, *parts)


def shards(tokens, norm_gain, weight_values, weight_scale, key_cotangent):
    y, zl, x, c = (lax.axis_index(a) for a in ("y", "zl", "x", "c"))
    width = tokens.shape[1]
    columns = weight_values.shape[1]
    gain = norm_gain.reshape(1, width)
    devices = 1
    for axis in EVERY:
        devices *= lax.axis_size(axis)

    def offset(core, first, second):
        masks = (1 + 2 * core, 3 - 2 * core)
        return first * masks[0] ^ second * masks[1]

    label = jnp.arange(32, dtype=jnp.int32)
    bits = [label // 16] + [label // k % 2 for k in (8, 4, 2, 1)]
    tables = []
    for core in (c, 1 - c):
        chip = (zl ^ bits[0]) * 4 + (x ^ offset(core, bits[3], bits[4]))
        tables.append((chip * 2 + core) * 4 + (y ^ offset(core, bits[1], bits[2])))

    def nodes_of(pieces):
        at = [((zl ^ z) * 4 + (x ^ offset(c, k % 2, k // 2))) * 2 + (c ^ lane) for z, k, lane in pieces]
        return jnp.stack(at).astype(jnp.int32)

    own = widen_weight(weight_values, weight_scale)
    own_c = swap(own, "c")
    up = pair_z(own)
    cot_own = key_cotangent.T
    base = jnp.stack([own, own_c])
    cot_got = swap(cot_own, "c")
    mine, other, inverse = norm_tiles(tokens, gain, tie(jnp.stack(tables), own))
    got = swap(other, "c")
    near = pair(base, "x", 0)

    first, kept_first = grad_tiles(mine, got, cot_own, cot_got, 0)
    mine, up, first = lax.optimization_barrier((mine, up, first))
    second, kept_second = grad_tiles(mine, got, cot_own, cot_got, 1)
    moved = [pair(first, "y", 0), pair_z(second)]
    above = jnp.stack([up, swap(up, "c")])
    moved[0], above = lax.optimization_barrier((moved[0], above))
    above_near = pair(above, "x", 0)
    (first, kept_first), (second, kept_second) = map(
        add_halves, (kept_first, kept_second), moved
    )

    first, near = lax.optimization_barrier((first, near))
    moved = [pair_z(first), pair(second, "y", 0)]
    near_c = swap(near, "c")
    far = pair(near_c[1:], "x", 0)
    early = [base, above, near, near_c]
    sums = forward(tokens, inverse, gain, early, nodes_of(BASE + ABOVE + NEAR + NEAR_C))
    moved[1], sums, above_near, far = lax.optimization_barrier((moved[1], sums, above_near, far))
    (first, kept_first), (second, kept_second) = map(
        add_halves, (kept_first, kept_second), moved
    )

    send, above_near, far = lax.optimization_barrier((jnp.stack([first, second]), above_near, far))
    moved = pair(send, "y", 1)
    above_near_c = swap(above_near, "c")
    above_far = pair(above_near_c[1:], "x", 0)
    far_c = swap(far, "c")
    moved, far_c, above_near_c = lax.optimization_barrier((moved, far_c, above_near_c))
    total = jnp.stack([add(kept_first, moved[0]), add(kept_second, moved[1])], axis=1)

    peer = x ^ offset(c, jnp.arange(4) // 2, jnp.arange(4) % 2)
    node_tile = ((zl * 4 + peer) * 2 + c) * 4 + y
    at = jnp.concatenate([node_tile, y[None], peer]).astype(jnp.int32)
    parts = list(spread(total, gain, base, near, near_c, far, at, devices))
    parts[0], above_far = lax.optimization_barrier((parts[0], above_far))
    moved = [parts[0], pair(parts[2], "x", 0), pair(parts[1], "x", 1), across(parts[3], "x")]
    above_far_c = swap(above_far, "c")
    late = [above_near, above_near_c, far, above_far, far_c, above_far_c]
    late_at = nodes_of(ABOVE_NEAR + ABOVE_NEAR_C + FAR + ABOVE_FAR + FAR_C + ABOVE_FAR_C)
    projected, moment = forward_last(tokens, inverse, gain, key_cotangent, late, sums, late_at)
    moved[3], moment = lax.optimization_barrier((moved[3], moment))
    send = merge(moved)

    def part_of_grads(before, weights, pieces):
        return backward(
            tokens, inverse, gain, key_cotangent, moment, weights, nodes_of(pieces), before
        )

    send, moment = lax.optimization_barrier((send, moment))
    moved = pair(send, "zh", 0)
    token_grads = part_of_grads((), [base, above, near], BASE + ABOVE + NEAR)
    moved, token_grads = lax.optimization_barrier((moved, token_grads))
    send = merge((send, moved))
    send, token_grads = lax.optimization_barrier((send, token_grads))
    moved = pair(send, "zh", 1)
    token_grads = part_of_grads(
        (token_grads,), [near_c, above_near, far], NEAR_C + ABOVE_NEAR + FAR
    )
    moved, token_grads = lax.optimization_barrier((moved, token_grads))
    send = merge((send, moved), 1.0 / devices)

    parts = (send, pair(send, "y", 0), pair(send, "y", 1), across(send, "y"))
    quarters = jnp.stack([y ^ offset(c, k % 2, k // 2) for k in range(4)]).astype(jnp.int32)
    token_grads = part_of_grads(
        (tie(token_grads, send),),
        [above_near_c, above_far, far_c, above_far_c],
        ABOVE_NEAR_C + ABOVE_FAR + FAR_C + ABOVE_FAR_C,
    )
    parts, token_grads = lax.optimization_barrier((parts, token_grads))
    weight_grads, gains = finish(parts, quarters)
    gains = (gains, swap(gains, "c"), swap(gains, "zl"), swap(gains, ("zl", "c")))
    nodes = jnp.stack([(zl ^ k // 2) * 8 + (c ^ k % 2) for k in range(4)]).astype(jnp.int32)
    gain_grads = order(gains, nodes).reshape(width)
    return (projected, token_grads, weight_grads, gain_grads)


def solution(mesh):
    fine = Mesh(mesh.devices.reshape(4, 4, 2, 4, 2), EVERY)
    rows = P(EVERY, None)
    return jax.shard_map(
        shards,
        mesh=fine,
        in_specs=(rows, P(), P(NODE, None), P(NODE, None), rows),
        out_specs=(rows, rows, P(NODE, None), P()),
        check_vma=False,
    )
```
